32 devices in a mesh: dp: 8 (over y, x, core), blk: 4 (over z).
Axes of the slice: x: 2, y: 2, z: 4, core: 2. Of those that a mesh axis runs over, the one named last changes fastest.
Arguments:
- tokens: bfloat16 [24, 1024, 768], P('dp', 'blk'), may hold values from -6 to 6
- live_count: int32 [8], P('dp'), may hold values from 1 to 3, as said below
- first_gain: float32 [768], replicated, may hold values from 0.1 to 1.9
- first_shift: float32 [768], replicated, may hold values from -1.75 to 1.75
- joint_weight: bfloat16 [768, 2304], replicated, may hold values from -0.21875 to 0.21875
- query_bias: float32 [768], replicated, may hold values from -3 to 3
- value_bias: float32 [768], replicated, may hold values from -0.3125 to 0.3125
- out_weight: bfloat16 [768, 768], replicated, may hold values from -2.5 to 2.5
- out_bias: float32 [768], replicated, may hold values from -1.75 to 1.75
- second_gain: float32 [768], replicated, may hold values from 0.1 to 1.9
- second_shift: float32 [768], replicated, may hold values from -1.75 to 1.75
- up_weight: bfloat16 [768, 3072], replicated, may hold values from -0.21875 to 0.21875
- up_bias: float32 [3072], replicated, may hold values from -1.75 to 1.75
- down_weight: bfloat16 [3072, 768], replicated, may hold values from -0.109375 to 0.109375
- down_bias: float32 [768], replicated, may hold values from -1.75 to 1.75
- cotangent: bfloat16 [24, 1024, 768], P('dp', 'blk'), may hold values from -6 to 6
Outputs:
- output: bfloat16 [24, 1024, 768], P('dp', 'blk')
- grad_tokens: bfloat16 [24, 1024, 768], P('dp', 'blk')
- grad_first_gain: float32 [768], replicated
- grad_first_shift: float32 [768], replicated
- grad_joint_weight: float32 [768, 2304], replicated
- grad_query_bias: float32 [768], replicated
- grad_value_bias: float32 [768], replicated
- grad_out_weight: float32 [768, 768], replicated
- grad_out_bias: float32 [768], replicated
- grad_second_gain: float32 [768], replicated
- grad_second_shift: float32 [768], replicated
- grad_up_weight: float32 [768, 3072], replicated
- grad_up_bias: float32 [3072], replicated
- grad_down_weight: float32 [3072, 768], replicated
- grad_down_bias: float32 [768], replicated
The draws below stay inside these ranges and needn't reach their ends.
Inputs may be any that keep to these rules, and one draw needn't show every extreme that they name: `live_count`: some index of dp has 3 live sequences and some other index has 1.
All inputs are finite; a program needn't handle non-finite values.
Results may differ from the reference program's by a relative error of at most 0.017.
Values may be sent and summed in bfloat16 or wider, within the bound.
No kernel may reach another device: no remote copies, remote signals or barrier semaphores. Data moves between devices by JAX's collectives and lax.ppermute only.
A program may use at most 256 MiB of HBM per device.

```python
import math
from functools import partial
import jax
import jax.numpy as jnp
from jax import lax

D = 768
HEADS = 12
HEAD_DIM = 64
FF = 3072
SLOTS = 3
LENGTH = 1024
SEQS = 24
N_DP = 8


def draw_live_count(key, part):
    key = jax.random.fold_in(key, 17)
    first_key, second_key = jax.random.split(key)
    counts = jax.random.randint(first_key, (N_DP,), 1, SLOTS + 1, dtype=jnp.int32)
    shuffled = jax.random.permutation(second_key, N_DP)
    counts = counts.at[shuffled[0]].set(SLOTS)
    counts = counts.at[shuffled[1]].set(1)
    return counts


def block_levels(own_key, extent, pieces, least, top_value):
    factor_of, own = 1.0, jax.random.fold_in(own_key, 6)
    for position, shards_of in pieces:
        draws = jnp.exp(jax.random.uniform(jax.random.fold_in(own, position), (shards_of,), jnp.float32, least / len(pieces), top_value / len(pieces)))
        factor_of = factor_of * jnp.repeat(draws, extent[position] // shards_of).reshape([-1 if axis == position else 1 for axis in range(len(extent))])
    return factor_of


def scatter_about(stream_key, shape, scale, most, shards=(), held_as=jnp.bfloat16):
    loudness = block_levels(stream_key, shape, shards, -0.22, 0.18) if shards else 1.0
    values = jax.random.normal(stream_key, shape, jnp.float32) * scale * loudness
    return jnp.minimum(jnp.maximum(values, -most), most).astype(held_as)


def setup_inputs(seed: int = 0) -> dict:
    seeds = jax.random.split(jax.random.key(seed), 17)
    tokens = scatter_about(seeds[0], (SEQS, LENGTH, D), 1.0, 6.0, ((0, 8), (1, 4)))
    live_count = draw_live_count(jax.random.fold_in(seeds[16], 71), 0)
    first_gain = jnp.clip(1.0 + 0.18 * jax.random.normal(seeds[2], (D,), jnp.float32), 0.1, 1.9)
    first_shift = scatter_about(seeds[3], (D,), 0.3, 1.75, (), jnp.float32)
    joint_weight = scatter_about(seeds[4], (D, 3 * D), D ** -0.5, 0.21875)
    query_bias = scatter_about(seeds[5], (D,), 0.5, 3.0, (), jnp.float32)
    value_bias = scatter_about(seeds[6], (D,), 0.05, 0.3125, (), jnp.float32)
    out_weight = scatter_about(seeds[7], (D, D), (max(1, 8 * D // LENGTH)) ** -0.5, 2.5)
    out_bias = scatter_about(seeds[8], (D,), 0.3, 1.75, (), jnp.float32)
    second_gain = jnp.clip(1.0 + 0.18 * jax.random.normal(seeds[9], (D,), jnp.float32), 0.1, 1.9)
    second_shift = scatter_about(seeds[10], (D,), 0.3, 1.75, (), jnp.float32)
    up_weight = scatter_about(seeds[11], (D, FF), D ** -0.5, 0.21875)
    up_bias = scatter_about(seeds[12], (FF,), 0.3, 1.75, (), jnp.float32)
    down_weight = scatter_about(seeds[13], (FF, D), FF ** -0.5, 0.109375)
    down_bias = scatter_about(seeds[14], (D,), 0.3, 1.75, (), jnp.float32)
    cotangent = scatter_about(seeds[15], (SEQS, LENGTH, D), 1.0, 6.0, ((0, 8), (1, 4)))
    return dict(tokens=tokens, live_count=live_count, first_gain=first_gain, first_shift=first_shift, joint_weight=joint_weight, query_bias=query_bias, value_bias=value_bias, out_weight=out_weight, out_bias=out_bias, second_gain=second_gain, second_shift=second_shift, up_weight=up_weight, up_bias=up_bias, down_weight=down_weight, down_bias=down_bias, cotangent=cotangent)


EXACT_DOT = lax.Precision.HIGHEST

@jax.custom_vjp
def low(v):
    return lax.optimization_barrier(v.astype(jnp.bfloat16)).astype(jnp.float32)

@jax.custom_vjp
def low_back(v):
    return v

def low_keep(v):
    return (low(v), None)

def low_pass(kept, grad):
    return (grad,)

def back_keep(v):
    return (v, None)

def back_low(kept, grad):
    return (low(grad),)
low.defvjp(low_keep, low_pass)
low_back.defvjp(back_keep, back_low)

def layer_norm(values, norm_gain, norm_shift):
    center = values - lax.optimization_barrier(jnp.mean(values, axis=-1, keepdims=True))
    spread = lax.optimization_barrier(jnp.mean(center * center, axis=-1, keepdims=True))
    return center * lax.rsqrt(spread + 1e-05) * norm_gain + norm_shift

def matmul(first_op, second_op):
    return jnp.dot(first_op, second_op, precision=EXACT_DOT)

def attend_one(triple):
    query_rows, key_rows, value_rows = triple
    seq_len = query_rows.shape[0]
    query_heads = query_rows.reshape(seq_len, HEADS, HEAD_DIM)
    key_heads = key_rows.reshape(seq_len, HEADS, HEAD_DIM)
    value_heads = value_rows.reshape(seq_len, HEADS, HEAD_DIM)
    scores = jnp.einsum('qhd,khd->hqk', query_heads, key_heads, precision=EXACT_DOT) * (1.0 / math.sqrt(HEAD_DIM))
    scores = low_back(scores)
    places = jnp.arange(seq_len, dtype=jnp.int32)
    causal = places[None, :, None] >= places[None, None, :]
    masked = jnp.where(causal, scores, -1e+30)
    row_max = lax.optimization_barrier(jnp.max(masked, axis=-1, keepdims=True))
    unnormed = jnp.exp(masked - row_max)
    weights = low(unnormed / lax.optimization_barrier(jnp.sum(unnormed, axis=-1, keepdims=True)))
    mixed = jnp.einsum('hqk,khd->qhd', weights, value_heads, precision=EXACT_DOT)
    return mixed.reshape(seq_len, D)

def forward(live_rows, tokens, first_gain, first_shift, joint_weight, query_bias, value_bias, out_weight, out_bias, second_gain, second_shift, up_weight, up_bias, down_weight, down_bias):
    flat_rows = tokens.reshape(-1, D)
    attn_in = low(layer_norm(flat_rows, first_gain, first_shift))
    joined = matmul(attn_in, joint_weight)
    query_rows = low_back(low(joined[:, :D] + query_bias))
    key_rows = low_back(low(joined[:, D:2 * D]))
    value_rows = low_back(low(joined[:, 2 * D:] + value_bias))
    mixed = lax.map(jax.checkpoint(attend_one), (query_rows.reshape(SEQS, LENGTH, D), key_rows.reshape(SEQS, LENGTH, D), value_rows.reshape(SEQS, LENGTH, D)))
    mixed = low_back(low(mixed.reshape(-1, D)))
    branch = low_back(matmul(mixed, out_weight) + out_bias)
    hidden = flat_rows + branch
    mlp_in = low(layer_norm(hidden, second_gain, second_shift))
    pre_act = low_back(matmul(mlp_in, up_weight) + up_bias)
    active = low_back(low(jax.nn.gelu(pre_act, approximate=True)))
    result = hidden + low_back(matmul(active, down_weight) + down_bias)
    return (result * live_rows).reshape(tokens.shape)

def reference(tokens, live_count, first_gain, first_shift, joint_weight, query_bias, value_bias, out_weight, out_bias, second_gain, second_shift, up_weight, up_bias, down_weight, down_bias, cotangent):
    slot_ids = jnp.arange(SLOTS, dtype=jnp.int32)
    live_slots = (slot_ids[None, :] < live_count[:, None]).astype(jnp.float32).reshape(SEQS)
    live_rows = jnp.repeat(live_slots, LENGTH)[:, None]
    params = (tokens.astype(jnp.float32), first_gain, first_shift, joint_weight.astype(jnp.float32), query_bias, value_bias, out_weight.astype(jnp.float32), out_bias, second_gain, second_shift, up_weight.astype(jnp.float32), up_bias, down_weight.astype(jnp.float32), down_bias)
    result, pullback = jax.vjp(partial(forward, live_rows), *params)
    grads = pullback(cotangent.astype(jnp.float32))
    return (result.astype(jnp.bfloat16), grads[0].astype(jnp.bfloat16), grads[1], grads[2], grads[3], grads[4], grads[5], grads[6], grads[7], grads[8], grads[9], grads[10], grads[11], grads[12], grads[13])
```

```python
import math
from functools import partial
import jax
import jax.numpy as jnp
from jax import lax
from jax.experimental import pallas as pl
from jax.experimental.pallas import tpu as pltpu
from jax.sharding import PartitionSpec as P

BF = jnp.bfloat16
F32 = jnp.float32
HEADS = 12
EPS = 1e-5
ROWS = 256
VMEM_LIMIT = 60 * 2**20


def params(**kw):
    return pltpu.CompilerParams(vmem_limit_bytes=VMEM_LIMIT, **kw)


def mm(a, b, ca, cb):
    return lax.dot_general(a, b, (((ca,), (cb,)), ((), ())), preferred_element_type=F32)


def shape(s, d):
    return jax.ShapeDtypeStruct(s, d)


def whole(s):
    n = len(s)
    return pl.BlockSpec(s, lambda *_: (0,) * n)


def norm_stats(t):
    c = t - jnp.mean(t, axis=-1, keepdims=True)
    r = lax.rsqrt(jnp.mean(c * c, axis=-1, keepdims=True) + EPS)
    return c * r, r


def joint_kernel(x_ref, g_ref, s_ref, w_ref, b_ref, a_ref, q_ref):
    j = pl.program_id(0)
    d = x_ref.shape[1]

    @pl.when(j == 0)
    def _():
        for i in range(x_ref.shape[0] // ROWS):
            rows = pl.ds(i * ROWS, ROWS)
            n, _ = norm_stats(x_ref[rows, :].astype(F32))
            a_ref[rows, :] = (n * g_ref[...] + s_ref[...]).astype(BF)

    scale = jnp.where(j == 0, 0.125, 1.0).astype(BF)
    for i in range(x_ref.shape[0] // ROWS):
        rows = pl.ds(i * ROWS, ROWS)
        q_ref[rows, :] = (mm(a_ref[rows, :], w_ref[...], 1, 0) + b_ref[...]).astype(BF) * scale


def joint_call(x, gain, shift, w, bias):
    L, d = x.shape
    return pl.pallas_call(
        joint_kernel,
        grid=(3,),
        in_specs=[whole((L, d)), whole((1, d)), whole((1, d)),
                  pl.BlockSpec((d, d), lambda j: (0, j)), pl.BlockSpec((1, d), lambda j: (0, j))],
        out_specs=[whole((L, d)), pl.BlockSpec((L, d), lambda j: (0, j))],
        out_shape=[shape((L, d), BF), shape((L, 3 * d), BF)],
        compiler_params=params(),
        name="joint",
    )(x, gain, shift, w, bias)


def attend_kernel(q_ref, k_ref, v_ref, o_ref, p_ref):
    L = q_ref.shape[0]
    lane = lax.broadcasted_iota(jnp.int32, (ROWS, 128), 1)
    row = lax.broadcasted_iota(jnp.int32, (ROWS, ROWS), 0)
    col = lax.broadcasted_iota(jnp.int32, (ROWS, ROWS), 1)
    tri = col <= row
    for i in range(L // ROWS):
        rows = pl.ds(i * ROWS, ROWS)
        q = q_ref[rows, :]
        outs = []
        for h in range(2):
            mine = (lane < 64) if h == 0 else (lane >= 64)
            qh = jnp.where(mine, q, jnp.zeros_like(q))
            s_diag = jnp.where(tri, mm(qh, k_ref[rows, :], 1, 1), -1e30)
            m = jnp.max(s_diag, axis=-1, keepdims=True)
            if i:
                prev = pl.ds(0, i * ROWS)
                s_prev = mm(qh, k_ref[prev, :], 1, 1)
                m = jnp.maximum(m, jnp.max(s_prev, axis=-1, keepdims=True))
                e_prev = jnp.exp(s_prev - m)
                total = jnp.sum(e_prev, axis=-1, keepdims=True)
            e_diag = jnp.exp(s_diag - m)
            t_diag = jnp.sum(e_diag, axis=-1, keepdims=True)
            total = total + t_diag if i else t_diag
            inv = 1.0 / total
            p_diag = (e_diag * inv).astype(BF)
            p_ref[h, rows, rows] = p_diag
            acc = mm(p_diag, v_ref[rows, :], 1, 0)
            if i:
                p_prev = (e_prev * inv).astype(BF)
                p_ref[h, rows, prev] = p_prev
                acc += mm(p_prev, v_ref[prev, :], 1, 0)
            outs.append(acc)
        o_ref[rows, :] = jnp.where(lane < 64, outs[0], outs[1]).astype(BF)


def attend_call(qkv):
    L, d3 = qkv.shape
    n = d3 // 3 // 128
    col = lambda k: pl.BlockSpec((L, 128), lambda j: (0, k * n + j))
    return pl.pallas_call(
        attend_kernel,
        grid=(n,),
        in_specs=[col(0), col(1), col(2)],
        out_specs=[col(0), pl.BlockSpec((2, L, L), lambda j: (j, 0, 0))],
        out_shape=[shape((L, d3 // 3), BF), shape((2 * n, L, L), BF)],
        compiler_params=params(),
        name="attend",
    )(qkv, qkv, qkv)


def out_kernel(m_ref, w_ref, b_ref, x_ref, g_ref, s_ref, h_ref, a_ref):
    h = x_ref[...].astype(F32) + mm(m_ref[...], w_ref[...], 1, 0) + b_ref[...]
    h_ref[...] = h
    n, _ = norm_stats(h)
    a_ref[...] = (n * g_ref[...] + s_ref[...]).astype(BF)


def out_call(mixed, w, b, x, gain, shift):
    L, d = x.shape
    blk = pl.BlockSpec((ROWS, d), lambda i: (i, 0))
    return pl.pallas_call(
        out_kernel,
        grid=(L // ROWS,),
        in_specs=[blk, whole((d, d)), whole((1, d)), blk, whole((1, d)), whole((1, d))],
        out_specs=[blk, blk],
        out_shape=[shape((L, d), F32), shape((L, d), BF)],
        compiler_params=params(),
        name="out_proj",
    )(mixed, w, b, x, gain, shift)


GC = math.sqrt(2.0 / math.pi)


def gelu_both(u):
    u2 = u * u
    t = jnp.tanh(u * (GC + GC * 0.044715 * u2))
    half = 0.5 + 0.5 * t
    return u * half, half + u * (0.5 - 0.5 * t * t) * (GC + 3 * GC * 0.044715 * u2)


def mlp_kernel(first, a_ref, c_ref, up_ref, ub_ref, dn_ref, *rest):
    if first:
        unit_ref, gb_ref, r_ref, e_ref, act, gpre = rest
    else:
        r0_ref, e0_ref, unit_ref, gb_ref, r_ref, e_ref, act, gpre = rest
    j = pl.program_id(0)
    L = a_ref.shape[0]
    gb = jnp.zeros(gb_ref.shape, F32)
    for i in range(L // ROWS):
        rows = pl.ds(i * ROWS, ROWS)
        u = mm(a_ref[rows, :], up_ref[...], 1, 0) + ub_ref[...]
        ga = mm(c_ref[rows, :], dn_ref[...], 1, 1).astype(BF)
        g, dg = gelu_both(u)
        act[rows, :] = g.astype(BF)
        gp = (ga.astype(F32) * dg).astype(BF)
        gpre[rows, :] = gp
        gb = gb + jnp.sum(gp.astype(F32), axis=0, keepdims=True)
    gb_ref[...] = gb
    unit_ref[0, 0] = mm(act[...], c_ref[...], 0, 0).astype(BF)
    unit_ref[0, 1] = mm(a_ref[...], gpre[...], 0, 0).astype(BF)

    @pl.when(j == 0)
    def _():
        for i in range(L // ROWS):
            rows = pl.ds(i * ROWS, ROWS)
            r = mm(act[rows, :], dn_ref[...], 1, 0)
            e = mm(gpre[rows, :], up_ref[...], 1, 1)
            if first:
                r_ref[rows, :] = r
                e_ref[rows, :] = e
            else:
                r_ref[rows, :] = r + r0_ref[rows, :]
                e_ref[rows, :] = e + e0_ref[rows, :]

    @pl.when(j > 0)
    def _():
        for i in range(L // ROWS):
            rows = pl.ds(i * ROWS, ROWS)
            r_ref[rows, :] += mm(act[rows, :], dn_ref[...], 1, 0)
            e_ref[rows, :] += mm(gpre[rows, :], up_ref[...], 1, 1)


def mlp_call(a, c, up, ub, dn, lo, tiles, tile, state=None):
    L, d = a.shape
    first = state is None
    at = lambda j: lo + j
    return pl.pallas_call(
        partial(mlp_kernel, first),
        grid=(tiles,),
        in_specs=[whole((L, d)), whole((L, d)),
                  pl.BlockSpec((d, tile), lambda j: (0, at(j))),
                  pl.BlockSpec((1, tile), lambda j: (0, at(j))),
                  pl.BlockSpec((tile, d), lambda j: (at(j), 0))]
        + ([] if first else [whole((L, d)), whole((L, d))]),
        out_specs=[pl.BlockSpec((1, 2, tile, d), lambda j: (j, 0, 0, 0)),
                   pl.BlockSpec((1, tile), lambda j: (0, j)),
                   whole((L, d)), whole((L, d))],
        out_shape=[shape((tiles, 2, tile, d), BF),
                   shape((1, tiles * tile), F32), shape((L, d), F32), shape((L, d), F32)],
        scratch_shapes=[pltpu.VMEM((L, tile), BF), pltpu.VMEM((L, tile), BF)],
        compiler_params=params(),
        name="mlp",
    )(a, c, up, ub, dn, *(() if first else state))


def norm_back(e, n, r):
    return r * (e - jnp.mean(e, axis=-1, keepdims=True) - n * jnp.mean(e * n, axis=-1, keepdims=True))


def middle_kernel(r_ref, e_ref, h_ref, c_ref, m_ref, w_ref, g_ref, db_ref, live_ref,
                  o_ref, gh_ref, gm_ref, dw_ref, sums_ref, acc):
    i = pl.program_id(0)

    @pl.when(i == 0)
    def _():
        acc[...] = jnp.zeros_like(acc)
        sums_ref[...] = jnp.zeros_like(sums_ref)

    h = h_ref[...]
    o_ref[...] = ((h + r_ref[...] + db_ref[...]) * live_ref[...]).astype(BF)
    n, r = norm_stats(h)
    e = e_ref[...]
    c = c_ref[...].astype(F32)
    gh = c + norm_back(e * g_ref[...], n, r)
    gh_ref[...] = gh
    gb = gh.astype(BF)
    gm_ref[...] = mm(gb, w_ref[...], 1, 1).astype(BF)
    acc[...] += mm(m_ref[...], gb, 0, 0)
    rows = lambda t: jnp.sum(t, axis=0, keepdims=True)
    sums_ref[0:1, :] += rows(e * n)
    sums_ref[1:2, :] += rows(e)
    sums_ref[2:3, :] += rows(gb.astype(F32))
    sums_ref[3:4, :] += rows(c)

    @pl.when(i == pl.num_programs(0) - 1)
    def _():
        dw_ref[...] = acc[...].astype(BF)


def middle_call(r, e, h, c, mixed, w, gain, down_bias, live):
    L, d = h.shape
    blk = pl.BlockSpec((ROWS, d), lambda i: (i, 0))
    return pl.pallas_call(
        middle_kernel,
        grid=(L // ROWS,),
        in_specs=[blk, blk, blk, blk, blk, whole((d, d)), whole((1, d)), whole((1, d)), whole((1, d))],
        out_specs=[blk, blk, blk, whole((d, d)), whole((8, d))],
        out_shape=[shape((L, d), BF), shape((L, d), F32), shape((L, d), BF), shape((d, d), BF), shape((8, d), F32)],
        scratch_shapes=[pltpu.VMEM((d, d), F32)],
        compiler_params=params(),
        name="middle",
    )(r, e, h, c, mixed, w, gain, down_bias, live)


def attend_back_kernel(q_ref, k_ref, v_ref, p_ref, g_ref, m_ref, dq_ref, dk_ref, dv_ref, dk_acc, dv_acc):
    L = q_ref.shape[0]
    lane = lax.broadcasted_iota(jnp.int32, (ROWS, 128), 1)
    low = lane < 64
    nb = L // ROWS
    for i in range(nb):
        rows = pl.ds(i * ROWS, ROWS)
        past = pl.ds(0, (i + 1) * ROWS)
        g = g_ref[rows, :]
        gm = g.astype(F32) * m_ref[rows, :].astype(F32)
        q = q_ref[rows, :]
        dqs, dks, dvs = [], [], []
        for h in range(2):
            mine = low if h == 0 else ~low
            gh = jnp.where(mine, g, jnp.zeros_like(g))
            delta = jnp.sum(jnp.where(mine, gm, 0.0), axis=-1, keepdims=True)
            p = p_ref[h, rows, past]
            dp = mm(gh, v_ref[past, :], 1, 1)
            ds = (p.astype(F32) * (dp - delta)).astype(BF)
            dqs.append(mm(ds, k_ref[past, :], 1, 0))
            dks.append(mm(ds, q, 0, 0))
            dvs.append(mm(p, g, 0, 0))
        dq_ref[rows, :] = (jnp.where(low, dqs[0], dqs[1]) * 0.125).astype(BF)
        lowp = lax.broadcasted_iota(jnp.int32, ((i + 1) * ROWS, 128), 1) < 64
        dk = jnp.where(lowp, dks[0], dks[1])
        dv = jnp.where(lowp, dvs[0], dvs[1])
        if i:
            prev = pl.ds(0, i * ROWS)
            dk_acc[prev, :] += dk[: i * ROWS]
            dv_acc[prev, :] += dv[: i * ROWS]
        dk_acc[rows, :] = dk[i * ROWS :]
        dv_acc[rows, :] = dv[i * ROWS :]
    dk_ref[...] = dk_acc[...].astype(BF)
    dv_ref[...] = dv_acc[...].astype(BF)


def attend_back_call(qkv, p, gm, mixed):
    L, d3 = qkv.shape
    n = d3 // 3 // 128
    col = lambda k: pl.BlockSpec((L, 128), lambda j: (0, k * n + j))
    s = shape((L, d3 // 3), BF)
    return pl.pallas_call(
        attend_back_kernel,
        grid=(n,),
        in_specs=[col(0), col(1), col(2), pl.BlockSpec((2, L, L), lambda j: (j, 0, 0)), col(0), col(0)],
        out_specs=[col(0)] * 3,
        out_shape=[s] * 3,
        scratch_shapes=[pltpu.VMEM((L, 128), F32), pltpu.VMEM((L, 128), F32)],
        compiler_params=params(),
        name="attend_back",
    )(qkv, qkv, qkv, p, gm, mixed)


def joint_weight_kernel(a_ref, q_ref, k_ref, v_ref, w_ref, sums_ref):
    d = a_ref.shape[1]
    sums_ref[...] = jnp.zeros_like(sums_ref)
    for n, ref in enumerate((q_ref, k_ref, v_ref)):
        w_ref[n] = mm(a_ref[...], ref[...], 0, 0).astype(BF)
    sums_ref[0:1, :] = jnp.sum(q_ref[...].astype(F32), axis=0, keepdims=True)
    sums_ref[1:2, :] = jnp.sum(v_ref[...].astype(F32), axis=0, keepdims=True)


def joint_weight_call(a, dq, dk, dv):
    L, d = a.shape
    return pl.pallas_call(
        joint_weight_kernel,
        out_shape=[shape((3, d, d), BF), shape((8, d), F32)],
        compiler_params=params(),
        name="joint_weight",
    )(a, dq, dk, dv)


def tokens_kernel(q_ref, k_ref, v_ref, w_ref, x_ref, gh_ref, g_ref, o_ref, sums_ref):
    i = pl.program_id(0)
    d = x_ref.shape[1]

    @pl.when(i == 0)
    def _():
        sums_ref[...] = jnp.zeros_like(sums_ref)

    e = mm(q_ref[...], w_ref[:, 0:d], 1, 1) + mm(k_ref[...], w_ref[:, d:2 * d], 1, 1) + mm(v_ref[...], w_ref[:, 2 * d:], 1, 1)
    n, r = norm_stats(x_ref[...].astype(F32))
    o_ref[...] = (gh_ref[...] + norm_back(e * g_ref[...], n, r)).astype(BF)
    sums_ref[0:1, :] += jnp.sum(e * n, axis=0, keepdims=True)
    sums_ref[1:2, :] += jnp.sum(e, axis=0, keepdims=True)


def tokens_call(dq, dk, dv, w, x, gh, gain):
    L, d = x.shape
    blk = pl.BlockSpec((ROWS, d), lambda i: (i, 0))
    return pl.pallas_call(
        tokens_kernel,
        grid=(L // ROWS,),
        in_specs=[blk, blk, blk, whole((d, 3 * d)), blk, blk, whole((1, d))],
        out_specs=[blk, whole((8, d))],
        out_shape=[shape((L, d), BF), shape((8, d), F32)],
        compiler_params=params(),
        name="tokens_back",
    )(dq, dk, dv, w, x, gh, gain)


def bits_of(count):
    assert count & (count - 1) == 0
    return count.bit_length() - 1


class Moves:
    def __init__(self, n_dp, n_blk, slots):
        assert slots <= n_blk
        self.n_dp, self.n_blk, self.slots = n_dp, n_blk, slots
        self.dp, self.blk = lax.axis_index("dp"), lax.axis_index("blk")
        self.odd = self.dp % 2

    def slot(self, blk):
        return jnp.where(self.odd == 1, self.n_blk - 1 - blk, blk)

    def perm(self, step, back):
        pairs = []
        for g in range(self.n_dp):
            for b in range(self.n_blk):
                d = (b + step) % self.n_blk
                s = self.n_blk - 1 - d if g % 2 else d
                if s < self.slots:
                    pair = (g * self.n_blk + b, g * self.n_blk + d)
                    pairs.append(pair[::-1] if back else pair)
        return pairs

    def gather(self, x):
        parts = []
        for step in range(self.n_blk):
            s = jnp.minimum(self.slot((self.blk + step) % self.n_blk), self.slots - 1)
            part = lax.dynamic_index_in_dim(x, s, 0, keepdims=False)
            if step:
                part = lax.ppermute(part, ("dp", "blk"), self.perm(step, False))
            parts.append(part)
        return parts

    def join(self, parts, scale=None):
        block, d = parts[0].shape
        out = jnp.zeros((self.n_blk, block, d), parts[0].dtype)
        for step, part in enumerate(parts):
            if scale is not None:
                part = part * scale
            out = lax.dynamic_update_index_in_dim(out, part, (self.blk - step) % self.n_blk, 0)
        return out.reshape(self.n_blk * block, d)

    def scatter(self, y):
        y = y.reshape(self.n_blk, -1, y.shape[-1])
        parts = []
        for step in range(self.n_blk):
            part = lax.dynamic_index_in_dim(y, (self.blk - step) % self.n_blk, 0, keepdims=False)
            if step:
                part = lax.ppermute(part, ("dp", "blk"), self.perm(step, True))
            parts.append(part)
        held = jnp.stack(parts)
        slots = []
        for s in range(self.slots):
            home = jnp.where(self.odd == 1, self.n_blk - 1 - s, s)
            slots.append(lax.dynamic_index_in_dim(held, (home - self.blk) % self.n_blk, 0, keepdims=False))
        return jnp.stack(slots)


def swap(x, n, bit):
    return lax.ppermute(x, ("dp", "blk"), [(i, i ^ (1 << bit)) for i in range(n)])


def sum_scatter(x, n, me, order):
    for bit in order:
        half = x.shape[0] // 2
        up = (me >> bit) & 1
        sent = lax.dynamic_slice_in_dim(x, (1 - up) * half, half, 0)
        kept = lax.dynamic_slice_in_dim(x, up * half, half, 0)
        x = kept + swap(sent, n, bit)
    return x


def spread(x, n, me, order):
    for bit in reversed(order):
        up = (me >> bit) & 1
        other = swap(x, n, bit)
        x = jnp.where(up == 0, jnp.stack([x, other]), jnp.stack([other, x])).reshape(2 * x.shape[0], x.shape[1])
    return x


def sum_small(x, n, order):
    for bit in order:
        x = x + swap(x, n, bit)
    return x


def on_device(n_dp, n_blk, tokens, live_count, first_gain, first_shift, joint_weight, query_bias, value_bias,
              out_weight, out_bias, second_gain, second_shift, up_weight, up_bias, down_weight, down_bias, cotangent):
    slots, block, d = tokens.shape
    n = n_dp * n_blk
    ff = up_weight.shape[1]
    tiles = ff // d
    moves = Moves(n_dp, n_blk, slots)
    me = moves.dp * n_blk + moves.blk
    row = lambda v: v.reshape(1, -1)
    mine = moves.slot(moves.blk)
    live = ((mine < slots) & (mine < live_count[0])).astype(F32)

    x = moves.join(moves.gather(tokens))
    c = moves.join(moves.gather(cotangent), live.astype(BF))

    bias = jnp.concatenate([query_bias, jnp.zeros((d,), F32), value_bias])
    attn_in, qkv = joint_call(x, row(first_gain), row(first_shift), joint_weight, row(bias))
    mixed, p = attend_call(qkv)
    hidden, mlp_in = out_call(mixed, out_weight, row(out_bias), x, row(second_gain), row(second_shift))

    low, dp_bits = bits_of(n_blk), bits_of(n_dp)
    core, plane = low, [low + 1 + i for i in range(dp_bits - 1)]
    orders = [[core] + plane + list(range(low)), [core] + plane[::-1] + list(range(low))]

    def all_sum(x):
        half = x.shape[0] // 2
        return [spread(sum_scatter(x[i * half : (i + 1) * half], n, me, o), n, me, o) for i, o in enumerate(orders)]

    state, downs, ups, up_biases = None, [], [], []
    per = tiles // 2
    for part in range(2):
        units, gb, r, e = mlp_call(mlp_in, c, up_weight, row(up_bias), down_weight, part * per, per, d, state)
        state = (r, e)
        got = jnp.concatenate(all_sum(units.reshape(-1, d))).reshape(units.shape)
        downs += [got[i, 0] for i in range(per)]
        ups += [got[i, 1] for i in range(per)]
        up_biases.append(gb.reshape(-1, d))
    out, gh, gm, dwo, sums2 = middle_call(r, e, hidden, c, mixed, out_weight, row(second_gain), row(down_bias),
                                          jnp.full((1, d), 1.0, F32) * live)
    output = moves.scatter(out)
    dq, dk, dv = attend_back_call(qkv, p, gm, mixed)
    dj, sums1 = joint_weight_call(attn_in, dq, dk, dv)
    got = jnp.concatenate(all_sum(jnp.concatenate([dwo[None], dj]).reshape(-1, d))).reshape(4, d, d)
    gx, sums0 = tokens_call(dq, dk, dv, joint_weight, x, gh, row(first_gain))
    grad_tokens = moves.scatter(gx)
    small = jnp.concatenate([sums0[:2], sums1[:2], sums2[:4]] + up_biases)
    small = sum_small(small, n, orders[0])
    wide = lambda v: v.astype(F32)
    return (output, grad_tokens, small[0], small[1], wide(jnp.concatenate([got[1], got[2], got[3]], axis=1)),
            small[2], small[3], wide(got[0]), small[6], small[4], small[5], wide(jnp.concatenate(ups, axis=1)),
            small[8:].reshape(-1), wide(jnp.concatenate(downs, axis=0)), small[7])


def solution(mesh):
    seq = P("dp", "blk", None)
    n_dp, n_blk = mesh.shape["dp"], mesh.shape["blk"]
    return jax.shard_map(
        partial(on_device, n_dp, n_blk), mesh=mesh,
        in_specs=(seq, P("dp")) + (P(),) * 13 + (seq,),
        out_specs=(seq, seq) + (P(),) * 13,
        check_vma=False,
    )
```

```python
import math
from functools import partial
import jax
import jax.numpy as jnp
from jax import lax
from jax.experimental import pallas as pl
from jax.experimental.pallas import tpu as pltpu
from jax.sharding import PartitionSpec as P

BF = jnp.bfloat16
F32 = jnp.float32
HEADS = 12
EPS = 1e-5
ROWS = 256
STEP = 512
COST = 1000
MIB = dict(joint_sent=30, joint_kept=30, tokens_back=24, place=30, place_joint=30, halve=16, double=16, arrange=16, small=8,
           vectors=8)


def params(name, length=1024):
    return pltpu.CompilerParams(vmem_limit_bytes=min(60, MIB.get(name, 60) * max(length, 1024) // 1024) * 2**20)


def cost(us):
    return pl.CostEstimate(flops=int(us * COST), bytes_accessed=1000, transcendentals=0)


def mm(a, b, ca, cb):
    return lax.dot_general(a, b, (((ca,), (cb,)), ((), ())), preferred_element_type=F32)


def shape(s, d):
    return pltpu.HBM(s, d)


def whole(s):
    n = len(s)
    return pl.BlockSpec(s, lambda *_: (0,) * n)


def norm_stats(t):
    c = t - jnp.mean(t, axis=-1, keepdims=True)
    r = lax.rsqrt(jnp.mean(c * c, axis=-1, keepdims=True) + EPS)
    return c * r, r


(FIRST_GAIN, FIRST_SHIFT, QUERY_BIAS, ZERO, VALUE_BIAS, OUT_BIAS, SECOND_GAIN, SECOND_SHIFT, DOWN_BIAS, LIVE,
 UP_BIAS) = range(11)


def row_of(ref, n):
    return ref[n : n + 1, :]


def once(s):
    n = len(s)
    return pl.BlockSpec(s, lambda *_: (0,) * n, pipeline_mode=pl.Buffered(1))


def vectors_kernel(live_ref, *refs):
    out_ref = refs[-1]
    d = out_ref.shape[1]
    out_ref[...] = jnp.zeros_like(out_ref)
    at = (FIRST_GAIN, FIRST_SHIFT, QUERY_BIAS, VALUE_BIAS, OUT_BIAS, SECOND_GAIN, SECOND_SHIFT, DOWN_BIAS)
    for n, ref in zip(at, refs):
        out_ref[n : n + 1, :] = ref[...].reshape(1, d)
    for n in range(refs[-2].shape[0] // d):
        out_ref[UP_BIAS + n : UP_BIAS + n + 1, :] = refs[-2][pl.ds(n * d, d)].reshape(1, d)
    out_ref[LIVE : LIVE + 1, :] = jnp.full((1, d), live_ref[0], F32)


def vectors_call(vectors, live):
    d, ff = vectors[0].shape[0], vectors[-1].shape[0]
    v = pl.BlockSpec(memory_space=pltpu.VMEM)
    return pl.pallas_call(
        vectors_kernel,
        in_specs=[pl.BlockSpec(memory_space=pltpu.SMEM)] + [v] * len(vectors),
        out_shape=shape(((UP_BIAS + ff // d + 7) // 8 * 8, d), F32),
        compiler_params=params("vectors"),
        cost_estimate=cost(1),
        name="vectors",
    )(live, *vectors)


def joint_kernel(x_ref, w_ref, v_ref, a_ref, q_ref):
    d = x_ref.shape[1]

    def norm(i):
        n, _ = norm_stats(x_ref[pl.ds(i * ROWS, ROWS), :].astype(F32))
        return (n * row_of(v_ref, FIRST_GAIN) + row_of(v_ref, FIRST_SHIFT)).astype(BF)

    ahead = norm(0)
    for i in range(STEP // ROWS):
        a, rows = ahead, pl.ds(i * ROWS, ROWS)
        a_ref[rows, :] = a
        for j, bias in enumerate((QUERY_BIAS, ZERO, VALUE_BIAS)):
            if j == 1 and (i + 1) * ROWS < STEP:
                ahead = norm(i + 1)
            cols = pl.ds(j * d, d)
            t = (mm(a, w_ref[:, cols], 1, 0) + row_of(v_ref, bias)).astype(BF)
            q_ref[rows, cols] = t * jnp.asarray(0.125, BF) if j == 0 else t


def joint_call(x, w, vecs):
    L, d = x.shape
    return pl.pallas_call(
        joint_kernel,
        grid=(L // STEP,),
        in_specs=[pl.BlockSpec((STEP, d), lambda i: (i, 0)), once((d, 3 * d)), once(vecs.shape)],
        out_specs=[pl.BlockSpec((STEP, d), lambda i: (i, 0)), pl.BlockSpec((STEP, 3 * d), lambda i: (i, 0))],
        out_shape=[shape((L, d), BF), shape((L, 3 * d), BF)],
        compiler_params=params("joint", L),
        cost_estimate=cost(7),
        name="joint",
    )(x, w, vecs)


def tri_cols(L):
    n = L // ROWS
    return n * (n + 1) // 2 * ROWS


def attend_kernel(q_ref, k_ref, v_ref, o_ref, p_ref, i_ref):
    L = q_ref.shape[0]
    low = lax.broadcasted_iota(jnp.int32, (ROWS, 128), 1) < 64
    low_all = lax.broadcasted_iota(jnp.int32, (L, 128), 1) < 64
    tri = lax.broadcasted_iota(jnp.int32, (ROWS, ROWS), 1) <= lax.broadcasted_iota(jnp.int32, (ROWS, ROWS), 0)
    v = v_ref[...]
    one = jnp.ones_like(v)
    vs = [jnp.where(low_all, v, one), jnp.where(low_all, one, v)]
    jobs = [(i, h) for i in range(L // ROWS) for h in range(2)]

    def score(i, h):
        q = q_ref[pl.ds(i * ROWS, ROWS), :]
        qh = jnp.where(low if h == 0 else ~low, q, jnp.zeros_like(q))
        return mm(qh, k_ref[pl.ds(0, (i + 1) * ROWS), :], 1, 1)

    outs = [None, None]
    ahead = [score(*job) for job in jobs[:2]]
    for t, (i, h) in enumerate(jobs):
        s = ahead.pop(0)
        if t + 2 < len(jobs):
            ahead.append(score(*jobs[t + 2]))
        past = (i + 1) * ROWS
        diag = jnp.where(tri, s[:, i * ROWS :], -1e30)
        m = jnp.max(diag, axis=-1, keepdims=True)
        if i:
            m = jnp.maximum(m, jnp.max(s[:, : i * ROWS], axis=-1, keepdims=True))
            p = jnp.concatenate([jnp.exp(s[:, : i * ROWS] - m).astype(BF), jnp.exp(diag - m).astype(BF)], axis=1)
        else:
            p = jnp.exp(diag - m).astype(BF)
        p_ref[h, :, pl.ds(i * (i + 1) // 2 * ROWS, past)] = p
        outs[h] = mm(p, vs[h][:past], 1, 0)
        if h == 1:
            rows = pl.ds(i * ROWS, ROWS)
            inv = 1.0 / jnp.where(low, pltpu.roll(outs[0], 64, 1), pltpu.roll(outs[1], 64, 1))
            o_ref[rows, :] = (jnp.where(low, outs[0], outs[1]) * inv).astype(BF)
            i_ref[rows, :] = inv.astype(BF)


def attend_call(qkv):
    L, d3 = qkv.shape
    n = d3 // 3 // 128
    col = lambda k: pl.BlockSpec((L, 128), lambda j: (0, k * n + j))
    return pl.pallas_call(
        attend_kernel,
        grid=(n,),
        in_specs=[col(0), col(1), col(2)],
        out_specs=[col(0), pl.BlockSpec((2, ROWS, tri_cols(L)), lambda j: (j, 0, 0)), col(0)],
        out_shape=[shape((L, d3 // 3), BF), shape((2 * n, ROWS, tri_cols(L)), BF), shape((L, d3 // 3), BF)],
        compiler_params=params("attend", L),
        cost_estimate=cost(15),
        name="attend",
    )(qkv, qkv, qkv)


GC = math.sqrt(2.0 / math.pi)


def gelu_both(u):
    u2 = u * u
    t = jnp.tanh(u * (GC + GC * 0.044715 * u2))
    half = 0.5 + 0.5 * t
    return u * half, half + u * (0.5 - 0.5 * t * t) * (GC + 3 * GC * 0.044715 * u2)


def norm_back(e, n, r):
    return r * (e - jnp.mean(e, axis=-1, keepdims=True) - n * jnp.mean(e * n, axis=-1, keepdims=True))


def mlp_kernel(before, tiles, joined, after, steps, t_ref, *refs):
    refs = list(refs)
    take = lambda n: [refs.pop(0) for _ in range(n)]
    if before:
        m_ref, w_ref, x_ref = take(3)
    else:
        a_ref, = take(1)
    c_ref, up_ref, dn_ref, v_ref = take(4)
    if joined:
        other_ref, = take(1)
    if after:
        h_ref, m_ref, w_ref = take(3)
        past = take(after)
    if before:
        h_out, a_out = take(2)
    units = take(2 if joined else 1)
    gb_ref, = take(1)
    several = tiles > 1 or after
    if after:
        o_ref, gh_ref, gm_ref, dw_ref, sums_ref = take(5)
    else:
        r_out, e_out = take(2)
    act, gpre, r_acc, e_acc = take(4)
    if joined:
        unit, = take(1)
    if before:
        a_ref, = take(1)
    if after:
        acc, = take(1)
    j = pl.program_id(0)
    L, d = c_ref.shape
    lead = steps if before else 0

    if before:
        @pl.when(j < lead)
        def _():
            part = lambda i: mm(m_ref[pl.ds(i * ROWS, ROWS), :], w_ref[...], 1, 0)
            ahead = part(0)
            for i in range(STEP // ROWS):
                got, rows = ahead, pl.ds(i * ROWS, ROWS)
                if (i + 1) * ROWS < STEP:
                    ahead = part(i + 1)
                h = x_ref[rows, :].astype(F32) + got + row_of(v_ref, OUT_BIAS)
                h_out[rows, :] = h
                n, _ = norm_stats(h)
                a = (n * row_of(v_ref, SECOND_GAIN) + row_of(v_ref, SECOND_SHIFT)).astype(BF)
                a_out[rows, :] = a
                a_ref[pl.ds(pl.multiple_of(j * STEP + i * ROWS, ROWS), ROWS), :] = a

    @pl.when((j >= lead) & (j < lead + tiles))
    def _():
        bias = v_ref[pl.ds(UP_BIAS + t_ref[j - lead], 1), :]

        def pair(rows):
            return (mm(a_ref[rows, :], up_ref[...], 1, 0) + bias,
                    mm(c_ref[rows, :], dn_ref[...], 1, 1).astype(BF).astype(F32))

        def pass_rows(i, gb):
            rows = [pl.ds(pl.multiple_of(i * STEP + n * ROWS, ROWS), ROWS) for n in range(STEP // ROWS)]
            ahead = pair(rows[0])
            for n, here in enumerate(rows):
                u, ga = ahead
                if n + 1 < len(rows):
                    ahead = pair(rows[n + 1])
                g, dg = gelu_both(u)
                g = g.astype(BF)
                gp = (ga * dg).astype(BF)
                act[here, :] = g
                gpre[here, :] = gp
                gb = gb + jnp.sum(gp.astype(F32), axis=0, keepdims=True)
                r = mm(g, dn_ref[...], 1, 0)
                e = mm(gp, up_ref[...], 1, 1)
                if tiles > 1:
                    r = r + jnp.where(j > lead, r_acc[here, :], 0.0)
                    e = e + jnp.where(j > lead, e_acc[here, :], 0.0)
                if several:
                    r_acc[here, :] = r
                    e_acc[here, :] = e
                else:
                    r_out[here, :] = r.astype(BF)
                    e_out[here, :] = e.astype(BF)
            return gb

        gb_ref[0] = lax.fori_loop(0, L // STEP, pass_rows, jnp.zeros((1, d), F32))

        def weights(n, _):
            cols = pl.ds(pl.multiple_of(n * ROWS, ROWS), ROWS)
            under = pl.ds(pl.multiple_of(d + n * ROWS, ROWS), ROWS)
            down, up = mm(act[:, cols], c_ref[...], 0, 0), mm(a_ref[:, cols], gpre[...], 0, 0)
            into = unit if joined else units[0].at[0]
            if joined:
                down, up = down + other_ref[cols, :].astype(F32), up + other_ref[under, :].astype(F32)
            into[cols, :] = down.astype(BF)
            into[under, :] = up.astype(BF)
            return 0

        lax.fori_loop(0, d // ROWS, weights, 0)
        if joined:
            bit = t_ref[tiles]
            units[0][...] = unit[pl.ds(pl.multiple_of((1 - bit) * d, d), d), :]
            units[1][...] = unit[pl.ds(pl.multiple_of(bit * d, d), d), :]

    if not after:
        if several:
            @pl.when(j == lead + tiles - 1)
            def _():
                r_out[...] = r_acc[...].astype(BF)
                e_out[...] = e_acc[...].astype(BF)
        return

    @pl.when(j == tiles)
    def _():
        acc[...] = jnp.zeros_like(acc)
        sums_ref[...] = jnp.zeros_like(sums_ref)

    @pl.when(j >= tiles)
    def _():
        for i in range(STEP // ROWS):
            rows = pl.ds(i * ROWS, ROWS)
            at = pl.ds(pl.multiple_of((j - tiles) * STEP + i * ROWS, ROWS), ROWS)
            r, e = r_acc[at, :], e_acc[at, :]
            for n in range(0, after, 2):
                r = r + past[n][rows, :].astype(F32)
                e = e + past[n + 1][rows, :].astype(F32)
            h = h_ref[rows, :]
            o_ref[rows, :] = ((h + r + row_of(v_ref, DOWN_BIAS)) * row_of(v_ref, LIVE)).astype(BF)
            n, s = norm_stats(h)
            c = c_ref[at, :].astype(F32)
            gh = c + norm_back(e * row_of(v_ref, SECOND_GAIN), n, s)
            gh_ref[rows, :] = gh
            gb = gh.astype(BF)
            gm_ref[rows, :] = mm(gb, w_ref[...], 1, 1).astype(BF)
            acc[...] += mm(m_ref[rows, :], gb, 0, 0)
            add = lambda t: jnp.sum(t, axis=0, keepdims=True)
            sums_ref[0:1, :] += add(e * n)
            sums_ref[1:2, :] += add(e)
            sums_ref[2:3, :] += add(gb.astype(F32))
            sums_ref[3:4, :] += add(c)

    @pl.when(j == tiles + steps - 1)
    def _():
        dw_ref[...] = acc[...].astype(BF)


def mlp_call(tile_bit, tiles, c, up, dn, vecs, a=None, before=None, other=None, after=None):
    L, d = c.shape
    steps = L // STEP
    lead = steps if before else 0
    tile = lambda j: jnp.clip(j - lead, 0, tiles - 1)
    mode = dict(pipeline_mode=pl.Buffered(1)) if tiles == 1 else {}
    first = pl.BlockSpec((STEP, d), lambda j, _: (jnp.minimum(j, steps - 1), 0))
    last = pl.BlockSpec((STEP, d), lambda j, _: (jnp.clip(j - 1, 0, steps - 1), 0))
    seq = shape((L, d), BF)
    in_specs, args, out_specs, out_shape = [], [], [], []
    if before:
        in_specs += [first, once((d, d)), first]
        args += list(before)
        out_specs += [first, first]
        out_shape += [shape((L, d), F32), seq]
    else:
        in_specs += [once((L, d))]
        args += [a]
    in_specs += [once((L, d)), pl.BlockSpec((d, d), lambda j, t: (0, t[tile(j)]), **mode),
                 pl.BlockSpec((d, d), lambda j, t: (t[tile(j)], 0), **mode), once(vecs.shape)]
    args += [c, up, dn, vecs]
    scratch = [pltpu.VMEM((L, d), BF), pltpu.VMEM((L, d), BF)]
    scratch += [pltpu.VMEM((L, d), F32)] * 2 if after or tiles > 1 else [pltpu.VMEM((16, 128), F32)] * 2
    if other is not None:
        in_specs += [once((2 * d, d))]
        args += [other]
        out_specs += [whole((d, d))] * 2
        out_shape += [shape((d, d), BF)] * 2
        scratch += [pltpu.VMEM((2 * d, d), BF)]
    else:
        out_specs += [pl.BlockSpec((1, 2 * d, d), lambda j, _: (tile(j), 0, 0))]
        out_shape += [shape((tiles, 2 * d, d), BF)]
    out_specs += [pl.BlockSpec((1, 1, d), lambda j, _: (tile(j), 0, 0))]
    out_shape += [shape((tiles, 1, d), F32)]
    if before:
        scratch += [pltpu.VMEM((L, d), BF)]
    if after:
        in_specs += [last, last, once((d, d))] + [last] * (len(after) - 3)
        args += list(after)
        out_specs += [last, last, last, whole((d, d)), whole((8, d))]
        out_shape += [seq, shape((L, d), F32), seq, shape((d, d), BF), shape((8, d), F32)]
        scratch += [pltpu.VMEM((d, d), F32)]
    else:
        out_specs += [whole((L, d))] * 2
        out_shape += [seq, seq]
    return pl.pallas_call(
        partial(mlp_kernel, before is not None, tiles, other is not None, len(after) - 3 if after else 0, steps),
        grid_spec=pltpu.PrefetchScalarGridSpec(
            num_scalar_prefetch=1,
            grid=(tiles + lead + (steps if after else 0),),
            in_specs=in_specs, out_specs=out_specs, scratch_shapes=scratch,
        ),
        out_shape=out_shape,
        compiler_params=params("mlp", L),
        cost_estimate=cost(12 * tiles),
        name="mlp",
    )(tile_bit, *args)


def attend_back_kernel(q_ref, k_ref, v_ref, p_ref, i_ref, g_ref, m_ref, dq_ref, dk_ref, dv_ref, dk_acc, dv_acc):
    L = q_ref.shape[0]
    low = lax.broadcasted_iota(jnp.int32, (ROWS, 128), 1) < 64
    nb = L // ROWS
    jobs = [(i, h) for i in reversed(range(nb)) for h in range(2)]
    strips = {}
    def strip(i):
        if i not in strips:
            rows = pl.ds(i * ROWS, ROWS)
            g32 = g_ref[rows, :].astype(F32) * i_ref[rows, :].astype(F32)
            g = g32.astype(BF)
            gm = g32 * m_ref[rows, :].astype(F32)
            strips[i] = (g, gm, q_ref[rows, :].T, g.T)
        return strips[i]

    def dprob(i, h):
        g, gm, _, _ = strip(i)
        mine = low if h == 0 else ~low
        gh = jnp.where(mine, g, jnp.zeros_like(g))
        delta = jnp.sum(jnp.where(mine, gm, 0.0), axis=-1, keepdims=True)
        return mm(gh, v_ref[pl.ds(0, (i + 1) * ROWS), :], 1, 1), delta

    dqs = {}
    ahead = [dprob(*jobs[0])]
    for t, (i, h) in enumerate(jobs):
        dp, delta = ahead.pop(0)
        if t + 1 < len(jobs):
            ahead.append(dprob(*jobs[t + 1]))
        n = (i + 1) * ROWS
        past = pl.ds(0, n)
        _, _, qt, gt = strip(i)
        p = p_ref[h, :, pl.ds(i * (i + 1) // 2 * ROWS, n)]
        side = pl.ds(64 * h, 64)
        dv = mm(gt[64 * h : 64 * h + 64], p, 1, 0)
        ds = (p.astype(F32) * (dp - delta)).astype(BF)
        dqs[h] = mm(ds, k_ref[past, :], 1, 0)
        dk = mm(qt[64 * h : 64 * h + 64], ds, 1, 0)
        if i == nb - 1:
            dk_acc[side, past] = dk
            dv_acc[side, past] = dv
        else:
            dk_acc[side, past] += dk
            dv_acc[side, past] += dv
        if h == 1:
            dq_ref[pl.ds(i * ROWS, ROWS), :] = (jnp.where(low, dqs[0], dqs[1]) * 0.125).astype(BF)
    dk_ref[...] = dk_acc[...].T.astype(BF)
    dv_ref[...] = dv_acc[...].T.astype(BF)


def attend_back_call(qkv, p, inv, gm, mixed, lo, count, held=()):
    L, d3 = qkv.shape
    n = d3 // 3 // 128
    col = lambda k: pl.BlockSpec((L, 128), lambda j: (0, k * n + lo + j))
    s = shape((L, d3 // 3), BF)
    kernel = attend_back_kernel
    if held:
        kernel = lambda *refs: attend_back_kernel(*refs[:7], *refs[10:])
    return pl.pallas_call(
        kernel,
        grid=(count,),
        in_specs=[col(0), col(1), col(2), pl.BlockSpec((2, ROWS, tri_cols(L)), lambda j: (lo + j, 0, 0)), col(0), col(0), col(0)]
        + [pl.BlockSpec(memory_space=pl.ANY)] * len(held),
        out_specs=[col(0)] * 3,
        out_shape=[s] * 3,
        input_output_aliases={7 + i: i for i in range(len(held))},
        scratch_shapes=[pltpu.VMEM((128, L), F32), pltpu.VMEM((128, L), F32)],
        compiler_params=params("attend_back", L),
        cost_estimate=cost(3 * count),
        name="attend_back",
    )(qkv, qkv, qkv, p, inv, gm, mixed, *held)


def joint_sent_kernel(core_ref, a_ref, q_ref, k_ref, v_ref, w_ref, out_ref, sums_ref):
    d = a_ref.shape[1]
    sums_ref[...] = jnp.zeros_like(sums_ref)
    sums_ref[0:1, :] = jnp.sum(q_ref[...].astype(F32), axis=0, keepdims=True)
    sums_ref[1:2, :] = jnp.sum(v_ref[...].astype(F32), axis=0, keepdims=True)

    @pl.when(core_ref[0] == 1)
    def _():
        out_ref[0:d, :] = mm(a_ref[...], q_ref[...], 0, 0).astype(BF)
        out_ref[d : 2 * d, :] = mm(a_ref[...], k_ref[...], 0, 0).astype(BF)

    @pl.when(core_ref[0] == 0)
    def _():
        out_ref[0:d, :] = mm(a_ref[...], v_ref[...], 0, 0).astype(BF)
        out_ref[d : 2 * d, :] = w_ref[...]


def joint_sent_call(core, a, dq, dk, dv, dw):
    L, d = a.shape
    return pl.pallas_call(
        joint_sent_kernel,
        grid_spec=pltpu.PrefetchScalarGridSpec(
            num_scalar_prefetch=1, grid=(1,), in_specs=[once((L, d))] * 4 + [once((d, d))],
            out_specs=[whole((2 * d, d)), whole((8, d))]),
        out_shape=[shape((2 * d, d), BF), shape((8, d), F32)],
        compiler_params=params("joint_sent", L),
        cost_estimate=cost(5),
        name="joint_sent",
    )(core, a, dq, dk, dv, dw)


def joint_kept_kernel(core_ref, a_ref, q_ref, k_ref, v_ref, w_ref, other_ref, sent_ref, kept_ref, unit):
    d = a_ref.shape[1]
    add = lambda t, n: (t + other_ref[n * d : (n + 1) * d, :].astype(F32)).astype(BF)

    @pl.when(core_ref[0] == 0)
    def _():
        unit[0:d, :] = add(mm(a_ref[...], q_ref[...], 0, 0), 0)
        unit[d : 2 * d, :] = add(mm(a_ref[...], k_ref[...], 0, 0), 1)

    @pl.when(core_ref[0] == 1)
    def _():
        unit[0:d, :] = add(mm(a_ref[...], v_ref[...], 0, 0), 0)
        unit[d : 2 * d, :] = add(w_ref[...].astype(F32), 1)

    bit = core_ref[1]
    sent_ref[...] = unit[pl.ds(pl.multiple_of((1 - bit) * d, d), d), :]
    kept_ref[...] = unit[pl.ds(pl.multiple_of(bit * d, d), d), :]


def joint_kept_call(core_bit, a, dq, dk, dv, dw, other):
    L, d = a.shape
    return pl.pallas_call(
        joint_kept_kernel,
        grid_spec=pltpu.PrefetchScalarGridSpec(
            num_scalar_prefetch=1, grid=(1,), in_specs=[once((L, d))] * 4 + [once((d, d)), once((2 * d, d))],
            out_specs=[whole((d, d)), whole((d, d))], scratch_shapes=[pltpu.VMEM((2 * d, d), BF)]),
        out_shape=[shape((d, d), BF)] * 2,
        compiler_params=params("joint_kept", L),
        cost_estimate=cost(5),
        name="joint_kept",
    )(core_bit, a, dq, dk, dv, dw, other)


def tokens_kernel(q_ref, k_ref, v_ref, w_ref, x_ref, gh_ref, vec_ref, o_ref, sums_ref):
    i = pl.program_id(0)
    d = x_ref.shape[1]

    @pl.when(i == 0)
    def _():
        sums_ref[...] = jnp.zeros_like(sums_ref)

    def back(i):
        rows = pl.ds(i * ROWS, ROWS)
        return (mm(q_ref[rows, :], w_ref[:, 0:d], 1, 1) + mm(k_ref[rows, :], w_ref[:, d : 2 * d], 1, 1)
                + mm(v_ref[rows, :], w_ref[:, 2 * d :], 1, 1))

    ahead = back(0)
    for j in range(STEP // ROWS):
        e, rows = ahead, pl.ds(j * ROWS, ROWS)
        if (j + 1) * ROWS < STEP:
            ahead = back(j + 1)
        n, r = norm_stats(x_ref[rows, :].astype(F32))
        o_ref[rows, :] = (gh_ref[rows, :] + norm_back(e * row_of(vec_ref, FIRST_GAIN), n, r)).astype(BF)
        sums_ref[0:1, :] += jnp.sum(e * n, axis=0, keepdims=True)
        sums_ref[1:2, :] += jnp.sum(e, axis=0, keepdims=True)


def tokens_call(dq, dk, dv, w, x, gh, vecs):
    L, d = x.shape
    blk = pl.BlockSpec((STEP, d), lambda i: (i, 0))
    return pl.pallas_call(
        tokens_kernel,
        grid=(L // STEP,),
        in_specs=[blk, blk, blk, once((d, 3 * d)), blk, blk, once(vecs.shape)],
        out_specs=[blk, whole((8, d))],
        out_shape=[shape((L, d), BF), shape((8, d), F32)],
        compiler_params=params("tokens_back", L),
        cost_estimate=cost(9),
        name="tokens_back",
    )(dq, dk, dv, w, x, gh, vecs)


def place_kernel(core_ref, own_ref, other_ref, *rest):
    down_ref, up_ref = rest[-2:]
    d = down_ref.shape[1]
    for n, ref in enumerate((own_ref, other_ref)):
        @pl.when(pl.program_id(0) == n)
        def _(ref=ref):
            down_ref[...] = ref[0:d, :].astype(F32)
            up_ref[...] = ref[d : 2 * d, :].astype(F32)


def place_call(core, own, other, tile, ff, held=()):
    d = own.shape[1]
    at = lambda n, s: tile + jnp.where(n == 0, s[0], 1 - s[0])
    return pl.pallas_call(
        place_kernel,
        grid_spec=pltpu.PrefetchScalarGridSpec(
            num_scalar_prefetch=1,
            grid=(2,),
            in_specs=[whole((2 * d, d))] * 2 + [pl.BlockSpec(memory_space=pl.ANY)] * len(held),
            out_specs=[pl.BlockSpec((d, d), lambda n, s: (at(n, s), 0)), pl.BlockSpec((d, d), lambda n, s: (0, at(n, s)))],
        ),
        out_shape=[shape((ff, d), F32), shape((d, ff), F32)],
        input_output_aliases={3 + i: i for i in range(len(held))},
        compiler_params=params("place"),
        cost_estimate=cost(5),
        name="place",
    )(core, own, other, *held)


def place_joint_kernel(core_ref, own_ref, other_ref, joint_ref, out_ref, small_ref):
    d = out_ref.shape[0]

    for core, (qk_ref, vw_ref) in enumerate(((own_ref, other_ref), (other_ref, own_ref))):
        @pl.when(core_ref[0] == core)
        def _(qk_ref=qk_ref, vw_ref=vw_ref):
            joint_ref[:, 0:d] = qk_ref[0:d, :].astype(F32)
            joint_ref[:, d : 2 * d] = qk_ref[d : 2 * d, :].astype(F32)
            joint_ref[:, 2 * d : 3 * d] = vw_ref[0:d, :].astype(F32)
            out_ref[...] = vw_ref[d : 2 * d, :].astype(F32)

    small_ref[...] = own_ref[2 * d :, :].astype(F32) + other_ref[2 * d :, :].astype(F32)


def place_joint(core, own, other):
    rows, d = own.shape
    v = pl.BlockSpec(memory_space=pltpu.VMEM)
    return pl.pallas_call(
        place_joint_kernel,
        in_specs=[pl.BlockSpec(memory_space=pltpu.SMEM), v, v],
        out_specs=[v] * 3,
        out_shape=[shape((d, 3 * d), F32), shape((d, d), F32), shape((rows - 2 * d, d), F32)],
        compiler_params=params("place_joint"),
        cost_estimate=cost(5),
        name="place_joint",
    )(core, own, other)


def halve_kernel(up_ref, a_ref, b_ref, c_ref, d_ref, sent_ref, kept_ref):
    sent_ref[...] = a_ref[...] + b_ref[...]
    kept_ref[...] = c_ref[...] + d_ref[...]


def halve_call(up, kept, other):
    rows, d = kept.shape[0] // 2, kept.shape[1]
    block = rows if rows <= 384 else rows // 2
    n = rows // block
    go = pl.BlockSpec((block, d), lambda i, up: ((1 - up[0]) * n + i, 0))
    stay = pl.BlockSpec((block, d), lambda i, up: (up[0] * n + i, 0))
    out = pl.BlockSpec((block, d), lambda i, up: (i, 0))
    s = shape((rows, d), BF)
    return pl.pallas_call(
        halve_kernel,
        grid_spec=pltpu.PrefetchScalarGridSpec(
            num_scalar_prefetch=1, grid=(n,), in_specs=[go, go, stay, stay], out_specs=[out, out]),
        out_shape=[s, s],
        compiler_params=params("halve"),
        cost_estimate=cost(2),
        name="halve",
    )(up, kept, other, kept, other)


def double_kernel(rows, up_ref, a_ref, b_ref, o_ref):
    up = up_ref[0]
    o_ref[pl.ds(pl.multiple_of(up * rows, 16), rows), :] = a_ref[0:rows, :]
    o_ref[pl.ds(pl.multiple_of((1 - up) * rows, 16), rows), :] = b_ref[0:rows, :]
    if a_ref.shape[0] > rows:
        tail = a_ref[rows:, :].astype(F32) + b_ref[rows:, :].astype(F32)
        o_ref[2 * rows :, :] = tail.astype(BF)


def double_call(up, kept, other, tail=0):
    rows, d = kept.shape[0] - tail, kept.shape[1]
    v = pl.BlockSpec(memory_space=pltpu.VMEM)
    return pl.pallas_call(
        partial(double_kernel, rows),
        in_specs=[pl.BlockSpec(memory_space=pltpu.SMEM), v, v],
        out_specs=v,
        out_shape=shape((2 * rows + tail, d), BF),
        compiler_params=params("double"),
        cost_estimate=cost(2),
        name="double",
    )(up, kept, other)


def arrange_kernel(places, at_ref, *refs):
    out_ref = refs[-1]
    for k, ref in enumerate(refs[:-1]):
        if places < len(refs) - 1:
            @pl.when(at_ref[k] < places)
            def _(k=k, ref=ref):
                out_ref[at_ref[k]] = ref[...]
        else:
            out_ref[at_ref[k]] = ref[...]


def arrange_call(at, parts, places):
    block, d = parts[0].shape
    v = pl.BlockSpec(memory_space=pltpu.VMEM)
    return pl.pallas_call(
        partial(arrange_kernel, places),
        in_specs=[pl.BlockSpec(memory_space=pltpu.SMEM)] + [v] * len(parts),
        out_specs=v,
        out_shape=shape((places, block, d), BF),
        compiler_params=params("arrange"),
        cost_estimate=cost(2),
        name="arrange",
    )(at, *parts)


def small_kernel(core_ref, first_ref, joint_ref, second_ref, b0, b1, b2, b3, o_ref):
    o_ref[...] = jnp.zeros_like(o_ref)
    o_ref[0:2, :] = first_ref[0:2, :].astype(BF)
    o_ref[2:4, :] = joint_ref[0:2, :].astype(BF)
    o_ref[4:8, :] = second_ref[0:4, :].astype(BF)
    for n, (u, v) in enumerate(((b0, b1), (b1, b0), (b2, b3), (b3, b2))):
        o_ref[8 + n : 9 + n, :] = jnp.where(core_ref[0] == 0, u[0], v[0]).astype(BF)


def small_call(core, first, joint, second, up_bias):
    v = pl.BlockSpec(memory_space=pltpu.VMEM)
    return pl.pallas_call(
        small_kernel,
        in_specs=[pl.BlockSpec(memory_space=pltpu.SMEM)] + [v] * 7,
        out_specs=v,
        out_shape=shape((16, first.shape[1]), BF),
        compiler_params=params("small"),
        cost_estimate=cost(1),
        name="small",
    )(core, first, joint, second, *up_bias)


def bits_of(count):
    assert count & (count - 1) == 0
    return count.bit_length() - 1


class Moves:
    def __init__(self, n_dp, n_blk, slots):
        assert slots <= n_blk
        self.n_dp, self.n_blk, self.slots = n_dp, n_blk, slots
        self.dp, self.blk = lax.axis_index("dp"), lax.axis_index("blk")
        self.odd = self.dp % 2

    def slot(self, blk):
        return jnp.where(self.odd == 1, self.n_blk - 1 - blk, blk)

    def perm(self, step, back):
        pairs = []
        for g in range(self.n_dp):
            for b in range(self.n_blk):
                d = (b + step) % self.n_blk
                s = self.n_blk - 1 - d if g % 2 else d
                if s < self.slots:
                    pair = (g * self.n_blk + b, g * self.n_blk + d)
                    pairs.append(pair[::-1] if back else pair)
        return pairs

    def send_out(self, x, beside=None):
        parts = []
        for step in range(self.n_blk):
            if beside is not None and step == self.n_blk - 1:
                x = lax.optimization_barrier((x, beside))[0]
            s = jnp.minimum(self.slot((self.blk + step) % self.n_blk), self.slots - 1)
            part = lax.dynamic_index_in_dim(x, s, 0, keepdims=False)
            parts.append(lax.ppermute(part, ("dp", "blk"), self.perm(step, False)) if step else part)
        return parts

    def join(self, parts):
        at = (self.blk - jnp.arange(self.n_blk, dtype=jnp.int32)) % self.n_blk
        return arrange_call(at, parts, self.n_blk).reshape(-1, parts[0].shape[1])

    def send_back(self, y):
        y = y.reshape(self.n_blk, -1, y.shape[-1])
        parts = []
        for step in range(self.n_blk):
            part = lax.dynamic_index_in_dim(y, (self.blk - step) % self.n_blk, 0, keepdims=False)
            parts.append(lax.ppermute(part, ("dp", "blk"), self.perm(step, True)) if step else part)
        return parts

    def unjoin(self, parts):
        at = self.slot((self.blk + jnp.arange(self.n_blk, dtype=jnp.int32)) % self.n_blk)
        return arrange_call(at, parts, self.slots)


class Order:
    def __init__(self):
        self.last = None

    def take(self, *arrays):
        if self.last is not None:
            arrays = lax.optimization_barrier(arrays + (self.last,))[:-1]
        return arrays if len(arrays) > 1 else arrays[0]

    def mark(self, array):
        self.last = array


class Sum:
    def __init__(self, moves):
        self.n = moves.n_dp * moves.n_blk
        self.me = moves.dp * moves.n_blk + moves.blk
        low, high = bits_of(moves.n_blk), bits_of(moves.n_dp)
        plane = [low + 1 + i for i in range(high - 1)]
        self.core = low
        self.orders = [plane + list(range(low)), plane[::-1] + list(range(low))]
        self.stages = len(self.orders[0])
        self.tail = None

    def order(self, i, stage):
        return self.core if stage < 0 else self.orders[(i >> self.core) & 1][stage]

    def swap(self, x, stage):
        return lax.ppermute(x, ("dp", "blk"), [(i, i ^ (1 << self.order(i, stage))) for i in range(self.n)])

    def up(self, stage, me=None):
        me = self.me if me is None else me
        odd = (me >> self.core) & 1
        return jnp.where(odd == 0, (me >> self.order(0, stage)) & 1, (me >> self.order(1 << self.core, stage)) & 1)

    def cross(self, sent):
        self.moving = self.swap(sent, -1)

    def crossed(self, order):
        return order.take(self.moving)

    def begin(self, sent, kept):
        self.sent, self.kept, self.stage, self.gathering = sent, kept, 0, False
        self.send()

    def send(self):
        if not self.gathering:
            self.moving = self.swap(self.sent, self.stage)
        else:
            self.moving = self.swap(self.kept, self.stage)

    def step(self, order):
        other, self.kept = order.take(self.moving, self.kept)
        if not self.gathering:
            self.stage += 1
            if self.stage == self.stages:
                self.kept = self.kept + other
                if self.tail is not None:
                    self.kept = jnp.concatenate([self.kept, self.tail])
                self.gathering = True
                self.stage -= 1
            else:
                half = self.kept.shape[0] // 2
                up = self.up(self.stage)
                if half % 16 == 0:
                    self.sent, self.kept = halve_call(up.reshape(1), self.kept, other)
                else:
                    part = lambda x, at: lax.dynamic_slice_in_dim(x, at * half, half, 0)
                    self.sent = part(self.kept, 1 - up) + part(other, 1 - up)
                    self.kept = part(self.kept, up) + part(other, up)
        else:
            tail = 0 if self.tail is None else self.tail.shape[0]
            self.kept = double_call(self.up(self.stage).reshape(1), self.kept, other, tail)
            self.stage -= 1
        order.mark(self.kept)
        self.send()

    def finish(self, order):
        theirs = order.take(self.moving)
        return ((self.me >> self.core) & 1).reshape(1), self.kept, theirs


PLAN = (
    "m1", "m2", "m3", "m4", "o", "1", "ab1", "1", "x", "ab2", "2", "1", "O", "js", "2", "jk", "1", "2", "tok", "3",
    "1", "3", "2", "1", "3", "2", "3", "1", "3", "2", "1", "g", "3", "2", "a", "3", "1", "b", "3", "c", "2", "3",
    "G", "2",
)


def on_device(n_dp, n_blk, tokens, live_count, first_gain, first_shift, joint_weight, query_bias, value_bias,
              out_weight, out_bias, second_gain, second_shift, up_weight, up_bias, down_weight, down_bias, cotangent):
    slots, block, d = tokens.shape
    ff = up_weight.shape[1]
    assert ff == 4 * d
    pairs = d // 128
    moves = Moves(n_dp, n_blk, slots)
    order = Order()
    mine = moves.slot(moves.blk)
    live = ((mine < slots) & (mine < live_count[0])).astype(F32)
    core = moves.odd.reshape(1)
    vecs = vectors_call([first_gain, first_shift, query_bias, value_bias, out_bias, second_gain, second_shift,
                         down_bias, up_bias], live.reshape(1))
    live_slots = jnp.arange(slots, dtype=jnp.int32) < live_count[0]

    x_parts = moves.send_out(tokens, vecs)
    x = moves.join(x_parts)
    attn_in, qkv = joint_call(x, joint_weight, vecs)
    c = jnp.where(live_slots[:, None, None], lax.optimization_barrier((cotangent, x))[0], jnp.zeros_like(cotangent))
    c_parts = moves.send_out(c)
    c_parts[0] = jnp.where(mine < slots, c_parts[0], jnp.zeros_like(c_parts[0]))
    mixed, p, inv = attend_call(qkv)
    order.mark(mixed)
    c = moves.join(list(order.take(*c_parts)))

    sums = {name: Sum(moves) for name in "123"}
    got = {}
    bit = sums["2"].up(0).reshape(1)
    tile = lambda which, tiles, **more: mlp_call(which, tiles, c, up_weight, down_weight, vecs, **more)

    def m1():
        got["hidden"], got["a"], sent, got["gb1"], *past = tile(1 - core, 1, before=(mixed, out_weight, x))
        sums["1"].cross(sent[0])
        got["past"] = tuple(past)
        return past[0]

    def m2():
        sent, got["gb3"], *past = tile(3 - core, 1, a=order.take(got["a"]))
        sums["2"].cross(sent[0])
        got["past"] += tuple(past)
        return past[0]

    def m3():
        other = sums["1"].crossed(order)
        sent, kept, got["gb0"], *past = tile(jnp.concatenate([core, bit]), 1, a=order.take(got["a"]), other=other)
        sums["1"].begin(sent, kept)
        got["past"] += tuple(past)
        return past[0]

    def m4():
        other = sums["2"].crossed(order)
        after = (got["hidden"], mixed, out_weight) + got["past"]
        sent, kept, gb, out, gh, gm, dwo, s = tile(jnp.concatenate([2 + core, bit]), 1, a=order.take(got["a"]), other=other,
                                                   after=after)
        sums["2"].begin(sent, kept)
        got.update(gb2=gb, out=out, gh=gh, gm=gm, dwo=dwo, sums2=s)
        return gh

    def ab1():
        count = pairs // 2 if "ab2" in PLAN else pairs
        got["back"] = attend_back_call(qkv, p, inv, order.take(got["gm"]), mixed, 0, count)
        return got["back"][0]

    def ab2():
        got["back"] = attend_back_call(qkv, p, inv, order.take(got["gm"]), mixed, pairs // 2, pairs - pairs // 2,
                                       got["back"])
        return got["back"][0]

    def js():
        sent, got["sums1"] = joint_sent_call(core, order.take(attn_in), *got["back"], got["dwo"])
        sums["3"].cross(sent)
        return sent

    def jk():
        other = sums["3"].crossed(order)
        sent, kept = joint_kept_call(jnp.concatenate([core, bit]), order.take(attn_in), *got["back"], got["dwo"], other)
        sums["3"].begin(sent, kept)
        return kept

    def tok():
        dq, dk, dv = got["back"]
        got["gx"], sums0 = tokens_call(order.take(dq), dk, dv, joint_weight, x, got["gh"], vecs)
        order.mark(got["gx"])
        sums["3"].tail = small_call(core, order.take(sums0), got["sums1"], got["sums2"], [got["gb%d" % n] for n in range(4)])
        return sums["3"].tail

    def send(name):
        got[name + "_parts"] = moves.send_back(order.take(got[name]))

    def part(name, k):
        parts = got[name + "_parts"]
        if k < len(parts):
            parts[k] = order.take(parts[k])
            order.mark(parts[k])

    def join(name):
        got[name] = moves.unjoin(list(order.take(*got[name + "_parts"])))
        return got[name]

    def step(name):
        total = sums.get(name)
        if total is None:
            return
        if not total.gathering or total.stage >= 0:
            total.step(order)
        else:
            sums[name] = None
            if name == "3":
                got["joint"] = place_joint(*total.finish(order))
                order.mark(got["joint"][1])
            else:
                got["wide"] = place_call(*total.finish(order), 2 * int(name) - 2, ff, got.get("wide", ()))
                order.mark(got["wide"][0])

    kernels = dict(m1=m1, m2=m2, m3=m3, m4=m4, ab1=ab1, ab2=ab2, js=js, jk=jk, tok=tok)
    for word in PLAN + ("2", "1", "3") * 12:
        if word in kernels:
            order.mark(kernels[word]())
        elif word in "abc":
            part("gx", 1 + "abc".index(word))
        elif word in "xyz":
            part("out", 1 + "xyz".index(word))
        elif word in "og":
            send({"o": "out", "g": "gx"}[word])
        elif word in "OG":
            order.mark(join({"O": "out", "G": "gx"}[word]))
        else:
            step(word)
    small = got["joint"][2]
    return (got["out"], got["gx"], small[0], small[1], got["joint"][0], small[2], small[3], got["joint"][1], small[6],
            small[4], small[5], got["wide"][1], small[8:12].reshape(-1), got["wide"][0], small[7])


def solution(mesh):
    seq = P("dp", "blk", None)
    n_dp, n_blk = mesh.shape["dp"], mesh.shape["blk"]
    return jax.shard_map(
        partial(on_device, n_dp, n_blk), mesh=mesh,
        in_specs=(seq, P("dp")) + (P(),) * 13 + (seq,),
        out_specs=(seq, seq) + (P(),) * 13,
        check_vma=False,
    )
```

```python
import math
from functools import partial
import jax
import jax.numpy as jnp
from jax import lax
from jax.experimental import pallas as pl
from jax.experimental.pallas import tpu as pltpu
from jax.sharding import PartitionSpec as P

BF = jnp.bfloat16
F32 = jnp.float32
HEADS = 12
EPS = 1e-5
ROWS = 256
STEP = 512
COST = 1000
MIB = dict(arrange=8, double=16, halve=16, joint=30, joint_kept=30, joint_sent=30, mlp=57, place=30, place_joint=30,
           small=8, tokens_back=24, vectors=8)


def params(name, length=1024):
    return pltpu.CompilerParams(vmem_limit_bytes=min(60, MIB.get(name, 60) * max(length, 1024) // 1024) * 2**20)


def cost(us):
    return pl.CostEstimate(flops=int(us * COST), bytes_accessed=1000, transcendentals=0)


def mm(a, b, ca, cb):
    return lax.dot_general(a, b, (((ca,), (cb,)), ((), ())), preferred_element_type=F32)


def shape(s, d):
    return pltpu.HBM(s, d)


def whole(s):
    n = len(s)
    return pl.BlockSpec(s, lambda *_: (0,) * n)


def norm_stats(t):
    c = t - jnp.mean(t, axis=-1, keepdims=True)
    r = lax.rsqrt(jnp.mean(c * c, axis=-1, keepdims=True) + EPS)
    return c * r, r


(FIRST_GAIN, FIRST_SHIFT, QUERY_BIAS, ZERO, VALUE_BIAS, OUT_BIAS, SECOND_GAIN, SECOND_SHIFT, DOWN_BIAS, LIVE,
 UP_BIAS) = range(11)


def row_of(ref, n):
    return ref[n : n + 1, :]


def once(s):
    n = len(s)
    return pl.BlockSpec(s, lambda *_: (0,) * n, pipeline_mode=pl.Buffered(1))


def vectors_kernel(live_ref, *refs):
    out_ref = refs[-1]
    d = out_ref.shape[1]
    out_ref[...] = jnp.zeros_like(out_ref)
    at = (FIRST_GAIN, FIRST_SHIFT, QUERY_BIAS, VALUE_BIAS, OUT_BIAS, SECOND_GAIN, SECOND_SHIFT, DOWN_BIAS)
    for n, ref in zip(at, refs):
        out_ref[n : n + 1, :] = ref[...].reshape(1, d)
    for n in range(refs[-2].shape[0] // d):
        out_ref[UP_BIAS + n : UP_BIAS + n + 1, :] = refs[-2][pl.ds(n * d, d)].reshape(1, d)
    out_ref[LIVE : LIVE + 1, :] = jnp.full((1, d), live_ref[0], F32)


def vectors_call(vectors, live):
    d, ff = vectors[0].shape[0], vectors[-1].shape[0]
    v = pl.BlockSpec(memory_space=pltpu.VMEM)
    return pl.pallas_call(
        vectors_kernel,
        in_specs=[pl.BlockSpec(memory_space=pltpu.SMEM)] + [v] * len(vectors),
        out_shape=shape(((UP_BIAS + ff // d + 7) // 8 * 8, d), F32),
        compiler_params=params("vectors"),
        cost_estimate=cost(1),
        name="vectors",
    )(live, *vectors)


def joint_kernel(x_ref, w_ref, v_ref, a_ref, q_ref):
    d = x_ref.shape[1]

    def norm(i):
        n, _ = norm_stats(x_ref[pl.ds(i * ROWS, ROWS), :].astype(F32))
        return (n * row_of(v_ref, FIRST_GAIN) + row_of(v_ref, FIRST_SHIFT)).astype(BF)

    ahead = norm(0)
    for i in range(STEP // ROWS):
        a, rows = ahead, pl.ds(i * ROWS, ROWS)
        a_ref[rows, :] = a
        for j, bias in enumerate((QUERY_BIAS, ZERO, VALUE_BIAS)):
            if j == 1 and (i + 1) * ROWS < STEP:
                ahead = norm(i + 1)
            cols = pl.ds(j * d, d)
            t = (mm(a, w_ref[:, cols], 1, 0) + row_of(v_ref, bias)).astype(BF)
            q_ref[rows, cols] = t * jnp.asarray(0.125, BF) if j == 0 else t


def joint_call(x, w, vecs):
    L, d = x.shape
    return pl.pallas_call(
        joint_kernel,
        grid=(L // STEP,),
        in_specs=[pl.BlockSpec((STEP, d), lambda i: (i, 0)), once((d, 3 * d)), once(vecs.shape)],
        out_specs=[pl.BlockSpec((STEP, d), lambda i: (i, 0)), pl.BlockSpec((STEP, 3 * d), lambda i: (i, 0))],
        out_shape=[shape((L, d), BF), shape((L, 3 * d), BF)],
        compiler_params=params("joint", L),
        cost_estimate=cost(7),
        name="joint",
    )(x, w, vecs)


def tri_cols(L):
    n = L // ROWS
    return n * (n + 1) // 2 * ROWS


def attend_kernel(q_ref, k_ref, v_ref, o_ref, p_ref, i_ref):
    L = q_ref.shape[0]
    low = lax.broadcasted_iota(jnp.int32, (ROWS, 128), 1) < 64
    low_all = lax.broadcasted_iota(jnp.int32, (L, 128), 1) < 64
    tri = lax.broadcasted_iota(jnp.int32, (ROWS, ROWS), 1) <= lax.broadcasted_iota(jnp.int32, (ROWS, ROWS), 0)
    v = v_ref[...]
    one = jnp.ones_like(v)
    vs = [jnp.where(low_all, v, one), jnp.where(low_all, one, v)]
    jobs = [(i, h) for i in range(L // ROWS) for h in range(2)]

    def score(i, h):
        q = q_ref[pl.ds(i * ROWS, ROWS), :]
        qh = jnp.where(low if h == 0 else ~low, q, jnp.zeros_like(q))
        return mm(qh, k_ref[pl.ds(0, (i + 1) * ROWS), :], 1, 1)

    outs = [None, None]
    ahead = [score(*job) for job in jobs[:2]]
    for t, (i, h) in enumerate(jobs):
        s = ahead.pop(0)
        if t + 2 < len(jobs):
            ahead.append(score(*jobs[t + 2]))
        past = (i + 1) * ROWS
        diag = jnp.where(tri, s[:, i * ROWS :], -1e30)
        m = jnp.max(diag, axis=-1, keepdims=True)
        if i:
            m = jnp.maximum(m, jnp.max(s[:, : i * ROWS], axis=-1, keepdims=True))
            p = jnp.concatenate([jnp.exp(s[:, : i * ROWS] - m).astype(BF), jnp.exp(diag - m).astype(BF)], axis=1)
        else:
            p = jnp.exp(diag - m).astype(BF)
        p_ref[h, :, pl.ds(i * (i + 1) // 2 * ROWS, past)] = p
        outs[h] = mm(p, vs[h][:past], 1, 0)
        if h == 1:
            rows = pl.ds(i * ROWS, ROWS)
            inv = 1.0 / jnp.where(low, pltpu.roll(outs[0], 64, 1), pltpu.roll(outs[1], 64, 1))
            o_ref[rows, :] = (jnp.where(low, outs[0], outs[1]) * inv).astype(BF)
            i_ref[rows, :] = inv.astype(BF)


def attend_call(qkv):
    L, d3 = qkv.shape
    n = d3 // 3 // 128
    col = lambda k: pl.BlockSpec((L, 128), lambda j: (0, k * n + j))
    return pl.pallas_call(
        attend_kernel,
        grid=(n,),
        in_specs=[col(0), col(1), col(2)],
        out_specs=[col(0), pl.BlockSpec((2, ROWS, tri_cols(L)), lambda j: (j, 0, 0)), col(0)],
        out_shape=[shape((L, d3 // 3), BF), shape((2 * n, ROWS, tri_cols(L)), BF), shape((L, d3 // 3), BF)],
        compiler_params=params("attend", L),
        cost_estimate=cost(15),
        name="attend",
    )(qkv, qkv, qkv)


GC = math.sqrt(2.0 / math.pi)


def gelu_both(u):
    u2 = u * u
    t = jnp.tanh(u * (GC + GC * 0.044715 * u2))
    half = 0.5 + 0.5 * t
    return u * half, half + u * (0.5 - 0.5 * t * t) * (GC + 3 * GC * 0.044715 * u2)


def norm_back(e, n, r):
    return r * (e - jnp.mean(e, axis=-1, keepdims=True) - n * jnp.mean(e * n, axis=-1, keepdims=True))


def mlp_kernel(before, tiles, joined, after, steps, t_ref, *refs):
    refs = list(refs)
    take = lambda n: [refs.pop(0) for _ in range(n)]
    if before:
        m_ref, w_ref, x_ref = take(3)
    else:
        a_ref, = take(1)
    c_ref, up_ref, dn_ref, v_ref = take(4)
    if joined:
        other_ref, = take(1)
    if after:
        w_ref, *late = take(3 + after)
    if before:
        h_out, a_out = take(2)
    units = take(2 if joined else 1)
    gb_ref, = take(1)
    several = tiles > 1 or after
    if after:
        o_ref, gh_ref, gm_ref, dw_ref, sums_ref = take(5)
    else:
        r_out, e_out = take(2)
    act, gpre, r_acc, e_acc = take(4)
    if joined:
        unit, = take(1)
    if before:
        a_ref, = take(1)
    if after:
        acc, sems, *held = take(4 + after)
    j = pl.program_id(0)
    L, d = c_ref.shape
    lead = steps if before else 0

    def block(s):
        rows = pl.ds(s * STEP, STEP)
        return [pltpu.make_async_copy(src.at[rows, :], dst.at[s % 2], sems.at[s % 2, n])
                for n, (src, dst) in enumerate(zip(late, held))]

    if after:
        @pl.when(j == 0)
        def _():
            for s in range(2):
                for c in block(s):
                    c.start()

    if before:
        @pl.when(j < lead)
        def _():
            part = lambda i: mm(m_ref[pl.ds(i * ROWS, ROWS), :], w_ref[...], 1, 0)
            ahead = part(0)
            for i in range(STEP // ROWS):
                got, rows = ahead, pl.ds(i * ROWS, ROWS)
                if (i + 1) * ROWS < STEP:
                    ahead = part(i + 1)
                h = x_ref[rows, :].astype(F32) + got + row_of(v_ref, OUT_BIAS)
                h_out[rows, :] = h
                n, _ = norm_stats(h)
                a = (n * row_of(v_ref, SECOND_GAIN) + row_of(v_ref, SECOND_SHIFT)).astype(BF)
                a_out[rows, :] = a
                a_ref[pl.ds(pl.multiple_of(j * STEP + i * ROWS, ROWS), ROWS), :] = a

    @pl.when((j >= lead) & (j < lead + tiles))
    def _():
        bias = v_ref[pl.ds(UP_BIAS + t_ref[j - lead], 1), :]

        def pair(rows):
            return (mm(a_ref[rows, :], up_ref[...], 1, 0) + bias,
                    mm(c_ref[rows, :], dn_ref[...], 1, 1).astype(BF).astype(F32))

        def pass_rows(i, gb):
            rows = [pl.ds(pl.multiple_of(i * STEP + n * ROWS, ROWS), ROWS) for n in range(STEP // ROWS)]
            ahead = pair(rows[0])
            for n, here in enumerate(rows):
                u, ga = ahead
                if n + 1 < len(rows):
                    ahead = pair(rows[n + 1])
                g, dg = gelu_both(u)
                g = g.astype(BF)
                gp = (ga * dg).astype(BF)
                act[here, :] = g
                gpre[here, :] = gp
                gb = gb + jnp.sum(gp.astype(F32), axis=0, keepdims=True)
                r = mm(g, dn_ref[...], 1, 0)
                e = mm(gp, up_ref[...], 1, 1)
                if tiles > 1:
                    r = r + jnp.where(j > lead, r_acc[here, :], 0.0)
                    e = e + jnp.where(j > lead, e_acc[here, :], 0.0)
                if several:
                    r_acc[here, :] = r
                    e_acc[here, :] = e
                else:
                    r_out[here, :] = r.astype(BF)
                    e_out[here, :] = e.astype(BF)
            return gb

        gb_ref[0] = lax.fori_loop(0, L // STEP, pass_rows, jnp.zeros((1, d), F32))

        def weights(n, _):
            cols = pl.ds(pl.multiple_of(n * ROWS, ROWS), ROWS)
            under = pl.ds(pl.multiple_of(d + n * ROWS, ROWS), ROWS)
            down, up = mm(act[:, cols], c_ref[...], 0, 0), mm(a_ref[:, cols], gpre[...], 0, 0)
            into = unit if joined else units[0].at[0]
            if joined:
                down, up = down + other_ref[cols, :].astype(F32), up + other_ref[under, :].astype(F32)
            into[cols, :] = down.astype(BF)
            into[under, :] = up.astype(BF)
            return 0

        lax.fori_loop(0, d // ROWS, weights, 0)
        if joined:
            bit = t_ref[tiles]
            units[0][...] = unit[pl.ds(pl.multiple_of((1 - bit) * d, d), d), :]
            units[1][...] = unit[pl.ds(pl.multiple_of(bit * d, d), d), :]

    if not after:
        if several:
            @pl.when(j == lead + tiles - 1)
            def _():
                r_out[...] = r_acc[...].astype(BF)
                e_out[...] = e_acc[...].astype(BF)
        return

    @pl.when(j == tiles)
    def _():
        acc[...] = jnp.zeros_like(acc)
        sums_ref[...] = jnp.zeros_like(sums_ref)

    for s in range(steps):
        @pl.when(j == tiles + s)
        def _(s=s):
            for c in block(s):
                c.wait()
            h_ref, m_ref, *past = (t.at[s % 2] for t in held)
            for i in range(STEP // ROWS):
                rows = pl.ds(i * ROWS, ROWS)
                at = pl.ds(s * STEP + i * ROWS, ROWS)
                r, e = r_acc[at, :], e_acc[at, :]
                for n in range(0, after, 2):
                    r = r + past[n][rows, :].astype(F32)
                    e = e + past[n + 1][rows, :].astype(F32)
                h = h_ref[rows, :]
                o_ref[rows, :] = ((h + r + row_of(v_ref, DOWN_BIAS)) * row_of(v_ref, LIVE)).astype(BF)
                n, q = norm_stats(h)
                c = c_ref[at, :].astype(F32)
                gh = c + norm_back(e * row_of(v_ref, SECOND_GAIN), n, q)
                gh_ref[rows, :] = gh
                gb = gh.astype(BF)
                gm_ref[rows, :] = mm(gb, w_ref[...], 1, 1).astype(BF)
                acc[...] += mm(m_ref[rows, :], gb, 0, 0)
                add = lambda t: jnp.sum(t, axis=0, keepdims=True)
                sums_ref[0:1, :] += add(e * n)
                sums_ref[1:2, :] += add(e)
                sums_ref[2:3, :] += add(gb.astype(F32))
                sums_ref[3:4, :] += add(c)
            if s + 2 < steps:
                for c in block(s + 2):
                    c.start()
            if s == steps - 1:
                dw_ref[...] = acc[...].astype(BF)


def mlp_call(tile_bit, tiles, c, up, dn, vecs, a=None, before=None, other=None, after=None):
    L, d = c.shape
    steps = L // STEP
    lead = steps if before else 0
    tile = lambda j: jnp.clip(j - lead, 0, tiles - 1)
    mode = dict(pipeline_mode=pl.Buffered(1)) if tiles == 1 else {}
    first = pl.BlockSpec((STEP, d), lambda j, _: (jnp.minimum(j, steps - 1), 0))
    last = pl.BlockSpec((STEP, d), lambda j, _: (jnp.clip(j - 1, 0, steps - 1), 0))
    seq = shape((L, d), BF)
    in_specs, args, out_specs, out_shape = [], [], [], []
    if before:
        in_specs += [first, once((d, d)), first]
        args += list(before)
        out_specs += [first, first]
        out_shape += [shape((L, d), F32), seq]
    else:
        in_specs += [once((L, d))]
        args += [a]
    in_specs += [once((L, d)), pl.BlockSpec((d, d), lambda j, t: (0, t[tile(j)]), **mode),
                 pl.BlockSpec((d, d), lambda j, t: (t[tile(j)], 0), **mode), once(vecs.shape)]
    args += [c, up, dn, vecs]
    scratch = [pltpu.VMEM((L, d), BF), pltpu.VMEM((L, d), BF)]
    scratch += [pltpu.VMEM((L, d), F32)] * 2 if after or tiles > 1 else [pltpu.VMEM((16, 128), F32)] * 2
    if other is not None:
        in_specs += [once((2 * d, d))]
        args += [other]
        out_specs += [whole((d, d))] * 2
        out_shape += [shape((d, d), BF)] * 2
        scratch += [pltpu.VMEM((2 * d, d), BF)]
    else:
        out_specs += [pl.BlockSpec((1, 2 * d, d), lambda j, _: (tile(j), 0, 0))]
        out_shape += [shape((tiles, 2 * d, d), BF)]
    out_specs += [pl.BlockSpec((1, 1, d), lambda j, _: (tile(j), 0, 0))]
    out_shape += [shape((tiles, 1, d), F32)]
    if before:
        scratch += [pltpu.VMEM((L, d), BF)]
    if after:
        hidden, mixed, w, *past = after
        in_specs += [once((d, d))] + [pl.BlockSpec(memory_space=pl.ANY)] * (2 + len(past))
        args += [w, hidden, mixed] + past
        out_specs += [last, last, last, whole((d, d)), whole((8, d))]
        out_shape += [seq, shape((L, d), F32), seq, shape((d, d), BF), shape((8, d), F32)]
        scratch += [pltpu.VMEM((d, d), F32), pltpu.SemaphoreType.DMA((2, len(past) + 2)), pltpu.VMEM((2, STEP, d), F32)]
        scratch += [pltpu.VMEM((2, STEP, d), BF)] * (1 + len(past))
    else:
        out_specs += [whole((L, d))] * 2
        out_shape += [seq, seq]
    return pl.pallas_call(
        partial(mlp_kernel, before is not None, tiles, other is not None, len(after) - 3 if after else 0, steps),
        grid_spec=pltpu.PrefetchScalarGridSpec(
            num_scalar_prefetch=1,
            grid=(tiles + lead + (steps if after else 0),),
            in_specs=in_specs, out_specs=out_specs, scratch_shapes=scratch,
        ),
        out_shape=out_shape,
        compiler_params=params("mlp", L),
        cost_estimate=cost(12 * tiles),
        name="mlp",
    )(tile_bit, *args)


def attend_back_kernel(q_ref, k_ref, v_ref, p_ref, i_ref, g_ref, m_ref, dq_ref, dk_ref, dv_ref, dk_acc, dv_acc):
    L = q_ref.shape[0]
    low = lax.broadcasted_iota(jnp.int32, (ROWS, 128), 1) < 64
    nb = L // ROWS
    jobs = [(i, h) for i in reversed(range(nb)) for h in range(2)]
    strips = {}
    def strip(i):
        if i not in strips:
            rows = pl.ds(i * ROWS, ROWS)
            g32 = g_ref[rows, :].astype(F32) * i_ref[rows, :].astype(F32)
            g = g32.astype(BF)
            gm = g32 * m_ref[rows, :].astype(F32)
            strips[i] = (g, gm, q_ref[rows, :].T, g.T)
        return strips[i]

    def dprob(i, h):
        g, gm, _, _ = strip(i)
        mine = low if h == 0 else ~low
        gh = jnp.where(mine, g, jnp.zeros_like(g))
        delta = jnp.sum(jnp.where(mine, gm, 0.0), axis=-1, keepdims=True)
        return mm(gh, v_ref[pl.ds(0, (i + 1) * ROWS), :], 1, 1), delta

    dqs = {}
    ahead = [dprob(*jobs[0])]
    for t, (i, h) in enumerate(jobs):
        dp, delta = ahead.pop(0)
        if t + 1 < len(jobs):
            ahead.append(dprob(*jobs[t + 1]))
        n = (i + 1) * ROWS
        past = pl.ds(0, n)
        _, _, qt, gt = strip(i)
        p = p_ref[h, :, pl.ds(i * (i + 1) // 2 * ROWS, n)]
        side = pl.ds(64 * h, 64)
        dv = mm(gt[64 * h : 64 * h + 64], p, 1, 0)
        ds = (p.astype(F32) * (dp - delta)).astype(BF)
        dqs[h] = mm(ds, k_ref[past, :], 1, 0)
        dk = mm(qt[64 * h : 64 * h + 64], ds, 1, 0)
        if i == nb - 1:
            dk_acc[side, past] = dk
            dv_acc[side, past] = dv
        else:
            dk_acc[side, past] += dk
            dv_acc[side, past] += dv
        if h == 1:
            dq_ref[pl.ds(i * ROWS, ROWS), :] = (jnp.where(low, dqs[0], dqs[1]) * 0.125).astype(BF)
    dk_ref[...] = dk_acc[...].T.astype(BF)
    dv_ref[...] = dv_acc[...].T.astype(BF)


def attend_back_call(qkv, p, inv, gm, mixed, lo, count, held=()):
    L, d3 = qkv.shape
    n = d3 // 3 // 128
    col = lambda k: pl.BlockSpec((L, 128), lambda j: (0, k * n + lo + j))
    s = shape((L, d3 // 3), BF)
    kernel = attend_back_kernel
    if held:
        kernel = lambda *refs: attend_back_kernel(*refs[:7], *refs[10:])
    return pl.pallas_call(
        kernel,
        grid=(count,),
        in_specs=[col(0), col(1), col(2), pl.BlockSpec((2, ROWS, tri_cols(L)), lambda j: (lo + j, 0, 0)), col(0), col(0), col(0)]
        + [pl.BlockSpec(memory_space=pl.ANY)] * len(held),
        out_specs=[col(0)] * 3,
        out_shape=[s] * 3,
        input_output_aliases={7 + i: i for i in range(len(held))},
        scratch_shapes=[pltpu.VMEM((128, L), F32), pltpu.VMEM((128, L), F32)],
        compiler_params=params("attend_back", L),
        cost_estimate=cost(3 * count),
        name="attend_back",
    )(qkv, qkv, qkv, p, inv, gm, mixed, *held)


def joint_sent_kernel(core_ref, a_ref, q_ref, k_ref, v_ref, w_ref, out_ref, sums_ref):
    d = a_ref.shape[1]
    sums_ref[...] = jnp.zeros_like(sums_ref)
    sums_ref[0:1, :] = jnp.sum(q_ref[...].astype(F32), axis=0, keepdims=True)
    sums_ref[1:2, :] = jnp.sum(v_ref[...].astype(F32), axis=0, keepdims=True)

    @pl.when(core_ref[0] == 1)
    def _():
        out_ref[0:d, :] = mm(a_ref[...], q_ref[...], 0, 0).astype(BF)
        out_ref[d : 2 * d, :] = mm(a_ref[...], k_ref[...], 0, 0).astype(BF)

    @pl.when(core_ref[0] == 0)
    def _():
        out_ref[0:d, :] = mm(a_ref[...], v_ref[...], 0, 0).astype(BF)
        out_ref[d : 2 * d, :] = w_ref[...]


def joint_sent_call(core, a, dq, dk, dv, dw):
    L, d = a.shape
    return pl.pallas_call(
        joint_sent_kernel,
        grid_spec=pltpu.PrefetchScalarGridSpec(
            num_scalar_prefetch=1, grid=(1,), in_specs=[once((L, d))] * 4 + [once((d, d))],
            out_specs=[whole((2 * d, d)), whole((8, d))]),
        out_shape=[shape((2 * d, d), BF), shape((8, d), F32)],
        compiler_params=params("joint_sent", L),
        cost_estimate=cost(5),
        name="joint_sent",
    )(core, a, dq, dk, dv, dw)


def joint_kept_kernel(core_ref, a_ref, q_ref, k_ref, v_ref, w_ref, other_ref, sent_ref, kept_ref, unit):
    d = a_ref.shape[1]
    add = lambda t, n: (t + other_ref[n * d : (n + 1) * d, :].astype(F32)).astype(BF)

    @pl.when(core_ref[0] == 0)
    def _():
        unit[0:d, :] = add(mm(a_ref[...], q_ref[...], 0, 0), 0)
        unit[d : 2 * d, :] = add(mm(a_ref[...], k_ref[...], 0, 0), 1)

    @pl.when(core_ref[0] == 1)
    def _():
        unit[0:d, :] = add(mm(a_ref[...], v_ref[...], 0, 0), 0)
        unit[d : 2 * d, :] = add(w_ref[...].astype(F32), 1)

    bit = core_ref[1]
    sent_ref[...] = unit[pl.ds(pl.multiple_of((1 - bit) * d, d), d), :]
    kept_ref[...] = unit[pl.ds(pl.multiple_of(bit * d, d), d), :]


def joint_kept_call(core_bit, a, dq, dk, dv, dw, other):
    L, d = a.shape
    return pl.pallas_call(
        joint_kept_kernel,
        grid_spec=pltpu.PrefetchScalarGridSpec(
            num_scalar_prefetch=1, grid=(1,), in_specs=[once((L, d))] * 4 + [once((d, d)), once((2 * d, d))],
            out_specs=[whole((d, d)), whole((d, d))], scratch_shapes=[pltpu.VMEM((2 * d, d), BF)]),
        out_shape=[shape((d, d), BF)] * 2,
        compiler_params=params("joint_kept", L),
        cost_estimate=cost(5),
        name="joint_kept",
    )(core_bit, a, dq, dk, dv, dw, other)


def tokens_kernel(q_ref, k_ref, v_ref, w_ref, x_ref, gh_ref, vec_ref, o_ref, sums_ref):
    i = pl.program_id(0)
    d = x_ref.shape[1]

    @pl.when(i == 0)
    def _():
        sums_ref[...] = jnp.zeros_like(sums_ref)

    def back(i):
        rows = pl.ds(i * ROWS, ROWS)
        return (mm(q_ref[rows, :], w_ref[:, 0:d], 1, 1) + mm(k_ref[rows, :], w_ref[:, d : 2 * d], 1, 1)
                + mm(v_ref[rows, :], w_ref[:, 2 * d :], 1, 1))

    ahead = back(0)
    for j in range(STEP // ROWS):
        e, rows = ahead, pl.ds(j * ROWS, ROWS)
        if (j + 1) * ROWS < STEP:
            ahead = back(j + 1)
        n, r = norm_stats(x_ref[rows, :].astype(F32))
        o_ref[rows, :] = (gh_ref[rows, :] + norm_back(e * row_of(vec_ref, FIRST_GAIN), n, r)).astype(BF)
        sums_ref[0:1, :] += jnp.sum(e * n, axis=0, keepdims=True)
        sums_ref[1:2, :] += jnp.sum(e, axis=0, keepdims=True)


def tokens_call(dq, dk, dv, w, x, gh, vecs):
    L, d = x.shape
    blk = pl.BlockSpec((STEP, d), lambda i: (i, 0))
    return pl.pallas_call(
        tokens_kernel,
        grid=(L // STEP,),
        in_specs=[blk, blk, blk, once((d, 3 * d)), blk, blk, once(vecs.shape)],
        out_specs=[blk, whole((8, d))],
        out_shape=[shape((L, d), BF), shape((8, d), F32)],
        compiler_params=params("tokens_back", L),
        cost_estimate=cost(9),
        name="tokens_back",
    )(dq, dk, dv, w, x, gh, vecs)


def place_kernel(core_ref, own_ref, other_ref, *rest):
    down_ref, up_ref = rest[-2:]
    d = down_ref.shape[1]
    for n, ref in enumerate((own_ref, other_ref)):
        @pl.when(pl.program_id(0) == n)
        def _(ref=ref):
            down_ref[...] = ref[0:d, :].astype(F32)
            up_ref[...] = ref[d : 2 * d, :].astype(F32)


def place_call(core, own, other, tile, ff, held=()):
    d = own.shape[1]
    at = lambda n, s: tile + jnp.where(n == 0, s[0], 1 - s[0])
    return pl.pallas_call(
        place_kernel,
        grid_spec=pltpu.PrefetchScalarGridSpec(
            num_scalar_prefetch=1,
            grid=(2,),
            in_specs=[whole((2 * d, d))] * 2 + [pl.BlockSpec(memory_space=pl.ANY)] * len(held),
            out_specs=[pl.BlockSpec((d, d), lambda n, s: (at(n, s), 0)), pl.BlockSpec((d, d), lambda n, s: (0, at(n, s)))],
        ),
        out_shape=[shape((ff, d), F32), shape((d, ff), F32)],
        input_output_aliases={3 + i: i for i in range(len(held))},
        compiler_params=params("place"),
        cost_estimate=cost(5),
        name="place",
    )(core, own, other, *held)


def place_joint_kernel(core_ref, own_ref, other_ref, joint_ref, out_ref, small_ref):
    d = out_ref.shape[0]

    for core, (qk_ref, vw_ref) in enumerate(((own_ref, other_ref), (other_ref, own_ref))):
        @pl.when(core_ref[0] == core)
        def _(qk_ref=qk_ref, vw_ref=vw_ref):
            joint_ref[:, 0:d] = qk_ref[0:d, :].astype(F32)
            joint_ref[:, d : 2 * d] = qk_ref[d : 2 * d, :].astype(F32)
            joint_ref[:, 2 * d : 3 * d] = vw_ref[0:d, :].astype(F32)
            out_ref[...] = vw_ref[d : 2 * d, :].astype(F32)

    small_ref[...] = own_ref[2 * d :, :].astype(F32) + other_ref[2 * d :, :].astype(F32)


def place_joint(core, own, other):
    rows, d = own.shape
    v = pl.BlockSpec(memory_space=pltpu.VMEM)
    return pl.pallas_call(
        place_joint_kernel,
        in_specs=[pl.BlockSpec(memory_space=pltpu.SMEM), v, v],
        out_specs=[v] * 3,
        out_shape=[shape((d, 3 * d), F32), shape((d, d), F32), shape((rows - 2 * d, d), F32)],
        compiler_params=params("place_joint"),
        cost_estimate=cost(5),
        name="place_joint",
    )(core, own, other)


def halve_kernel(up_ref, a_ref, b_ref, c_ref, d_ref, sent_ref, kept_ref):
    sent_ref[...] = a_ref[...] + b_ref[...]
    kept_ref[...] = c_ref[...] + d_ref[...]


def halve_call(up, kept, other):
    rows, d = kept.shape[0] // 2, kept.shape[1]
    block = rows if rows <= 384 else rows // 2
    n = rows // block
    go = pl.BlockSpec((block, d), lambda i, up: ((1 - up[0]) * n + i, 0))
    stay = pl.BlockSpec((block, d), lambda i, up: (up[0] * n + i, 0))
    out = pl.BlockSpec((block, d), lambda i, up: (i, 0))
    s = shape((rows, d), BF)
    return pl.pallas_call(
        halve_kernel,
        grid_spec=pltpu.PrefetchScalarGridSpec(
            num_scalar_prefetch=1, grid=(n,), in_specs=[go, go, stay, stay], out_specs=[out, out]),
        out_shape=[s, s],
        compiler_params=params("halve"),
        cost_estimate=cost(2),
        name="halve",
    )(up, kept, other, kept, other)


def double_kernel(rows, up_ref, a_ref, b_ref, o_ref):
    up = up_ref[0]
    o_ref[pl.ds(pl.multiple_of(up * rows, 16), rows), :] = a_ref[0:rows, :]
    o_ref[pl.ds(pl.multiple_of((1 - up) * rows, 16), rows), :] = b_ref[0:rows, :]
    if a_ref.shape[0] > rows:
        tail = a_ref[rows:, :].astype(F32) + b_ref[rows:, :].astype(F32)
        o_ref[2 * rows :, :] = tail.astype(BF)


def double_call(up, kept, other, tail=0):
    rows, d = kept.shape[0] - tail, kept.shape[1]
    v = pl.BlockSpec(memory_space=pltpu.VMEM)
    return pl.pallas_call(
        partial(double_kernel, rows),
        in_specs=[pl.BlockSpec(memory_space=pltpu.SMEM), v, v],
        out_specs=v,
        out_shape=shape((2 * rows + tail, d), BF),
        compiler_params=params("double"),
        cost_estimate=cost(2),
        name="double",
    )(up, kept, other)


def arrange_kernel(places, at_ref, *refs):
    out_ref = refs[-1]
    for k, ref in enumerate(refs[:-1]):
        if places < len(refs) - 1:
            @pl.when(at_ref[k] < places)
            def _(k=k, ref=ref):
                out_ref[at_ref[k]] = ref[...]
        else:
            out_ref[at_ref[k]] = ref[...]


def arrange_call(at, parts, places):
    block, d = parts[0].shape
    v = pl.BlockSpec(memory_space=pltpu.VMEM)
    return pl.pallas_call(
        partial(arrange_kernel, places),
        in_specs=[pl.BlockSpec(memory_space=pltpu.SMEM)] + [v] * len(parts),
        out_specs=v,
        out_shape=shape((places, block, d), BF),
        compiler_params=params("arrange"),
        cost_estimate=cost(2),
        name="arrange",
    )(at, *parts)


def small_kernel(core_ref, first_ref, joint_ref, second_ref, b0, b1, b2, b3, o_ref):
    o_ref[...] = jnp.zeros_like(o_ref)
    o_ref[0:2, :] = first_ref[0:2, :].astype(BF)
    o_ref[2:4, :] = joint_ref[0:2, :].astype(BF)
    o_ref[4:8, :] = second_ref[0:4, :].astype(BF)
    for n, (u, v) in enumerate(((b0, b1), (b1, b0), (b2, b3), (b3, b2))):
        o_ref[8 + n : 9 + n, :] = jnp.where(core_ref[0] == 0, u[0], v[0]).astype(BF)


def small_call(core, first, joint, second, up_bias):
    v = pl.BlockSpec(memory_space=pltpu.VMEM)
    return pl.pallas_call(
        small_kernel,
        in_specs=[pl.BlockSpec(memory_space=pltpu.SMEM)] + [v] * 7,
        out_specs=v,
        out_shape=shape((16, first.shape[1]), BF),
        compiler_params=params("small"),
        cost_estimate=cost(1),
        name="small",
    )(core, first, joint, second, *up_bias)


def bits_of(count):
    assert count & (count - 1) == 0
    return count.bit_length() - 1


class Moves:
    def __init__(self, n_dp, n_blk, slots):
        assert slots <= n_blk
        self.n_dp, self.n_blk, self.slots = n_dp, n_blk, slots
        self.dp, self.blk = lax.axis_index("dp"), lax.axis_index("blk")
        self.odd = self.dp % 2

    def slot(self, blk):
        return jnp.where(self.odd == 1, self.n_blk - 1 - blk, blk)

    def perm(self, step, back):
        pairs = []
        for g in range(self.n_dp):
            for b in range(self.n_blk):
                d = (b + step) % self.n_blk
                s = self.n_blk - 1 - d if g % 2 else d
                if s < self.slots:
                    pair = (g * self.n_blk + b, g * self.n_blk + d)
                    pairs.append(pair[::-1] if back else pair)
        return pairs

    def send_out(self, x, beside=None):
        parts = []
        for step in range(self.n_blk):
            if beside is not None and step == self.n_blk - 1:
                x = lax.optimization_barrier((x, beside))[0]
            s = jnp.minimum(self.slot((self.blk + step) % self.n_blk), self.slots - 1)
            part = lax.dynamic_index_in_dim(x, s, 0, keepdims=False)
            parts.append(lax.ppermute(part, ("dp", "blk"), self.perm(step, False)) if step else part)
        return parts

    def join(self, parts):
        at = (self.blk - jnp.arange(self.n_blk, dtype=jnp.int32)) % self.n_blk
        return arrange_call(at, parts, self.n_blk).reshape(-1, parts[0].shape[1])

    def send_back(self, y):
        y = y.reshape(self.n_blk, -1, y.shape[-1])
        parts = []
        for step in range(self.n_blk):
            part = lax.dynamic_index_in_dim(y, (self.blk - step) % self.n_blk, 0, keepdims=False)
            parts.append(lax.ppermute(part, ("dp", "blk"), self.perm(step, True)) if step else part)
        return parts

    def exchange_back(self, y):
        return lax.all_to_all(y.reshape(self.n_blk, -1, y.shape[-1]), "blk", 0, 0)

    def unexchange(self, y):
        return jnp.where(self.odd == 1, y[::-1][: self.slots], y[: self.slots])

    def unjoin(self, parts):
        at = self.slot((self.blk + jnp.arange(self.n_blk, dtype=jnp.int32)) % self.n_blk)
        return arrange_call(at, parts, self.slots)


class Order:
    def __init__(self):
        self.last = None

    def take(self, *arrays):
        if self.last is not None:
            arrays = lax.optimization_barrier(arrays + (self.last,))[:-1]
        return arrays if len(arrays) > 1 else arrays[0]

    def mark(self, array):
        self.last = array


class Sum:
    def __init__(self, moves):
        self.n = moves.n_dp * moves.n_blk
        self.me = moves.dp * moves.n_blk + moves.blk
        low, high = bits_of(moves.n_blk), bits_of(moves.n_dp)
        plane = [low + 1 + i for i in range(high - 1)]
        self.core = low
        self.orders = [plane + list(range(low)), plane[::-1] + list(range(low))]
        self.stages = len(self.orders[0])
        self.tail = None

    def order(self, i, stage):
        return self.core if stage < 0 else self.orders[(i >> self.core) & 1][stage]

    def swap(self, x, stage):
        return lax.ppermute(x, ("dp", "blk"), [(i, i ^ (1 << self.order(i, stage))) for i in range(self.n)])

    def up(self, stage, me=None):
        me = self.me if me is None else me
        odd = (me >> self.core) & 1
        return jnp.where(odd == 0, (me >> self.order(0, stage)) & 1, (me >> self.order(1 << self.core, stage)) & 1)

    def cross(self, sent):
        self.moving = self.swap(sent, -1)

    def crossed(self, order):
        return order.take(self.moving)

    def begin(self, sent, kept):
        self.sent, self.kept, self.stage, self.gathering = sent, kept, 0, False
        self.send()

    def send(self):
        if not self.gathering:
            self.moving = self.swap(self.sent, self.stage)
        else:
            self.moving = self.swap(self.kept, self.stage)

    def step(self, order):
        other, self.kept = order.take(self.moving, self.kept)
        if not self.gathering:
            self.stage += 1
            if self.stage == self.stages:
                self.kept = self.kept + other
                if self.tail is not None:
                    self.kept = jnp.concatenate([self.kept, self.tail])
                self.gathering = True
                self.stage -= 1
            else:
                half = self.kept.shape[0] // 2
                up = self.up(self.stage)
                if half % 16 == 0:
                    self.sent, self.kept = halve_call(up.reshape(1), self.kept, other)
                else:
                    part = lambda x, at: lax.dynamic_slice_in_dim(x, at * half, half, 0)
                    self.sent = part(self.kept, 1 - up) + part(other, 1 - up)
                    self.kept = part(self.kept, up) + part(other, up)
        else:
            tail = 0 if self.tail is None else self.tail.shape[0]
            self.kept = double_call(self.up(self.stage).reshape(1), self.kept, other, tail)
            self.stage -= 1
        order.mark(self.kept)
        self.send()

    def finish(self, order):
        theirs = order.take(self.moving)
        return ((self.me >> self.core) & 1).reshape(1), self.kept, theirs


PLAN = (
    "m1", "m2", "m3", "m4", "o", "1", "ab1", "1", "x", "ab2", "2", "1", "O", "js", "1", "tok", "2", "jk", "1", "2",
    "3", "3", "2", "1", "3", "2", "3", "1", "3", "2", "1", "g", "3", "2", "a", "3", "1", "b", "3", "c", "2", "3",
    "G", "2",
)


def on_device(n_dp, n_blk, tokens, live_count, first_gain, first_shift, joint_weight, query_bias, value_bias,
              out_weight, out_bias, second_gain, second_shift, up_weight, up_bias, down_weight, down_bias, cotangent):
    slots, block, d = tokens.shape
    ff = up_weight.shape[1]
    assert ff == 4 * d
    pairs = d // 128
    moves = Moves(n_dp, n_blk, slots)
    order = Order()
    mine = moves.slot(moves.blk)
    live = ((mine < slots) & (mine < live_count[0])).astype(F32)
    core = moves.odd.reshape(1)
    vecs = vectors_call([first_gain, first_shift, query_bias, value_bias, out_bias, second_gain, second_shift,
                         down_bias, up_bias], live.reshape(1))
    live_slots = jnp.arange(slots, dtype=jnp.int32) < live_count[0]

    x_parts = moves.send_out(tokens, vecs)
    x = moves.join(x_parts)
    attn_in, qkv = joint_call(x, joint_weight, vecs)
    c = jnp.where(live_slots[:, None, None], lax.optimization_barrier((cotangent, x))[0], jnp.zeros_like(cotangent))
    c_parts = moves.send_out(c)
    c_parts[0] = jnp.where(mine < slots, c_parts[0], jnp.zeros_like(c_parts[0]))
    mixed, p, inv = attend_call(qkv)
    order.mark(mixed)
    c = moves.join(list(order.take(*c_parts)))

    sums = {name: Sum(moves) for name in "123"}
    got = {}
    bit = sums["2"].up(0).reshape(1)
    tile = lambda which, tiles, **more: mlp_call(which, tiles, c, up_weight, down_weight, vecs, **more)

    def m1():
        got["hidden"], got["a"], sent, got["gb1"], *past = tile(1 - core, 1, before=(mixed, out_weight, x))
        sums["1"].cross(sent[0])
        got["past"] = tuple(past)
        return past[0]

    def m2():
        sent, got["gb3"], *past = tile(3 - core, 1, a=order.take(got["a"]))
        sums["2"].cross(sent[0])
        got["past"] += tuple(past)
        return past[0]

    def m3():
        other = sums["1"].crossed(order)
        sent, kept, got["gb0"], *past = tile(jnp.concatenate([core, bit]), 1, a=order.take(got["a"]), other=other)
        sums["1"].begin(sent, kept)
        got["past"] += tuple(past)
        return past[0]

    def m4():
        other = sums["2"].crossed(order)
        after = (got["hidden"], mixed, out_weight) + got["past"]
        sent, kept, gb, out, gh, gm, dwo, s = tile(jnp.concatenate([2 + core, bit]), 1, a=order.take(got["a"]), other=other,
                                                   after=after)
        sums["2"].begin(sent, kept)
        got.update(gb2=gb, out=out, gh=gh, gm=gm, dwo=dwo, sums2=s)
        return gh

    def ab1():
        count = pairs // 2 if "ab2" in PLAN else pairs
        got["back"] = attend_back_call(qkv, p, inv, order.take(got["gm"]), mixed, 0, count)
        return got["back"][0]

    def ab2():
        got["back"] = attend_back_call(qkv, p, inv, order.take(got["gm"]), mixed, pairs // 2, pairs - pairs // 2,
                                       got["back"])
        return got["back"][0]

    def js():
        sent, got["sums1"] = joint_sent_call(core, order.take(attn_in), *got["back"], got["dwo"])
        sums["3"].cross(sent)
        return sent

    def jk():
        other = sums["3"].crossed(order)
        sent, kept = joint_kept_call(jnp.concatenate([core, bit]), order.take(attn_in), *got["back"], got["dwo"], other)
        sums["3"].begin(sent, kept)
        return kept

    def tok():
        dq, dk, dv = got["back"]
        got["gx"], sums0 = tokens_call(order.take(dq), dk, dv, joint_weight, x, got["gh"], vecs)
        order.mark(got["gx"])
        sums["3"].tail = small_call(core, order.take(sums0), got["sums1"], got["sums2"], [got["gb%d" % n] for n in range(4)])
        return sums["3"].tail

    def send(name):
        if name == "out" and not PLAN.count("x"):
            got["out_moved"] = moves.exchange_back(order.take(got["out"]))
        else:
            got[name + "_parts"] = moves.send_back(order.take(got[name]))

    def part(name, k):
        parts = got[name + "_parts"]
        if k < len(parts):
            parts[k] = order.take(parts[k])
            order.mark(parts[k])

    def join(name):
        if name == "out" and "out_moved" in got:
            got["out"] = moves.unexchange(order.take(got["out_moved"]))
            return got["out"]
        got[name] = moves.unjoin(list(order.take(*got[name + "_parts"])))
        return got[name]

    def step(name):
        total = sums.get(name)
        if total is None:
            return
        if not total.gathering or total.stage >= 0:
            total.step(order)
        else:
            sums[name] = None
            if name == "3":
                got["joint"] = place_joint(*total.finish(order))
                order.mark(got["joint"][1])
            else:
                got["wide"] = place_call(*total.finish(order), 2 * int(name) - 2, ff, got.get("wide", ()))
                order.mark(got["wide"][0])

    kernels = dict(m1=m1, m2=m2, m3=m3, m4=m4, ab1=ab1, ab2=ab2, js=js, jk=jk, tok=tok)
    for word in PLAN + ("2", "1", "3") * 12:
        if word in kernels:
            order.mark(kernels[word]())
        elif word in "abc":
            part("gx", 1 + "abc".index(word))
        elif word in "xyz":
            part("out", 1 + "xyz".index(word))
        elif word in "og":
            send({"o": "out", "g": "gx"}[word])
        elif word in "OG":
            order.mark(join({"O": "out", "G": "gx"}[word]))
        else:
            step(word)
    small = got["joint"][2]
    return (got["out"], got["gx"], small[0], small[1], got["joint"][0], small[2], small[3], got["joint"][1], small[6],
            small[4], small[5], got["wide"][1], small[8:12].reshape(-1), got["wide"][0], small[7])


def solution(mesh):
    seq = P("dp", "blk", None)
    n_dp, n_blk = mesh.shape["dp"], mesh.shape["blk"]
    return jax.shard_map(
        partial(on_device, n_dp, n_blk), mesh=mesh,
        in_specs=(seq, P("dp")) + (P(),) * 13 + (seq,),
        out_specs=(seq, seq) + (P(),) * 13,
        check_vma=False,
    )
```

```python
import math
from functools import partial
import jax
import jax.numpy as jnp
from jax import lax
from jax.experimental import pallas as pl
from jax.experimental.pallas import tpu as pltpu
from jax.sharding import PartitionSpec as P

BF = jnp.bfloat16
F32 = jnp.float32
HEADS = 12
EPS = 1e-5
ROWS = 256
STEP = 512
COST = 1000
MIB = dict(arrange=8, double=16, halve=16, joint=30, joint_kept=30, joint_sent=30, mlp=60, place=30, place_joint=30,
           small=8, tokens_back=24, vectors=8)


def params(name, length=1024):
    return pltpu.CompilerParams(vmem_limit_bytes=min(60, MIB.get(name, 60) * max(length, 1024) // 1024) * 2**20)


def cost(us):
    return pl.CostEstimate(flops=int(us * COST), bytes_accessed=1000, transcendentals=0)


def mm(a, b, ca, cb):
    return lax.dot_general(a, b, (((ca,), (cb,)), ((), ())), preferred_element_type=F32)


def shape(s, d):
    return pltpu.HBM(s, d)


def whole(s):
    n = len(s)
    return pl.BlockSpec(s, lambda *_: (0,) * n)


def norm_stats(t):
    c = t - jnp.mean(t, axis=-1, keepdims=True)
    r = lax.rsqrt(jnp.mean(c * c, axis=-1, keepdims=True) + EPS)
    return c * r, r


(FIRST_GAIN, FIRST_SHIFT, QUERY_BIAS, ZERO, VALUE_BIAS, OUT_BIAS, SECOND_GAIN, SECOND_SHIFT, DOWN_BIAS, LIVE,
 UP_BIAS) = range(11)


def row_of(ref, n):
    return ref[n : n + 1, :]


def once(s):
    n = len(s)
    return pl.BlockSpec(s, lambda *_: (0,) * n, pipeline_mode=pl.Buffered(1))


def vectors_kernel(live_ref, *refs):
    out_ref = refs[-1]
    d = out_ref.shape[1]
    out_ref[...] = jnp.zeros_like(out_ref)
    at = (FIRST_GAIN, FIRST_SHIFT, QUERY_BIAS, VALUE_BIAS, OUT_BIAS, SECOND_GAIN, SECOND_SHIFT, DOWN_BIAS)
    for n, ref in zip(at, refs):
        out_ref[n : n + 1, :] = ref[...].reshape(1, d)
    for n in range(refs[-2].shape[0] // d):
        out_ref[UP_BIAS + n : UP_BIAS + n + 1, :] = refs[-2][pl.ds(n * d, d)].reshape(1, d)
    out_ref[LIVE : LIVE + 1, :] = jnp.full((1, d), live_ref[0], F32)


def vectors_call(vectors, live):
    d, ff = vectors[0].shape[0], vectors[-1].shape[0]
    v = pl.BlockSpec(memory_space=pltpu.VMEM)
    return pl.pallas_call(
        vectors_kernel,
        in_specs=[pl.BlockSpec(memory_space=pltpu.SMEM)] + [v] * len(vectors),
        out_shape=shape(((UP_BIAS + ff // d + 7) // 8 * 8, d), F32),
        compiler_params=params("vectors"),
        cost_estimate=cost(1),
        name="vectors",
    )(live, *vectors)


def joint_kernel(x_ref, w_ref, v_ref, a_ref, q_ref):
    d = x_ref.shape[1]

    def norm(i):
        n, _ = norm_stats(x_ref[pl.ds(i * ROWS, ROWS), :].astype(F32))
        return (n * row_of(v_ref, FIRST_GAIN) + row_of(v_ref, FIRST_SHIFT)).astype(BF)

    ahead = norm(0)
    for i in range(STEP // ROWS):
        a, rows = ahead, pl.ds(i * ROWS, ROWS)
        a_ref[rows, :] = a
        for j, bias in enumerate((QUERY_BIAS, ZERO, VALUE_BIAS)):
            if j == 1 and (i + 1) * ROWS < STEP:
                ahead = norm(i + 1)
            cols = pl.ds(j * d, d)
            t = (mm(a, w_ref[:, cols], 1, 0) + row_of(v_ref, bias)).astype(BF)
            q_ref[rows, cols] = t * jnp.asarray(0.125, BF) if j == 0 else t


def joint_call(x, w, vecs):
    L, d = x.shape
    return pl.pallas_call(
        joint_kernel,
        grid=(L // STEP,),
        in_specs=[pl.BlockSpec((STEP, d), lambda i: (i, 0)), once((d, 3 * d)), once(vecs.shape)],
        out_specs=[pl.BlockSpec((STEP, d), lambda i: (i, 0)), pl.BlockSpec((STEP, 3 * d), lambda i: (i, 0))],
        out_shape=[shape((L, d), BF), shape((L, 3 * d), BF)],
        compiler_params=params("joint", L),
        cost_estimate=cost(7),
        name="joint",
    )(x, w, vecs)


def tri_cols(L):
    n = L // ROWS
    return n * (n + 1) // 2 * ROWS


def attend_kernel(q_ref, k_ref, v_ref, o_ref, p_ref, i_ref):
    L = q_ref.shape[0]
    low = lax.broadcasted_iota(jnp.int32, (ROWS, 128), 1) < 64
    low_all = lax.broadcasted_iota(jnp.int32, (L, 128), 1) < 64
    tri = lax.broadcasted_iota(jnp.int32, (ROWS, ROWS), 1) <= lax.broadcasted_iota(jnp.int32, (ROWS, ROWS), 0)
    v = v_ref[...]
    one = jnp.ones_like(v)
    vs = [jnp.where(low_all, v, one), jnp.where(low_all, one, v)]
    jobs = [(i, h) for i in range(L // ROWS) for h in range(2)]

    def score(i, h):
        q = q_ref[pl.ds(i * ROWS, ROWS), :]
        qh = jnp.where(low if h == 0 else ~low, q, jnp.zeros_like(q))
        return mm(qh, k_ref[pl.ds(0, (i + 1) * ROWS), :], 1, 1)

    outs = [None, None]
    ahead = [score(*job) for job in jobs[:2]]
    for t, (i, h) in enumerate(jobs):
        s = ahead.pop(0)
        if t + 2 < len(jobs):
            ahead.append(score(*jobs[t + 2]))
        past = (i + 1) * ROWS
        diag = jnp.where(tri, s[:, i * ROWS :], -1e30)
        m = jnp.max(diag, axis=-1, keepdims=True)
        if i:
            m = jnp.maximum(m, jnp.max(s[:, : i * ROWS], axis=-1, keepdims=True))
            p = jnp.concatenate([jnp.exp(s[:, : i * ROWS] - m).astype(BF), jnp.exp(diag - m).astype(BF)], axis=1)
        else:
            p = jnp.exp(diag - m).astype(BF)
        p_ref[h, :, pl.ds(i * (i + 1) // 2 * ROWS, past)] = p
        outs[h] = mm(p, vs[h][:past], 1, 0)
        if h == 1:
            rows = pl.ds(i * ROWS, ROWS)
            inv = 1.0 / jnp.where(low, pltpu.roll(outs[0], 64, 1), pltpu.roll(outs[1], 64, 1))
            o_ref[rows, :] = (jnp.where(low, outs[0], outs[1]) * inv).astype(BF)
            i_ref[rows, :] = inv.astype(BF)


def attend_call(qkv):
    L, d3 = qkv.shape
    n = d3 // 3 // 128
    col = lambda k: pl.BlockSpec((L, 128), lambda j: (0, k * n + j))
    return pl.pallas_call(
        attend_kernel,
        grid=(n,),
        in_specs=[col(0), col(1), col(2)],
        out_specs=[col(0), pl.BlockSpec((2, ROWS, tri_cols(L)), lambda j: (j, 0, 0)), col(0)],
        out_shape=[shape((L, d3 // 3), BF), shape((2 * n, ROWS, tri_cols(L)), BF), shape((L, d3 // 3), BF)],
        compiler_params=params("attend", L),
        cost_estimate=cost(15),
        name="attend",
    )(qkv, qkv, qkv)


GC = math.sqrt(2.0 / math.pi)


def gelu_both(u):
    u2 = u * u
    t = jnp.tanh(u * (GC + GC * 0.044715 * u2))
    half = 0.5 + 0.5 * t
    return u * half, half + u * (0.5 - 0.5 * t * t) * (GC + 3 * GC * 0.044715 * u2)


def norm_back(e, n, r):
    return r * (e - jnp.mean(e, axis=-1, keepdims=True) - n * jnp.mean(e * n, axis=-1, keepdims=True))


def mlp_kernel(before, tiles, joined, after, steps, t_ref, *refs):
    refs = list(refs)
    take = lambda n: [refs.pop(0) for _ in range(n)]
    if before:
        m_ref, w_ref, x_ref = take(3)
    else:
        a_ref, = take(1)
    c_ref, up_ref, dn_ref, v_ref = take(4)
    if joined:
        other_ref, = take(1)
    if after:
        w_ref, *late = take(3 + after)
    if before:
        h_out, a_out = take(2)
    units = take(2 if joined else 1)
    gb_ref, = take(1)
    several = tiles > 1 or after
    if after:
        o_ref, gh_ref, gm_ref, dw_ref, sums_ref = take(5)
    else:
        r_out, e_out = take(2)
    act, gpre, r_acc, e_acc = take(4)
    if joined:
        unit, = take(1)
    if before:
        a_ref, = take(1)
    if after:
        acc, sems, *held = take(4 + after)
    j = pl.program_id(0)
    L, d = c_ref.shape
    lead = steps if before else 0

    def block(s):
        rows = pl.ds(s * STEP, STEP)
        return [pltpu.make_async_copy(src.at[rows, :], dst.at[s % 2], sems.at[s % 2, n])
                for n, (src, dst) in enumerate(zip(late, held))]

    if after:
        @pl.when(j == 0)
        def _():
            for s in range(2):
                for c in block(s):
                    c.start()

    if before:
        @pl.when(j < lead)
        def _():
            part = lambda i: mm(m_ref[pl.ds(i * ROWS, ROWS), :], w_ref[...], 1, 0)
            ahead = part(0)
            for i in range(STEP // ROWS):
                got, rows = ahead, pl.ds(i * ROWS, ROWS)
                if (i + 1) * ROWS < STEP:
                    ahead = part(i + 1)
                h = x_ref[rows, :].astype(F32) + got + row_of(v_ref, OUT_BIAS)
                h_out[rows, :] = h
                n, _ = norm_stats(h)
                a = (n * row_of(v_ref, SECOND_GAIN) + row_of(v_ref, SECOND_SHIFT)).astype(BF)
                a_out[rows, :] = a
                a_ref[pl.ds(pl.multiple_of(j * STEP + i * ROWS, ROWS), ROWS), :] = a

    @pl.when((j >= lead) & (j < lead + tiles))
    def _():
        bias = v_ref[pl.ds(UP_BIAS + t_ref[j - lead], 1), :]

        def pair(rows):
            return (mm(a_ref[rows, :], up_ref[...], 1, 0) + bias,
                    mm(c_ref[rows, :], dn_ref[...], 1, 1).astype(BF).astype(F32))

        def pass_rows(i, gb):
            rows = [pl.ds(pl.multiple_of(i * STEP + n * ROWS, ROWS), ROWS) for n in range(STEP // ROWS)]
            ahead = pair(rows[0])
            for n, here in enumerate(rows):
                u, ga = ahead
                if n + 1 < len(rows):
                    ahead = pair(rows[n + 1])
                g, dg = gelu_both(u)
                g = g.astype(BF)
                gp = (ga * dg).astype(BF)
                act[here, :] = g
                gpre[here, :] = gp
                gb = gb + jnp.sum(gp.astype(F32), axis=0, keepdims=True)
                r = mm(g, dn_ref[...], 1, 0)
                e = mm(gp, up_ref[...], 1, 1)
                if tiles > 1:
                    r = r + jnp.where(j > lead, r_acc[here, :], 0.0)
                    e = e + jnp.where(j > lead, e_acc[here, :], 0.0)
                if several:
                    r_acc[here, :] = r
                    e_acc[here, :] = e
                else:
                    r_out[here, :] = r.astype(BF)
                    e_out[here, :] = e.astype(BF)
            return gb

        gb_ref[0] = lax.fori_loop(0, L // STEP, pass_rows, jnp.zeros((1, d), F32))

        def weights(n, _):
            cols = pl.ds(pl.multiple_of(n * ROWS, ROWS), ROWS)
            under = pl.ds(pl.multiple_of(d + n * ROWS, ROWS), ROWS)
            down, up = mm(act[:, cols], c_ref[...], 0, 0), mm(a_ref[:, cols], gpre[...], 0, 0)
            into = unit if joined else units[0].at[0]
            if joined:
                down, up = down + other_ref[cols, :].astype(F32), up + other_ref[under, :].astype(F32)
            into[cols, :] = down.astype(BF)
            into[under, :] = up.astype(BF)
            return 0

        lax.fori_loop(0, d // ROWS, weights, 0)
        if joined:
            bit = t_ref[tiles]
            units[0][...] = unit[pl.ds(pl.multiple_of((1 - bit) * d, d), d), :]
            units[1][...] = unit[pl.ds(pl.multiple_of(bit * d, d), d), :]

    if not after:
        if several:
            @pl.when(j == lead + tiles - 1)
            def _():
                r_out[...] = r_acc[...].astype(BF)
                e_out[...] = e_acc[...].astype(BF)
        return

    @pl.when(j == tiles)
    def _():
        acc[...] = jnp.zeros_like(acc)
        sums_ref[...] = jnp.zeros_like(sums_ref)

    for s in range(steps):
        @pl.when(j == tiles + s)
        def _(s=s):
            for c in block(s):
                c.wait()
            h_ref, m_ref, *past = (t.at[s % 2] for t in held)
            for i in range(STEP // ROWS):
                rows = pl.ds(i * ROWS, ROWS)
                at = pl.ds(s * STEP + i * ROWS, ROWS)
                r, e = r_acc[at, :], e_acc[at, :]
                for n in range(0, after, 2):
                    r = r + past[n][rows, :].astype(F32)
                    e = e + past[n + 1][rows, :].astype(F32)
                h = h_ref[rows, :]
                o_ref[rows, :] = ((h + r + row_of(v_ref, DOWN_BIAS)) * row_of(v_ref, LIVE)).astype(BF)
                n, q = norm_stats(h)
                c = c_ref[at, :].astype(F32)
                gh = c + norm_back(e * row_of(v_ref, SECOND_GAIN), n, q)
                gh_ref[rows, :] = gh
                gb = gh.astype(BF)
                gm_ref[rows, :] = mm(gb, w_ref[...], 1, 1).astype(BF)
                acc[...] += mm(m_ref[rows, :], gb, 0, 0)
                add = lambda t: jnp.sum(t, axis=0, keepdims=True)
                sums_ref[0:1, :] += add(e * n)
                sums_ref[1:2, :] += add(e)
                sums_ref[2:3, :] += add(gb.astype(F32))
                sums_ref[3:4, :] += add(c)
            if s + 2 < steps:
                for c in block(s + 2):
                    c.start()
            if s == steps - 1:
                dw_ref[...] = acc[...].astype(BF)


def mlp_call(tile_bit, tiles, c, up, dn, vecs, a=None, before=None, other=None, after=None):
    L, d = c.shape
    steps = L // STEP
    lead = steps if before else 0
    tile = lambda j: jnp.clip(j - lead, 0, tiles - 1)
    mode = dict(pipeline_mode=pl.Buffered(1)) if tiles == 1 else {}
    first = pl.BlockSpec((STEP, d), lambda j, _: (jnp.minimum(j, steps - 1), 0))
    last = pl.BlockSpec((STEP, d), lambda j, _: (jnp.clip(j - 1, 0, steps - 1), 0))
    seq = shape((L, d), BF)
    in_specs, args, out_specs, out_shape = [], [], [], []
    if before:
        in_specs += [first, once((d, d)), first]
        args += list(before)
        out_specs += [first, first]
        out_shape += [shape((L, d), F32), seq]
    else:
        in_specs += [once((L, d))]
        args += [a]
    in_specs += [once((L, d)), pl.BlockSpec((d, d), lambda j, t: (0, t[tile(j)]), **mode),
                 pl.BlockSpec((d, d), lambda j, t: (t[tile(j)], 0), **mode), once(vecs.shape)]
    args += [c, up, dn, vecs]
    scratch = [pltpu.VMEM((L, d), BF), pltpu.VMEM((L, d), BF)]
    scratch += [pltpu.VMEM((L, d), F32)] * 2 if after or tiles > 1 else [pltpu.VMEM((16, 128), F32)] * 2
    if other is not None:
        in_specs += [once((2 * d, d))]
        args += [other]
        out_specs += [whole((d, d))] * 2
        out_shape += [shape((d, d), BF)] * 2
        scratch += [pltpu.VMEM((2 * d, d), BF)]
    else:
        out_specs += [pl.BlockSpec((1, 2 * d, d), lambda j, _: (tile(j), 0, 0))]
        out_shape += [shape((tiles, 2 * d, d), BF)]
    out_specs += [pl.BlockSpec((1, 1, d), lambda j, _: (tile(j), 0, 0))]
    out_shape += [shape((tiles, 1, d), F32)]
    if before:
        scratch += [pltpu.VMEM((L, d), BF)]
    if after:
        hidden, mixed, w, *past = after
        in_specs += [once((d, d))] + [pl.BlockSpec(memory_space=pl.ANY)] * (2 + len(past))
        args += [w, hidden, mixed] + past
        out_specs += [last, last, last, whole((d, d)), whole((8, d))]
        out_shape += [seq, shape((L, d), F32), seq, shape((d, d), BF), shape((8, d), F32)]
        scratch += [pltpu.VMEM((d, d), F32), pltpu.SemaphoreType.DMA((2, len(past) + 2)), pltpu.VMEM((2, STEP, d), F32)]
        scratch += [pltpu.VMEM((2, STEP, d), BF)] * (1 + len(past))
    else:
        out_specs += [whole((L, d))] * 2
        out_shape += [seq, seq]
    return pl.pallas_call(
        partial(mlp_kernel, before is not None, tiles, other is not None, len(after) - 3 if after else 0, steps),
        grid_spec=pltpu.PrefetchScalarGridSpec(
            num_scalar_prefetch=1,
            grid=(tiles + lead + (steps if after else 0),),
            in_specs=in_specs, out_specs=out_specs, scratch_shapes=scratch,
        ),
        out_shape=out_shape,
        compiler_params=params("mlp", L),
        cost_estimate=cost(12 * tiles),
        name="mlp",
    )(tile_bit, *args)


def attend_back_kernel(q_ref, k_ref, v_ref, p_ref, i_ref, g_ref, m_ref, dq_ref, dk_ref, dv_ref, dk_acc, dv_acc):
    L = q_ref.shape[0]
    low = lax.broadcasted_iota(jnp.int32, (ROWS, 128), 1) < 64
    nb = L // ROWS
    jobs = [(i, h) for i in reversed(range(nb)) for h in range(2)]
    strips = {}
    def strip(i):
        if i not in strips:
            rows = pl.ds(i * ROWS, ROWS)
            g32 = g_ref[rows, :].astype(F32) * i_ref[rows, :].astype(F32)
            g = g32.astype(BF)
            gm = g32 * m_ref[rows, :].astype(F32)
            strips[i] = (g, gm, q_ref[rows, :].T, g.T)
        return strips[i]

    def dprob(i, h):
        g, gm, _, _ = strip(i)
        mine = low if h == 0 else ~low
        gh = jnp.where(mine, g, jnp.zeros_like(g))
        delta = jnp.sum(jnp.where(mine, gm, 0.0), axis=-1, keepdims=True)
        return mm(gh, v_ref[pl.ds(0, (i + 1) * ROWS), :], 1, 1), delta

    dqs = {}
    ahead = [dprob(*jobs[0])]
    for t, (i, h) in enumerate(jobs):
        dp, delta = ahead.pop(0)
        if t + 1 < len(jobs):
            ahead.append(dprob(*jobs[t + 1]))
        n = (i + 1) * ROWS
        past = pl.ds(0, n)
        _, _, qt, gt = strip(i)
        p = p_ref[h, :, pl.ds(i * (i + 1) // 2 * ROWS, n)]
        side = pl.ds(64 * h, 64)
        dv = mm(gt[64 * h : 64 * h + 64], p, 1, 0)
        ds = (p.astype(F32) * (dp - delta)).astype(BF)
        dqs[h] = mm(ds, k_ref[past, :], 1, 0)
        dk = mm(qt[64 * h : 64 * h + 64], ds, 1, 0)
        if i == nb - 1:
            dk_acc[side, past] = dk
            dv_acc[side, past] = dv
        else:
            dk_acc[side, past] += dk
            dv_acc[side, past] += dv
        if h == 1:
            dq_ref[pl.ds(i * ROWS, ROWS), :] = (jnp.where(low, dqs[0], dqs[1]) * 0.125).astype(BF)
    dk_ref[...] = dk_acc[...].T.astype(BF)
    dv_ref[...] = dv_acc[...].T.astype(BF)


def attend_back_call(qkv, p, inv, gm, mixed, lo, count, held=()):
    L, d3 = qkv.shape
    n = d3 // 3 // 128
    col = lambda k: pl.BlockSpec((L, 128), lambda j: (0, k * n + lo + j))
    s = shape((L, d3 // 3), BF)
    kernel = attend_back_kernel
    if held:
        kernel = lambda *refs: attend_back_kernel(*refs[:7], *refs[10:])
    return pl.pallas_call(
        kernel,
        grid=(count,),
        in_specs=[col(0), col(1), col(2), pl.BlockSpec((2, ROWS, tri_cols(L)), lambda j: (lo + j, 0, 0)), col(0), col(0), col(0)]
        + [pl.BlockSpec(memory_space=pl.ANY)] * len(held),
        out_specs=[col(0)] * 3,
        out_shape=[s] * 3,
        input_output_aliases={7 + i: i for i in range(len(held))},
        scratch_shapes=[pltpu.VMEM((128, L), F32), pltpu.VMEM((128, L), F32)],
        compiler_params=params("attend_back", L),
        cost_estimate=cost(3 * count),
        name="attend_back",
    )(qkv, qkv, qkv, p, inv, gm, mixed, *held)


def joint_sent_kernel(core_ref, a_ref, q_ref, k_ref, v_ref, w_ref, out_ref, sums_ref):
    d = a_ref.shape[1]
    sums_ref[...] = jnp.zeros_like(sums_ref)
    sums_ref[0:1, :] = jnp.sum(q_ref[...].astype(F32), axis=0, keepdims=True)
    sums_ref[1:2, :] = jnp.sum(v_ref[...].astype(F32), axis=0, keepdims=True)

    @pl.when(core_ref[0] == 1)
    def _():
        out_ref[0:d, :] = mm(a_ref[...], q_ref[...], 0, 0).astype(BF)
        out_ref[d : 2 * d, :] = mm(a_ref[...], k_ref[...], 0, 0).astype(BF)

    @pl.when(core_ref[0] == 0)
    def _():
        out_ref[0:d, :] = mm(a_ref[...], v_ref[...], 0, 0).astype(BF)
        out_ref[d : 2 * d, :] = w_ref[...]


def joint_sent_call(core, a, dq, dk, dv, dw):
    L, d = a.shape
    return pl.pallas_call(
        joint_sent_kernel,
        grid_spec=pltpu.PrefetchScalarGridSpec(
            num_scalar_prefetch=1, grid=(1,), in_specs=[once((L, d))] * 4 + [once((d, d))],
            out_specs=[whole((2 * d, d)), whole((8, d))]),
        out_shape=[shape((2 * d, d), BF), shape((8, d), F32)],
        compiler_params=params("joint_sent", L),
        cost_estimate=cost(5),
        name="joint_sent",
    )(core, a, dq, dk, dv, dw)


def joint_kept_kernel(core_ref, a_ref, q_ref, k_ref, v_ref, w_ref, other_ref, sent_ref, kept_ref, unit):
    d = a_ref.shape[1]
    add = lambda t, n: (t + other_ref[n * d : (n + 1) * d, :].astype(F32)).astype(BF)

    @pl.when(core_ref[0] == 0)
    def _():
        unit[0:d, :] = add(mm(a_ref[...], q_ref[...], 0, 0), 0)
        unit[d : 2 * d, :] = add(mm(a_ref[...], k_ref[...], 0, 0), 1)

    @pl.when(core_ref[0] == 1)
    def _():
        unit[0:d, :] = add(mm(a_ref[...], v_ref[...], 0, 0), 0)
        unit[d : 2 * d, :] = add(w_ref[...].astype(F32), 1)

    bit = core_ref[1]
    sent_ref[...] = unit[pl.ds(pl.multiple_of((1 - bit) * d, d), d), :]
    kept_ref[...] = unit[pl.ds(pl.multiple_of(bit * d, d), d), :]


def joint_kept_call(core_bit, a, dq, dk, dv, dw, other):
    L, d = a.shape
    return pl.pallas_call(
        joint_kept_kernel,
        grid_spec=pltpu.PrefetchScalarGridSpec(
            num_scalar_prefetch=1, grid=(1,), in_specs=[once((L, d))] * 4 + [once((d, d)), once((2 * d, d))],
            out_specs=[whole((d, d)), whole((d, d))], scratch_shapes=[pltpu.VMEM((2 * d, d), BF)]),
        out_shape=[shape((d, d), BF)] * 2,
        compiler_params=params("joint_kept", L),
        cost_estimate=cost(5),
        name="joint_kept",
    )(core_bit, a, dq, dk, dv, dw, other)


def tokens_kernel(q_ref, k_ref, v_ref, w_ref, x_ref, gh_ref, vec_ref, o_ref, sums_ref):
    i = pl.program_id(0)
    d = x_ref.shape[1]

    @pl.when(i == 0)
    def _():
        sums_ref[...] = jnp.zeros_like(sums_ref)

    def back(i):
        rows = pl.ds(i * ROWS, ROWS)
        return (mm(q_ref[rows, :], w_ref[:, 0:d], 1, 1) + mm(k_ref[rows, :], w_ref[:, d : 2 * d], 1, 1)
                + mm(v_ref[rows, :], w_ref[:, 2 * d :], 1, 1))

    ahead = back(0)
    for j in range(STEP // ROWS):
        e, rows = ahead, pl.ds(j * ROWS, ROWS)
        if (j + 1) * ROWS < STEP:
            ahead = back(j + 1)
        n, r = norm_stats(x_ref[rows, :].astype(F32))
        o_ref[rows, :] = (gh_ref[rows, :] + norm_back(e * row_of(vec_ref, FIRST_GAIN), n, r)).astype(BF)
        sums_ref[0:1, :] += jnp.sum(e * n, axis=0, keepdims=True)
        sums_ref[1:2, :] += jnp.sum(e, axis=0, keepdims=True)


def tokens_call(dq, dk, dv, w, x, gh, vecs):
    L, d = x.shape
    blk = pl.BlockSpec((STEP, d), lambda i: (i, 0))
    return pl.pallas_call(
        tokens_kernel,
        grid=(L // STEP,),
        in_specs=[blk, blk, blk, once((d, 3 * d)), blk, blk, once(vecs.shape)],
        out_specs=[blk, whole((8, d))],
        out_shape=[shape((L, d), BF), shape((8, d), F32)],
        compiler_params=params("tokens_back", L),
        cost_estimate=cost(9),
        name="tokens_back",
    )(dq, dk, dv, w, x, gh, vecs)


def place_kernel(core_ref, own_ref, other_ref, *rest):
    down_ref, up_ref = rest[-2:]
    d = down_ref.shape[1]
    for n, ref in enumerate((own_ref, other_ref)):
        @pl.when(pl.program_id(0) == n)
        def _(ref=ref):
            down_ref[...] = ref[0:d, :].astype(F32)
            up_ref[...] = ref[d : 2 * d, :].astype(F32)


def place_call(core, own, other, tile, ff, held=()):
    d = own.shape[1]
    at = lambda n, s: tile + jnp.where(n == 0, s[0], 1 - s[0])
    return pl.pallas_call(
        place_kernel,
        grid_spec=pltpu.PrefetchScalarGridSpec(
            num_scalar_prefetch=1,
            grid=(2,),
            in_specs=[whole((2 * d, d))] * 2 + [pl.BlockSpec(memory_space=pl.ANY)] * len(held),
            out_specs=[pl.BlockSpec((d, d), lambda n, s: (at(n, s), 0)), pl.BlockSpec((d, d), lambda n, s: (0, at(n, s)))],
        ),
        out_shape=[shape((ff, d), F32), shape((d, ff), F32)],
        input_output_aliases={3 + i: i for i in range(len(held))},
        compiler_params=params("place"),
        cost_estimate=cost(5),
        name="place",
    )(core, own, other, *held)


def place_joint_kernel(core_ref, own_ref, other_ref, joint_ref, out_ref, small_ref):
    d = out_ref.shape[0]

    for core, (qk_ref, vw_ref) in enumerate(((own_ref, other_ref), (other_ref, own_ref))):
        @pl.when(core_ref[0] == core)
        def _(qk_ref=qk_ref, vw_ref=vw_ref):
            joint_ref[:, 0:d] = qk_ref[0:d, :].astype(F32)
            joint_ref[:, d : 2 * d] = qk_ref[d : 2 * d, :].astype(F32)
            joint_ref[:, 2 * d : 3 * d] = vw_ref[0:d, :].astype(F32)
            out_ref[...] = vw_ref[d : 2 * d, :].astype(F32)

    small_ref[...] = own_ref[2 * d :, :].astype(F32) + other_ref[2 * d :, :].astype(F32)


def place_joint(core, own, other):
    rows, d = own.shape
    v = pl.BlockSpec(memory_space=pltpu.VMEM)
    return pl.pallas_call(
        place_joint_kernel,
        in_specs=[pl.BlockSpec(memory_space=pltpu.SMEM), v, v],
        out_specs=[v] * 3,
        out_shape=[shape((d, 3 * d), F32), shape((d, d), F32), shape((rows - 2 * d, d), F32)],
        compiler_params=params("place_joint"),
        cost_estimate=cost(5),
        name="place_joint",
    )(core, own, other)


def halve_kernel(up_ref, a_ref, b_ref, c_ref, d_ref, sent_ref, kept_ref):
    sent_ref[...] = a_ref[...] + b_ref[...]
    kept_ref[...] = c_ref[...] + d_ref[...]


def halve_call(up, kept, other):
    rows, d = kept.shape[0] // 2, kept.shape[1]
    block = rows if rows <= 384 else rows // 2
    n = rows // block
    go = pl.BlockSpec((block, d), lambda i, up: ((1 - up[0]) * n + i, 0))
    stay = pl.BlockSpec((block, d), lambda i, up: (up[0] * n + i, 0))
    out = pl.BlockSpec((block, d), lambda i, up: (i, 0))
    s = shape((rows, d), BF)
    return pl.pallas_call(
        halve_kernel,
        grid_spec=pltpu.PrefetchScalarGridSpec(
            num_scalar_prefetch=1, grid=(n,), in_specs=[go, go, stay, stay], out_specs=[out, out]),
        out_shape=[s, s],
        compiler_params=params("halve"),
        cost_estimate=cost(2),
        name="halve",
    )(up, kept, other, kept, other)


def double_kernel(rows, up_ref, a_ref, b_ref, o_ref):
    up = up_ref[0]
    o_ref[pl.ds(pl.multiple_of(up * rows, 16), rows), :] = a_ref[0:rows, :]
    o_ref[pl.ds(pl.multiple_of((1 - up) * rows, 16), rows), :] = b_ref[0:rows, :]
    if a_ref.shape[0] > rows:
        tail = a_ref[rows:, :].astype(F32) + b_ref[rows:, :].astype(F32)
        o_ref[2 * rows :, :] = tail.astype(BF)


def double_call(up, kept, other, tail=0):
    rows, d = kept.shape[0] - tail, kept.shape[1]
    v = pl.BlockSpec(memory_space=pltpu.VMEM)
    return pl.pallas_call(
        partial(double_kernel, rows),
        in_specs=[pl.BlockSpec(memory_space=pltpu.SMEM), v, v],
        out_specs=v,
        out_shape=shape((2 * rows + tail, d), BF),
        compiler_params=params("double"),
        cost_estimate=cost(2),
        name="double",
    )(up, kept, other)


def arrange_kernel(places, at_ref, *refs):
    out_ref = refs[-1]
    for k, ref in enumerate(refs[:-1]):
        if places < len(refs) - 1:
            @pl.when(at_ref[k] < places)
            def _(k=k, ref=ref):
                out_ref[at_ref[k]] = ref[...]
        else:
            out_ref[at_ref[k]] = ref[...]


def arrange_call(at, parts, places):
    block, d = parts[0].shape
    v = pl.BlockSpec(memory_space=pltpu.VMEM)
    return pl.pallas_call(
        partial(arrange_kernel, places),
        in_specs=[pl.BlockSpec(memory_space=pltpu.SMEM)] + [v] * len(parts),
        out_specs=v,
        out_shape=shape((places, block, d), BF),
        compiler_params=params("arrange"),
        cost_estimate=cost(2),
        name="arrange",
    )(at, *parts)


def small_kernel(core_ref, first_ref, joint_ref, second_ref, b0, b1, b2, b3, o_ref):
    o_ref[...] = jnp.zeros_like(o_ref)
    o_ref[0:2, :] = first_ref[0:2, :].astype(BF)
    o_ref[2:4, :] = joint_ref[0:2, :].astype(BF)
    o_ref[4:8, :] = second_ref[0:4, :].astype(BF)
    for n, (u, v) in enumerate(((b0, b1), (b1, b0), (b2, b3), (b3, b2))):
        o_ref[8 + n : 9 + n, :] = jnp.where(core_ref[0] == 0, u[0], v[0]).astype(BF)


def small_call(core, first, joint, second, up_bias):
    v = pl.BlockSpec(memory_space=pltpu.VMEM)
    return pl.pallas_call(
        small_kernel,
        in_specs=[pl.BlockSpec(memory_space=pltpu.SMEM)] + [v] * 7,
        out_specs=v,
        out_shape=shape((16, first.shape[1]), BF),
        compiler_params=params("small"),
        cost_estimate=cost(1),
        name="small",
    )(core, first, joint, second, *up_bias)


def bits_of(count):
    assert count & (count - 1) == 0
    return count.bit_length() - 1


class Moves:
    def __init__(self, n_dp, n_blk, slots):
        assert slots <= n_blk
        self.n_dp, self.n_blk, self.slots = n_dp, n_blk, slots
        self.dp, self.blk = lax.axis_index("dp"), lax.axis_index("blk")
        self.odd = self.dp % 2

    def slot(self, blk):
        return jnp.where(self.odd == 1, self.n_blk - 1 - blk, blk)

    def perm(self, step, back):
        pairs = []
        for g in range(self.n_dp):
            for b in range(self.n_blk):
                d = (b + step) % self.n_blk
                s = self.n_blk - 1 - d if g % 2 else d
                if s < self.slots:
                    pair = (g * self.n_blk + b, g * self.n_blk + d)
                    pairs.append(pair[::-1] if back else pair)
        return pairs

    def send_out(self, x, beside=None):
        parts = []
        for step in range(self.n_blk):
            if beside is not None and step == self.n_blk - 1:
                x = lax.optimization_barrier((x, beside))[0]
            s = jnp.minimum(self.slot((self.blk + step) % self.n_blk), self.slots - 1)
            part = lax.dynamic_index_in_dim(x, s, 0, keepdims=False)
            parts.append(lax.ppermute(part, ("dp", "blk"), self.perm(step, False)) if step else part)
        return parts

    def join(self, parts):
        at = (self.blk - jnp.arange(self.n_blk, dtype=jnp.int32)) % self.n_blk
        return arrange_call(at, parts, self.n_blk).reshape(-1, parts[0].shape[1])

    def send_back(self, y):
        y = y.reshape(self.n_blk, -1, y.shape[-1])
        parts = []
        for step in range(self.n_blk):
            part = lax.dynamic_index_in_dim(y, (self.blk - step) % self.n_blk, 0, keepdims=False)
            parts.append(lax.ppermute(part, ("dp", "blk"), self.perm(step, True)) if step else part)
        return parts

    def exchange_back(self, y):
        return lax.all_to_all(y.reshape(self.n_blk, -1, y.shape[-1]), "blk", 0, 0)

    def unexchange(self, y):
        return jnp.where(self.odd == 1, y[::-1][: self.slots], y[: self.slots])

    def unjoin(self, parts):
        at = self.slot((self.blk + jnp.arange(self.n_blk, dtype=jnp.int32)) % self.n_blk)
        return arrange_call(at, parts, self.slots)


class Order:
    def __init__(self):
        self.last = None

    def take(self, *arrays):
        if self.last is not None:
            arrays = lax.optimization_barrier(arrays + (self.last,))[:-1]
        return arrays if len(arrays) > 1 else arrays[0]

    def mark(self, array):
        self.last = array


class Sum:
    def __init__(self, moves):
        self.n = moves.n_dp * moves.n_blk
        self.me = moves.dp * moves.n_blk + moves.blk
        low, high = bits_of(moves.n_blk), bits_of(moves.n_dp)
        plane = [low + 1 + i for i in range(high - 1)]
        self.core = low
        self.orders = [plane + list(range(low)), plane[::-1] + list(range(low))]
        self.stages = len(self.orders[0])
        self.tail = None

    def order(self, i, stage):
        return self.core if stage < 0 else self.orders[(i >> self.core) & 1][stage]

    def swap(self, x, stage):
        return lax.ppermute(x, ("dp", "blk"), [(i, i ^ (1 << self.order(i, stage))) for i in range(self.n)])

    def up(self, stage, me=None):
        me = self.me if me is None else me
        odd = (me >> self.core) & 1
        return jnp.where(odd == 0, (me >> self.order(0, stage)) & 1, (me >> self.order(1 << self.core, stage)) & 1)

    def cross(self, sent):
        self.moving = self.swap(sent, -1)

    def crossed(self, order):
        return order.take(self.moving)

    def begin(self, sent, kept):
        self.sent, self.kept, self.stage, self.gathering = sent, kept, 0, False
        self.send()

    def send(self):
        if not self.gathering:
            self.moving = self.swap(self.sent, self.stage)
        else:
            self.moving = self.swap(self.kept, self.stage)

    def step(self, order):
        other, self.kept = order.take(self.moving, self.kept)
        if not self.gathering:
            self.stage += 1
            if self.stage == self.stages:
                self.kept = self.kept + other
                if self.tail is not None:
                    self.kept = jnp.concatenate([self.kept, self.tail])
                self.gathering = True
                self.stage -= 1
            else:
                half = self.kept.shape[0] // 2
                up = self.up(self.stage)
                if half % 16 == 0:
                    self.sent, self.kept = halve_call(up.reshape(1), self.kept, other)
                else:
                    part = lambda x, at: lax.dynamic_slice_in_dim(x, at * half, half, 0)
                    self.sent = part(self.kept, 1 - up) + part(other, 1 - up)
                    self.kept = part(self.kept, up) + part(other, up)
        else:
            tail = 0 if self.tail is None else self.tail.shape[0]
            self.kept = double_call(self.up(self.stage).reshape(1), self.kept, other, tail)
            self.stage -= 1
        order.mark(self.kept)
        self.send()

    def finish(self, order):
        theirs = order.take(self.moving)
        return ((self.me >> self.core) & 1).reshape(1), self.kept, theirs


PLAN = (
    "m1", "m2", "m3", "m4", "o", "1", "ab1", "1", "x", "ab2", "2", "1", "O", "js", "tok", "2", "jk", "1", "2", "3",
    "1", "3", "2", "1", "3", "2", "3", "1", "g", "3", "2", "3", "2", "1", "a", "3", "3", "1", "b", "c", "2", "3",
    "G", "2",
)


def on_device(n_dp, n_blk, tokens, live_count, first_gain, first_shift, joint_weight, query_bias, value_bias,
              out_weight, out_bias, second_gain, second_shift, up_weight, up_bias, down_weight, down_bias, cotangent):
    slots, block, d = tokens.shape
    ff = up_weight.shape[1]
    assert ff == 4 * d
    pairs = d // 128
    moves = Moves(n_dp, n_blk, slots)
    order = Order()
    mine = moves.slot(moves.blk)
    live = ((mine < slots) & (mine < live_count[0])).astype(F32)
    core = moves.odd.reshape(1)
    vecs = vectors_call([first_gain, first_shift, query_bias, value_bias, out_bias, second_gain, second_shift,
                         down_bias, up_bias], live.reshape(1))
    live_slots = jnp.arange(slots, dtype=jnp.int32) < live_count[0]

    x_parts = moves.send_out(tokens, vecs)
    x = moves.join(x_parts)
    attn_in, qkv = joint_call(x, joint_weight, vecs)
    c = jnp.where(live_slots[:, None, None], lax.optimization_barrier((cotangent, x))[0], jnp.zeros_like(cotangent))
    c_parts = moves.send_out(c)
    c_parts[0] = jnp.where(mine < slots, c_parts[0], jnp.zeros_like(c_parts[0]))
    mixed, p, inv = attend_call(qkv)
    order.mark(mixed)
    c = moves.join(list(order.take(*c_parts)))

    sums = {name: Sum(moves) for name in "123"}
    got = {}
    bit = sums["2"].up(0).reshape(1)
    tile = lambda which, tiles, **more: mlp_call(which, tiles, c, up_weight, down_weight, vecs, **more)

    def m1():
        got["hidden"], got["a"], sent, got["gb1"], *past = tile(1 - core, 1, before=(mixed, out_weight, x))
        sums["1"].cross(sent[0])
        got["past"] = tuple(past)
        return past[0]

    def m2():
        sent, got["gb3"], *past = tile(3 - core, 1, a=order.take(got["a"]))
        sums["2"].cross(sent[0])
        got["past"] += tuple(past)
        return past[0]

    def m3():
        other = sums["1"].crossed(order)
        sent, kept, got["gb0"], *past = tile(jnp.concatenate([core, bit]), 1, a=order.take(got["a"]), other=other)
        sums["1"].begin(sent, kept)
        got["past"] += tuple(past)
        return past[0]

    def m4():
        other = sums["2"].crossed(order)
        after = (got["hidden"], mixed, out_weight) + got["past"]
        sent, kept, gb, out, gh, gm, dwo, s = tile(jnp.concatenate([2 + core, bit]), 1, a=order.take(got["a"]), other=other,
                                                   after=after)
        sums["2"].begin(sent, kept)
        got.update(gb2=gb, out=out, gh=gh, gm=gm, dwo=dwo, sums2=s)
        return gh

    def ab1():
        count = pairs // 2 if "ab2" in PLAN else pairs
        got["back"] = attend_back_call(qkv, p, inv, order.take(got["gm"]), mixed, 0, count)
        return got["back"][0]

    def ab2():
        got["back"] = attend_back_call(qkv, p, inv, order.take(got["gm"]), mixed, pairs // 2, pairs - pairs // 2,
                                       got["back"])
        return got["back"][0]

    def js():
        sent, got["sums1"] = joint_sent_call(core, order.take(attn_in), *got["back"], got["dwo"])
        sums["3"].cross(sent)
        return sent

    def jk():
        other = sums["3"].crossed(order)
        sent, kept = joint_kept_call(jnp.concatenate([core, bit]), order.take(attn_in), *got["back"], got["dwo"], other)
        sums["3"].begin(sent, kept)
        return kept

    def tok():
        dq, dk, dv = got["back"]
        got["gx"], sums0 = tokens_call(order.take(dq), dk, dv, joint_weight, x, got["gh"], vecs)
        order.mark(got["gx"])
        sums["3"].tail = small_call(core, order.take(sums0), got["sums1"], got["sums2"], [got["gb%d" % n] for n in range(4)])
        return sums["3"].tail

    def send(name):
        if name == "out" and not PLAN.count("x"):
            got["out_moved"] = moves.exchange_back(order.take(got["out"]))
        else:
            got[name + "_parts"] = moves.send_back(order.take(got[name]))

    def part(name, k):
        parts = got[name + "_parts"]
        if k < len(parts):
            parts[k] = order.take(parts[k])
            order.mark(parts[k])

    def join(name):
        if name == "out" and "out_moved" in got:
            got["out"] = moves.unexchange(order.take(got["out_moved"]))
            return got["out"]
        got[name] = moves.unjoin(list(order.take(*got[name + "_parts"])))
        return got[name]

    def step(name):
        total = sums.get(name)
        if total is None:
            return
        if not total.gathering or total.stage >= 0:
            total.step(order)
        else:
            sums[name] = None
            if name == "3":
                got["joint"] = place_joint(*total.finish(order))
                order.mark(got["joint"][1])
            else:
                got["wide"] = place_call(*total.finish(order), 2 * int(name) - 2, ff, got.get("wide", ()))
                order.mark(got["wide"][0])

    kernels = dict(m1=m1, m2=m2, m3=m3, m4=m4, ab1=ab1, ab2=ab2, js=js, jk=jk, tok=tok)
    for word in PLAN + ("2", "1", "3") * 12:
        if word in kernels:
            order.mark(kernels[word]())
        elif word in "abc":
            part("gx", 1 + "abc".index(word))
        elif word in "xyz":
            part("out", 1 + "xyz".index(word))
        elif word in "og":
            send({"o": "out", "g": "gx"}[word])
        elif word in "OG":
            order.mark(join({"O": "out", "G": "gx"}[word]))
        else:
            step(word)
    small = got["joint"][2]
    return (got["out"], got["gx"], small[0], small[1], got["joint"][0], small[2], small[3], got["joint"][1], small[6],
            small[4], small[5], got["wide"][1], small[8:12].reshape(-1), got["wide"][0], small[7])


def solution(mesh):
    seq = P("dp", "blk", None)
    n_dp, n_blk = mesh.shape["dp"], mesh.shape["blk"]
    return jax.shard_map(
        partial(on_device, n_dp, n_blk), mesh=mesh,
        in_specs=(seq, P("dp")) + (P(),) * 13 + (seq,),
        out_specs=(seq, seq) + (P(),) * 13,
        check_vma=False,
    )
```

```python
import math
from functools import partial
import jax
import jax.numpy as jnp
from jax import lax
from jax.experimental import pallas as pl
from jax.experimental.pallas import tpu as pltpu
from jax.sharding import PartitionSpec as P

BF = jnp.bfloat16
F32 = jnp.float32
HEADS = 12
EPS = 1e-5
ROWS = 256
STEP = 512
COST = 1000
MIB = dict(arrange=8, double=16, halve=16, joint=30, joint_kept=30, joint_sent=30, mlp=60, place=30, place_joint=30,
           small=8, tokens_back=24, vectors=8)


def params(name, length=1024):
    return pltpu.CompilerParams(vmem_limit_bytes=min(60, MIB.get(name, 60) * max(length, 1024) // 1024) * 2**20)


def cost(us):
    return pl.CostEstimate(flops=int(us * COST), bytes_accessed=1000, transcendentals=0)


def mm(a, b, ca, cb):
    return lax.dot_general(a, b, (((ca,), (cb,)), ((), ())), preferred_element_type=F32)


def shape(s, d):
    return pltpu.HBM(s, d)


def whole(s):
    n = len(s)
    return pl.BlockSpec(s, lambda *_: (0,) * n)


def norm_stats(t):
    c = t - jnp.mean(t, axis=-1, keepdims=True)
    r = lax.rsqrt(jnp.mean(c * c, axis=-1, keepdims=True) + EPS)
    return c * r, r


(FIRST_GAIN, FIRST_SHIFT, QUERY_BIAS, ZERO, VALUE_BIAS, OUT_BIAS, SECOND_GAIN, SECOND_SHIFT, DOWN_BIAS, LIVE,
 UP_BIAS) = range(11)


def row_of(ref, n):
    return ref[n : n + 1, :]


def once(s):
    n = len(s)
    return pl.BlockSpec(s, lambda *_: (0,) * n, pipeline_mode=pl.Buffered(1))


def vectors_kernel(live_ref, *refs):
    out_ref = refs[-1]
    d = out_ref.shape[1]
    out_ref[...] = jnp.zeros_like(out_ref)
    at = (FIRST_GAIN, FIRST_SHIFT, QUERY_BIAS, VALUE_BIAS, OUT_BIAS, SECOND_GAIN, SECOND_SHIFT, DOWN_BIAS)
    for n, ref in zip(at, refs):
        out_ref[n : n + 1, :] = ref[...].reshape(1, d)
    for n in range(refs[-2].shape[0] // d):
        out_ref[UP_BIAS + n : UP_BIAS + n + 1, :] = refs[-2][pl.ds(n * d, d)].reshape(1, d)
    out_ref[LIVE : LIVE + 1, :] = jnp.full((1, d), live_ref[0], F32)


def vectors_call(vectors, live):
    d, ff = vectors[0].shape[0], vectors[-1].shape[0]
    v = pl.BlockSpec(memory_space=pltpu.VMEM)
    return pl.pallas_call(
        vectors_kernel,
        in_specs=[pl.BlockSpec(memory_space=pltpu.SMEM)] + [v] * len(vectors),
        out_shape=shape(((UP_BIAS + ff // d + 7) // 8 * 8, d), F32),
        compiler_params=params("vectors"),
        cost_estimate=cost(1),
        name="vectors",
    )(live, *vectors)


def joint_kernel(x_ref, w_ref, v_ref, a_ref, q_ref):
    d = x_ref.shape[1]

    def norm(i):
        n, _ = norm_stats(x_ref[pl.ds(i * ROWS, ROWS), :].astype(F32))
        return (n * row_of(v_ref, FIRST_GAIN) + row_of(v_ref, FIRST_SHIFT)).astype(BF)

    ahead = norm(0)
    for i in range(STEP // ROWS):
        a, rows = ahead, pl.ds(i * ROWS, ROWS)
        a_ref[rows, :] = a
        for j, bias in enumerate((QUERY_BIAS, ZERO, VALUE_BIAS)):
            if j == 1 and (i + 1) * ROWS < STEP:
                ahead = norm(i + 1)
            cols = pl.ds(j * d, d)
            t = (mm(a, w_ref[:, cols], 1, 0) + row_of(v_ref, bias)).astype(BF)
            q_ref[rows, cols] = t * jnp.asarray(0.125, BF) if j == 0 else t


def joint_call(x, w, vecs):
    L, d = x.shape
    return pl.pallas_call(
        joint_kernel,
        grid=(L // STEP,),
        in_specs=[pl.BlockSpec((STEP, d), lambda i: (i, 0)), once((d, 3 * d)), once(vecs.shape)],
        out_specs=[pl.BlockSpec((STEP, d), lambda i: (i, 0)), pl.BlockSpec((STEP, 3 * d), lambda i: (i, 0))],
        out_shape=[shape((L, d), BF), shape((L, 3 * d), BF)],
        compiler_params=params("joint", L),
        cost_estimate=cost(7),
        name="joint",
    )(x, w, vecs)


def tri_cols(L):
    n = L // ROWS
    return n * (n + 1) // 2 * ROWS


def attend_kernel(q_ref, k_ref, v_ref, o_ref, p_ref, i_ref):
    L = q_ref.shape[0]
    low = lax.broadcasted_iota(jnp.int32, (ROWS, 128), 1) < 64
    low_all = lax.broadcasted_iota(jnp.int32, (L, 128), 1) < 64
    tri = lax.broadcasted_iota(jnp.int32, (ROWS, ROWS), 1) <= lax.broadcasted_iota(jnp.int32, (ROWS, ROWS), 0)
    v = v_ref[...]
    one = jnp.ones_like(v)
    vs = [jnp.where(low_all, v, one), jnp.where(low_all, one, v)]
    jobs = [(i, h) for i in range(L // ROWS) for h in range(2)]

    def score(i, h):
        q = q_ref[pl.ds(i * ROWS, ROWS), :]
        qh = jnp.where(low if h == 0 else ~low, q, jnp.zeros_like(q))
        return mm(qh, k_ref[pl.ds(0, (i + 1) * ROWS), :], 1, 1)

    outs = [None, None]
    ahead = [score(*job) for job in jobs[:2]]
    for t, (i, h) in enumerate(jobs):
        s = ahead.pop(0)
        if t + 2 < len(jobs):
            ahead.append(score(*jobs[t + 2]))
        past = (i + 1) * ROWS
        diag = jnp.where(tri, s[:, i * ROWS :], -1e30)
        m = jnp.max(diag, axis=-1, keepdims=True)
        if i:
            m = jnp.maximum(m, jnp.max(s[:, : i * ROWS], axis=-1, keepdims=True))
            p = jnp.concatenate([jnp.exp(s[:, : i * ROWS] - m).astype(BF), jnp.exp(diag - m).astype(BF)], axis=1)
        else:
            p = jnp.exp(diag - m).astype(BF)
        p_ref[h, :, pl.ds(i * (i + 1) // 2 * ROWS, past)] = p
        outs[h] = mm(p, vs[h][:past], 1, 0)
        if h == 1:
            rows = pl.ds(i * ROWS, ROWS)
            inv = 1.0 / jnp.where(low, pltpu.roll(outs[0], 64, 1), pltpu.roll(outs[1], 64, 1))
            o_ref[rows, :] = (jnp.where(low, outs[0], outs[1]) * inv).astype(BF)
            i_ref[rows, :] = inv.astype(BF)


def attend_call(qkv):
    L, d3 = qkv.shape
    n = d3 // 3 // 128
    col = lambda k: pl.BlockSpec((L, 128), lambda j: (0, k * n + j))
    return pl.pallas_call(
        attend_kernel,
        grid=(n,),
        in_specs=[col(0), col(1), col(2)],
        out_specs=[col(0), pl.BlockSpec((2, ROWS, tri_cols(L)), lambda j: (j, 0, 0)), col(0)],
        out_shape=[shape((L, d3 // 3), BF), shape((2 * n, ROWS, tri_cols(L)), BF), shape((L, d3 // 3), BF)],
        compiler_params=params("attend", L),
        cost_estimate=cost(15),
        name="attend",
    )(qkv, qkv, qkv)


GC = math.sqrt(2.0 / math.pi)


def gelu_both(u):
    u2 = u * u
    t = jnp.tanh(u * (GC + GC * 0.044715 * u2))
    half = 0.5 + 0.5 * t
    return u * half, half + u * (0.5 - 0.5 * t * t) * (GC + 3 * GC * 0.044715 * u2)


def norm_back(e, n, r):
    return r * (e - jnp.mean(e, axis=-1, keepdims=True) - n * jnp.mean(e * n, axis=-1, keepdims=True))


def mlp_kernel(before, tiles, joined, after, steps, t_ref, *refs):
    refs = list(refs)
    take = lambda n: [refs.pop(0) for _ in range(n)]
    if before:
        m_ref, w_ref, x_ref = take(3)
    else:
        a_ref, = take(1)
    c_ref, up_ref, dn_ref, v_ref = take(4)
    if joined:
        other_ref, = take(1)
    if after:
        w_ref, *late = take(3 + after)
    if before:
        h_out, a_out = take(2)
    units = take(2 if joined else 1)
    gb_ref, = take(1)
    several = tiles > 1 or after
    if after:
        o_ref, gh_ref, gm_ref, dw_ref, sums_ref = take(5)
    else:
        r_out, e_out = take(2)
    act, gpre, r_acc, e_acc = take(4)
    if joined:
        unit, = take(1)
    if before:
        a_ref, = take(1)
    if after:
        acc, sems, *held = take(4 + after)
    j = pl.program_id(0)
    L, d = c_ref.shape
    lead = steps if before else 0

    def block(s):
        rows = pl.ds(s * STEP, STEP)
        return [pltpu.make_async_copy(src.at[rows, :], dst.at[s % 2], sems.at[s % 2, n])
                for n, (src, dst) in enumerate(zip(late, held))]

    if after:
        @pl.when(j == 0)
        def _():
            for s in range(2):
                for c in block(s):
                    c.start()

    if before:
        @pl.when(j < lead)
        def _():
            part = lambda i: mm(m_ref[pl.ds(i * ROWS, ROWS), :], w_ref[...], 1, 0)
            ahead = part(0)
            for i in range(STEP // ROWS):
                got, rows = ahead, pl.ds(i * ROWS, ROWS)
                if (i + 1) * ROWS < STEP:
                    ahead = part(i + 1)
                h = x_ref[rows, :].astype(F32) + got + row_of(v_ref, OUT_BIAS)
                h_out[rows, :] = h
                n, _ = norm_stats(h)
                a = (n * row_of(v_ref, SECOND_GAIN) + row_of(v_ref, SECOND_SHIFT)).astype(BF)
                a_out[rows, :] = a
                a_ref[pl.ds(pl.multiple_of(j * STEP + i * ROWS, ROWS), ROWS), :] = a

    @pl.when((j >= lead) & (j < lead + tiles))
    def _():
        bias = v_ref[pl.ds(UP_BIAS + t_ref[j - lead], 1), :]

        def pair(rows):
            return (mm(a_ref[rows, :], up_ref[...], 1, 0) + bias,
                    mm(c_ref[rows, :], dn_ref[...], 1, 1).astype(BF).astype(F32))

        def pass_rows(i, gb):
            rows = [pl.ds(pl.multiple_of(i * STEP + n * ROWS, ROWS), ROWS) for n in range(STEP // ROWS)]
            ahead = pair(rows[0])
            for n, here in enumerate(rows):
                u, ga = ahead
                if n + 1 < len(rows):
                    ahead = pair(rows[n + 1])
                g, dg = gelu_both(u)
                g = g.astype(BF)
                gp = (ga * dg).astype(BF)
                act[here, :] = g
                gpre[here, :] = gp
                gb = gb + jnp.sum(gp.astype(F32), axis=0, keepdims=True)
                r = mm(g, dn_ref[...], 1, 0)
                e = mm(gp, up_ref[...], 1, 1)
                if tiles > 1:
                    r = r + jnp.where(j > lead, r_acc[here, :], 0.0)
                    e = e + jnp.where(j > lead, e_acc[here, :], 0.0)
                if several:
                    r_acc[here, :] = r
                    e_acc[here, :] = e
                else:
                    r_out[here, :] = r.astype(BF)
                    e_out[here, :] = e.astype(BF)
            return gb

        gb_ref[0] = lax.fori_loop(0, L // STEP, pass_rows, jnp.zeros((1, d), F32))

        def weights(n, _):
            cols = pl.ds(pl.multiple_of(n * ROWS, ROWS), ROWS)
            under = pl.ds(pl.multiple_of(d + n * ROWS, ROWS), ROWS)
            down, up = mm(act[:, cols], c_ref[...], 0, 0), mm(a_ref[:, cols], gpre[...], 0, 0)
            into = unit if joined else units[0].at[0]
            if joined:
                down, up = down + other_ref[cols, :].astype(F32), up + other_ref[under, :].astype(F32)
            into[cols, :] = down.astype(BF)
            into[under, :] = up.astype(BF)
            return 0

        lax.fori_loop(0, d // ROWS, weights, 0)
        if joined:
            bit = t_ref[tiles]
            units[0][...] = unit[pl.ds(pl.multiple_of((1 - bit) * d, d), d), :]
            units[1][...] = unit[pl.ds(pl.multiple_of(bit * d, d), d), :]

    if not after:
        if several:
            @pl.when(j == lead + tiles - 1)
            def _():
                r_out[...] = r_acc[...].astype(BF)
                e_out[...] = e_acc[...].astype(BF)
        return

    @pl.when(j == tiles)
    def _():
        acc[...] = jnp.zeros_like(acc)
        sums_ref[...] = jnp.zeros_like(sums_ref)

    for s in range(steps):
        @pl.when(j == tiles + s)
        def _(s=s):
            for c in block(s):
                c.wait()
            h_ref, m_ref, *past = (t.at[s % 2] for t in held)
            for i in range(STEP // ROWS):
                rows = pl.ds(i * ROWS, ROWS)
                at = pl.ds(s * STEP + i * ROWS, ROWS)
                r, e = r_acc[at, :], e_acc[at, :]
                for n in range(0, after, 2):
                    r = r + past[n][rows, :].astype(F32)
                    e = e + past[n + 1][rows, :].astype(F32)
                h = h_ref[rows, :]
                o_ref[rows, :] = ((h + r + row_of(v_ref, DOWN_BIAS)) * row_of(v_ref, LIVE)).astype(BF)
                n, q = norm_stats(h)
                c = c_ref[at, :].astype(F32)
                gh = c + norm_back(e * row_of(v_ref, SECOND_GAIN), n, q)
                gh_ref[rows, :] = gh
                gb = gh.astype(BF)
                gm_ref[rows, :] = mm(gb, w_ref[...], 1, 1).astype(BF)
                acc[...] += mm(m_ref[rows, :], gb, 0, 0)
                add = lambda t: jnp.sum(t, axis=0, keepdims=True)
                sums_ref[0:1, :] += add(e * n)
                sums_ref[1:2, :] += add(e)
                sums_ref[2:3, :] += add(gb.astype(F32))
                sums_ref[3:4, :] += add(c)
            if s + 2 < steps:
                for c in block(s + 2):
                    c.start()
            if s == steps - 1:
                dw_ref[...] = acc[...].astype(BF)


def mlp_call(tile_bit, tiles, c, up, dn, vecs, a=None, before=None, other=None, after=None):
    L, d = c.shape
    steps = L // STEP
    lead = steps if before else 0
    tile = lambda j: jnp.clip(j - lead, 0, tiles - 1)
    mode = dict(pipeline_mode=pl.Buffered(1)) if tiles == 1 else {}
    first = pl.BlockSpec((STEP, d), lambda j, _: (jnp.minimum(j, steps - 1), 0))
    last = pl.BlockSpec((STEP, d), lambda j, _: (jnp.clip(j - 1, 0, steps - 1), 0))
    seq = shape((L, d), BF)
    in_specs, args, out_specs, out_shape = [], [], [], []
    if before:
        in_specs += [first, once((d, d)), first]
        args += list(before)
        out_specs += [first, first]
        out_shape += [shape((L, d), F32), seq]
    else:
        in_specs += [once((L, d))]
        args += [a]
    in_specs += [once((L, d)), pl.BlockSpec((d, d), lambda j, t: (0, t[tile(j)]), **mode),
                 pl.BlockSpec((d, d), lambda j, t: (t[tile(j)], 0), **mode), once(vecs.shape)]
    args += [c, up, dn, vecs]
    scratch = [pltpu.VMEM((L, d), BF), pltpu.VMEM((L, d), BF)]
    scratch += [pltpu.VMEM((L, d), F32)] * 2 if after or tiles > 1 else [pltpu.VMEM((16, 128), F32)] * 2
    if other is not None:
        in_specs += [once((2 * d, d))]
        args += [other]
        out_specs += [whole((d, d))] * 2
        out_shape += [shape((d, d), BF)] * 2
        scratch += [pltpu.VMEM((2 * d, d), BF)]
    else:
        out_specs += [pl.BlockSpec((1, 2 * d, d), lambda j, _: (tile(j), 0, 0))]
        out_shape += [shape((tiles, 2 * d, d), BF)]
    out_specs += [pl.BlockSpec((1, 1, d), lambda j, _: (tile(j), 0, 0))]
    out_shape += [shape((tiles, 1, d), F32)]
    if before:
        scratch += [pltpu.VMEM((L, d), BF)]
    if after:
        hidden, mixed, w, *past = after
        in_specs += [once((d, d))] + [pl.BlockSpec(memory_space=pl.ANY)] * (2 + len(past))
        args += [w, hidden, mixed] + past
        out_specs += [last, last, last, whole((d, d)), whole((8, d))]
        out_shape += [seq, shape((L, d), F32), seq, shape((d, d), BF), shape((8, d), F32)]
        scratch += [pltpu.VMEM((d, d), F32), pltpu.SemaphoreType.DMA((2, len(past) + 2)), pltpu.VMEM((2, STEP, d), F32)]
        scratch += [pltpu.VMEM((2, STEP, d), BF)] * (1 + len(past))
    else:
        out_specs += [whole((L, d))] * 2
        out_shape += [seq, seq]
    return pl.pallas_call(
        partial(mlp_kernel, before is not None, tiles, other is not None, len(after) - 3 if after else 0, steps),
        grid_spec=pltpu.PrefetchScalarGridSpec(
            num_scalar_prefetch=1,
            grid=(tiles + lead + (steps if after else 0),),
            in_specs=in_specs, out_specs=out_specs, scratch_shapes=scratch,
        ),
        out_shape=out_shape,
        compiler_params=params("mlp", L),
        cost_estimate=cost(12 * tiles),
        name="mlp",
    )(tile_bit, *args)


def attend_back_kernel(q_ref, k_ref, v_ref, p_ref, i_ref, g_ref, m_ref, dq_ref, dk_ref, dv_ref, dk_acc, dv_acc):
    L = q_ref.shape[0]
    low = lax.broadcasted_iota(jnp.int32, (ROWS, 128), 1) < 64
    nb = L // ROWS
    jobs = [(i, h) for i in reversed(range(nb)) for h in range(2)]
    strips = {}
    def strip(i):
        if i not in strips:
            rows = pl.ds(i * ROWS, ROWS)
            g32 = g_ref[rows, :].astype(F32) * i_ref[rows, :].astype(F32)
            g = g32.astype(BF)
            gm = g32 * m_ref[rows, :].astype(F32)
            strips[i] = (g, gm, q_ref[rows, :].T, g.T)
        return strips[i]

    def dprob(i, h):
        g, gm, _, _ = strip(i)
        mine = low if h == 0 else ~low
        gh = jnp.where(mine, g, jnp.zeros_like(g))
        delta = jnp.sum(jnp.where(mine, gm, 0.0), axis=-1, keepdims=True)
        return mm(gh, v_ref[pl.ds(0, (i + 1) * ROWS), :], 1, 1), delta

    dqs = {}
    ahead = [dprob(*jobs[0])]
    for t, (i, h) in enumerate(jobs):
        dp, delta = ahead.pop(0)
        if t + 1 < len(jobs):
            ahead.append(dprob(*jobs[t + 1]))
        n = (i + 1) * ROWS
        past = pl.ds(0, n)
        _, _, qt, gt = strip(i)
        p = p_ref[h, :, pl.ds(i * (i + 1) // 2 * ROWS, n)]
        side = pl.ds(64 * h, 64)
        dv = mm(gt[64 * h : 64 * h + 64], p, 1, 0)
        ds = (p.astype(F32) * (dp - delta)).astype(BF)
        dqs[h] = mm(ds, k_ref[past, :], 1, 0)
        dk = mm(qt[64 * h : 64 * h + 64], ds, 1, 0)
        if i == nb - 1:
            dk_acc[side, past] = dk
            dv_acc[side, past] = dv
        else:
            dk_acc[side, past] += dk
            dv_acc[side, past] += dv
        if h == 1:
            dq_ref[pl.ds(i * ROWS, ROWS), :] = (jnp.where(low, dqs[0], dqs[1]) * 0.125).astype(BF)
    dk_ref[...] = dk_acc[...].T.astype(BF)
    dv_ref[...] = dv_acc[...].T.astype(BF)


def attend_back_call(qkv, p, inv, gm, mixed, lo, count, held=()):
    L, d3 = qkv.shape
    n = d3 // 3 // 128
    col = lambda k: pl.BlockSpec((L, 128), lambda j: (0, k * n + lo + j))
    s = shape((L, d3 // 3), BF)
    kernel = attend_back_kernel
    if held:
        kernel = lambda *refs: attend_back_kernel(*refs[:7], *refs[10:])
    return pl.pallas_call(
        kernel,
        grid=(count,),
        in_specs=[col(0), col(1), col(2), pl.BlockSpec((2, ROWS, tri_cols(L)), lambda j: (lo + j, 0, 0)), col(0), col(0), col(0)]
        + [pl.BlockSpec(memory_space=pl.ANY)] * len(held),
        out_specs=[col(0)] * 3,
        out_shape=[s] * 3,
        input_output_aliases={7 + i: i for i in range(len(held))},
        scratch_shapes=[pltpu.VMEM((128, L), F32), pltpu.VMEM((128, L), F32)],
        compiler_params=params("attend_back", L),
        cost_estimate=cost(3 * count),
        name="attend_back",
    )(qkv, qkv, qkv, p, inv, gm, mixed, *held)


def joint_sent_kernel(core_ref, a_ref, q_ref, k_ref, v_ref, w_ref, out_ref, sums_ref):
    d = a_ref.shape[1]
    sums_ref[...] = jnp.zeros_like(sums_ref)
    sums_ref[0:1, :] = jnp.sum(q_ref[...].astype(F32), axis=0, keepdims=True)
    sums_ref[1:2, :] = jnp.sum(v_ref[...].astype(F32), axis=0, keepdims=True)

    @pl.when(core_ref[0] == 1)
    def _():
        out_ref[0:d, :] = mm(a_ref[...], q_ref[...], 0, 0).astype(BF)
        out_ref[d : 2 * d, :] = mm(a_ref[...], k_ref[...], 0, 0).astype(BF)

    @pl.when(core_ref[0] == 0)
    def _():
        out_ref[0:d, :] = mm(a_ref[...], v_ref[...], 0, 0).astype(BF)
        out_ref[d : 2 * d, :] = w_ref[...]


def joint_sent_call(core, a, dq, dk, dv, dw):
    L, d = a.shape
    return pl.pallas_call(
        joint_sent_kernel,
        grid_spec=pltpu.PrefetchScalarGridSpec(
            num_scalar_prefetch=1, grid=(1,), in_specs=[once((L, d))] * 4 + [once((d, d))],
            out_specs=[whole((2 * d, d)), whole((8, d))]),
        out_shape=[shape((2 * d, d), BF), shape((8, d), F32)],
        compiler_params=params("joint_sent", L),
        cost_estimate=cost(5),
        name="joint_sent",
    )(core, a, dq, dk, dv, dw)


def joint_kept_kernel(core_ref, a_ref, q_ref, k_ref, v_ref, w_ref, other_ref, sent_ref, kept_ref, unit):
    d = a_ref.shape[1]
    add = lambda t, n: (t + other_ref[n * d : (n + 1) * d, :].astype(F32)).astype(BF)

    @pl.when(core_ref[0] == 0)
    def _():
        unit[0:d, :] = add(mm(a_ref[...], q_ref[...], 0, 0), 0)
        unit[d : 2 * d, :] = add(mm(a_ref[...], k_ref[...], 0, 0), 1)

    @pl.when(core_ref[0] == 1)
    def _():
        unit[0:d, :] = add(mm(a_ref[...], v_ref[...], 0, 0), 0)
        unit[d : 2 * d, :] = add(w_ref[...].astype(F32), 1)

    bit = core_ref[1]
    sent_ref[...] = unit[pl.ds(pl.multiple_of((1 - bit) * d, d), d), :]
    kept_ref[...] = unit[pl.ds(pl.multiple_of(bit * d, d), d), :]


def joint_kept_call(core_bit, a, dq, dk, dv, dw, other):
    L, d = a.shape
    return pl.pallas_call(
        joint_kept_kernel,
        grid_spec=pltpu.PrefetchScalarGridSpec(
            num_scalar_prefetch=1, grid=(1,), in_specs=[once((L, d))] * 4 + [once((d, d)), once((2 * d, d))],
            out_specs=[whole((d, d)), whole((d, d))], scratch_shapes=[pltpu.VMEM((2 * d, d), BF)]),
        out_shape=[shape((d, d), BF)] * 2,
        compiler_params=params("joint_kept", L),
        cost_estimate=cost(5),
        name="joint_kept",
    )(core_bit, a, dq, dk, dv, dw, other)


def tokens_kernel(q_ref, k_ref, v_ref, w_ref, x_ref, gh_ref, vec_ref, o_ref, sums_ref):
    i = pl.program_id(0)
    d = x_ref.shape[1]

    @pl.when(i == 0)
    def _():
        sums_ref[...] = jnp.zeros_like(sums_ref)

    def back(i):
        rows = pl.ds(i * ROWS, ROWS)
        return (mm(q_ref[rows, :], w_ref[:, 0:d], 1, 1) + mm(k_ref[rows, :], w_ref[:, d : 2 * d], 1, 1)
                + mm(v_ref[rows, :], w_ref[:, 2 * d :], 1, 1))

    ahead = back(0)
    for j in range(STEP // ROWS):
        e, rows = ahead, pl.ds(j * ROWS, ROWS)
        if (j + 1) * ROWS < STEP:
            ahead = back(j + 1)
        n, r = norm_stats(x_ref[rows, :].astype(F32))
        o_ref[rows, :] = (gh_ref[rows, :] + norm_back(e * row_of(vec_ref, FIRST_GAIN), n, r)).astype(BF)
        sums_ref[0:1, :] += jnp.sum(e * n, axis=0, keepdims=True)
        sums_ref[1:2, :] += jnp.sum(e, axis=0, keepdims=True)


def tokens_call(dq, dk, dv, w, x, gh, vecs):
    L, d = x.shape
    blk = pl.BlockSpec((STEP, d), lambda i: (i, 0))
    return pl.pallas_call(
        tokens_kernel,
        grid=(L // STEP,),
        in_specs=[blk, blk, blk, once((d, 3 * d)), blk, blk, once(vecs.shape)],
        out_specs=[blk, whole((8, d))],
        out_shape=[shape((L, d), BF), shape((8, d), F32)],
        compiler_params=params("tokens_back", L),
        cost_estimate=cost(9),
        name="tokens_back",
    )(dq, dk, dv, w, x, gh, vecs)


def place_kernel(core_ref, own_ref, other_ref, *rest):
    down_ref, up_ref = rest[-2:]
    d = down_ref.shape[1]
    for n, ref in enumerate((own_ref, other_ref)):
        @pl.when(pl.program_id(0) == n)
        def _(ref=ref):
            down_ref[...] = ref[0:d, :].astype(F32)
            up_ref[...] = ref[d : 2 * d, :].astype(F32)


def place_call(core, own, other, tile, ff, held=()):
    d = own.shape[1]
    at = lambda n, s: tile + jnp.where(n == 0, s[0], 1 - s[0])
    return pl.pallas_call(
        place_kernel,
        grid_spec=pltpu.PrefetchScalarGridSpec(
            num_scalar_prefetch=1,
            grid=(2,),
            in_specs=[whole((2 * d, d))] * 2 + [pl.BlockSpec(memory_space=pl.ANY)] * len(held),
            out_specs=[pl.BlockSpec((d, d), lambda n, s: (at(n, s), 0)), pl.BlockSpec((d, d), lambda n, s: (0, at(n, s)))],
        ),
        out_shape=[shape((ff, d), F32), shape((d, ff), F32)],
        input_output_aliases={3 + i: i for i in range(len(held))},
        compiler_params=params("place"),
        cost_estimate=cost(5),
        name="place",
    )(core, own, other, *held)


def place_half_kernel(other, core_ref, piece_ref, *refs):
    if other:
        tail_ref, _, _, joint_ref, out_ref, small_ref, wide, sems = refs
    else:
        joint_ref, out_ref, wide, sems = refs
    d = wide.shape[2]
    for n in range(2):
        wide[n] = piece_ref[n * d : (n + 1) * d, :].astype(F32)
    if other:
        small_ref[...] = tail_ref[...].astype(F32) + piece_ref[2 * d :, :].astype(F32)

    cols = lambda n: joint_ref.at[:, pl.ds(n * d, d)]
    for kind, places in enumerate(((cols(0), cols(1)), (cols(2), out_ref))):
        @pl.when(core_ref[0] == (1 - kind if other else kind))
        def _(places=places):
            copies = [pltpu.make_async_copy(wide.at[n], place, sems.at[n]) for n, place in enumerate(places)]
            for c in copies:
                c.start()
            for c in copies:
                c.wait()


def place_half(core, piece, d, own=None, held=()):
    v, far = pl.BlockSpec(memory_space=pltpu.VMEM), pl.BlockSpec(memory_space=pl.ANY)
    rows = piece.shape[0] - 2 * d
    more = own is not None
    return pl.pallas_call(
        partial(place_half_kernel, more),
        grid=(1,),
        in_specs=[pl.BlockSpec(memory_space=pltpu.SMEM), v]
        + ([pl.BlockSpec((rows, d), lambda i: (2 * d // rows, 0)), far, far] if more else []),
        out_specs=[far, far] + ([v] if more else []),
        out_shape=[shape((d, 3 * d), F32), shape((d, d), F32)] + ([shape((rows, d), F32)] if more else []),
        input_output_aliases={3: 0, 4: 1} if more else {},
        scratch_shapes=[pltpu.VMEM((2, d, d), F32), pltpu.SemaphoreType.DMA((2,))],
        compiler_params=params("place_joint"),
        cost_estimate=cost(3),
        name="place_half",
    )(core, piece, *((own,) + tuple(held) if more else ()))


def halve_kernel(up_ref, a_ref, b_ref, c_ref, d_ref, sent_ref, kept_ref):
    sent_ref[...] = a_ref[...] + b_ref[...]
    kept_ref[...] = c_ref[...] + d_ref[...]


def halve_call(up, kept, other):
    rows, d = kept.shape[0] // 2, kept.shape[1]
    block = rows if rows <= 384 else rows // 2
    n = rows // block
    go = pl.BlockSpec((block, d), lambda i, up: ((1 - up[0]) * n + i, 0))
    stay = pl.BlockSpec((block, d), lambda i, up: (up[0] * n + i, 0))
    out = pl.BlockSpec((block, d), lambda i, up: (i, 0))
    s = shape((rows, d), BF)
    return pl.pallas_call(
        halve_kernel,
        grid_spec=pltpu.PrefetchScalarGridSpec(
            num_scalar_prefetch=1, grid=(n,), in_specs=[go, go, stay, stay], out_specs=[out, out]),
        out_shape=[s, s],
        compiler_params=params("halve"),
        cost_estimate=cost(2),
        name="halve",
    )(up, kept, other, kept, other)


def double_kernel(rows, up_ref, a_ref, b_ref, o_ref):
    up = up_ref[0]
    o_ref[pl.ds(pl.multiple_of(up * rows, 16), rows), :] = a_ref[0:rows, :]
    o_ref[pl.ds(pl.multiple_of((1 - up) * rows, 16), rows), :] = b_ref[0:rows, :]
    if a_ref.shape[0] > rows:
        tail = a_ref[rows:, :].astype(F32) + b_ref[rows:, :].astype(F32)
        o_ref[2 * rows :, :] = tail.astype(BF)


def double_call(up, kept, other, tail=0):
    rows, d = kept.shape[0] - tail, kept.shape[1]
    v = pl.BlockSpec(memory_space=pltpu.VMEM)
    return pl.pallas_call(
        partial(double_kernel, rows),
        in_specs=[pl.BlockSpec(memory_space=pltpu.SMEM), v, v],
        out_specs=v,
        out_shape=shape((2 * rows + tail, d), BF),
        compiler_params=params("double"),
        cost_estimate=cost(2),
        name="double",
    )(up, kept, other)


def arrange_kernel(places, at_ref, *refs):
    out_ref = refs[-1]
    for k, ref in enumerate(refs[:-1]):
        if places < len(refs) - 1:
            @pl.when(at_ref[k] < places)
            def _(k=k, ref=ref):
                out_ref[at_ref[k]] = ref[...]
        else:
            out_ref[at_ref[k]] = ref[...]


def arrange_call(at, parts, places):
    block, d = parts[0].shape
    v = pl.BlockSpec(memory_space=pltpu.VMEM)
    return pl.pallas_call(
        partial(arrange_kernel, places),
        in_specs=[pl.BlockSpec(memory_space=pltpu.SMEM)] + [v] * len(parts),
        out_specs=v,
        out_shape=shape((places, block, d), BF),
        compiler_params=params("arrange"),
        cost_estimate=cost(2),
        name="arrange",
    )(at, *parts)


def small_kernel(core_ref, first_ref, joint_ref, second_ref, b0, b1, b2, b3, o_ref):
    o_ref[...] = jnp.zeros_like(o_ref)
    o_ref[0:2, :] = first_ref[0:2, :].astype(BF)
    o_ref[2:4, :] = joint_ref[0:2, :].astype(BF)
    o_ref[4:8, :] = second_ref[0:4, :].astype(BF)
    for n, (u, v) in enumerate(((b0, b1), (b1, b0), (b2, b3), (b3, b2))):
        o_ref[8 + n : 9 + n, :] = jnp.where(core_ref[0] == 0, u[0], v[0]).astype(BF)


def small_call(core, first, joint, second, up_bias):
    v = pl.BlockSpec(memory_space=pltpu.VMEM)
    return pl.pallas_call(
        small_kernel,
        in_specs=[pl.BlockSpec(memory_space=pltpu.SMEM)] + [v] * 7,
        out_specs=v,
        out_shape=shape((16, first.shape[1]), BF),
        compiler_params=params("small"),
        cost_estimate=cost(1),
        name="small",
    )(core, first, joint, second, *up_bias)


def bits_of(count):
    assert count & (count - 1) == 0
    return count.bit_length() - 1


class Moves:
    def __init__(self, n_dp, n_blk, slots):
        assert slots <= n_blk
        self.n_dp, self.n_blk, self.slots = n_dp, n_blk, slots
        self.dp, self.blk = lax.axis_index("dp"), lax.axis_index("blk")
        self.odd = self.dp % 2

    def slot(self, blk):
        return jnp.where(self.odd == 1, self.n_blk - 1 - blk, blk)

    def perm(self, step, back):
        pairs = []
        for g in range(self.n_dp):
            for b in range(self.n_blk):
                d = (b + step) % self.n_blk
                s = self.n_blk - 1 - d if g % 2 else d
                if s < self.slots:
                    pair = (g * self.n_blk + b, g * self.n_blk + d)
                    pairs.append(pair[::-1] if back else pair)
        return pairs

    def send_out(self, x, beside=None):
        parts = []
        for step in range(self.n_blk):
            if beside is not None and step == self.n_blk - 1:
                x = lax.optimization_barrier((x, beside))[0]
            s = jnp.minimum(self.slot((self.blk + step) % self.n_blk), self.slots - 1)
            part = lax.dynamic_index_in_dim(x, s, 0, keepdims=False)
            parts.append(lax.ppermute(part, ("dp", "blk"), self.perm(step, False)) if step else part)
        return parts

    def join(self, parts):
        at = (self.blk - jnp.arange(self.n_blk, dtype=jnp.int32)) % self.n_blk
        return arrange_call(at, parts, self.n_blk).reshape(-1, parts[0].shape[1])

    def send_back(self, y):
        y = y.reshape(self.n_blk, -1, y.shape[-1])
        parts = []
        for step in range(self.n_blk):
            part = lax.dynamic_index_in_dim(y, (self.blk - step) % self.n_blk, 0, keepdims=False)
            parts.append(lax.ppermute(part, ("dp", "blk"), self.perm(step, True)) if step else part)
        return parts

    def exchange_back(self, y):
        return lax.all_to_all(y.reshape(self.n_blk, -1, y.shape[-1]), "blk", 0, 0)

    def unexchange(self, y):
        return jnp.where(self.odd == 1, y[::-1][: self.slots], y[: self.slots])

    def unjoin(self, parts):
        at = self.slot((self.blk + jnp.arange(self.n_blk, dtype=jnp.int32)) % self.n_blk)
        return arrange_call(at, parts, self.slots)


class Order:
    def __init__(self):
        self.last = None

    def take(self, *arrays):
        if self.last is not None:
            arrays = lax.optimization_barrier(arrays + (self.last,))[:-1]
        return arrays if len(arrays) > 1 else arrays[0]

    def mark(self, array):
        self.last = array


class Sum:
    def __init__(self, moves):
        self.n = moves.n_dp * moves.n_blk
        self.me = moves.dp * moves.n_blk + moves.blk
        low, high = bits_of(moves.n_blk), bits_of(moves.n_dp)
        plane = [low + 1 + i for i in range(high - 1)]
        self.core = low
        self.orders = [plane + list(range(low)), plane[::-1] + list(range(low))]
        self.stages = len(self.orders[0])
        self.tail = None

    def order(self, i, stage):
        return self.core if stage < 0 else self.orders[(i >> self.core) & 1][stage]

    def swap(self, x, stage):
        return lax.ppermute(x, ("dp", "blk"), [(i, i ^ (1 << self.order(i, stage))) for i in range(self.n)])

    def up(self, stage, me=None):
        me = self.me if me is None else me
        odd = (me >> self.core) & 1
        return jnp.where(odd == 0, (me >> self.order(0, stage)) & 1, (me >> self.order(1 << self.core, stage)) & 1)

    def cross(self, sent):
        self.moving = self.swap(sent, -1)

    def crossed(self, order):
        return order.take(self.moving)

    def begin(self, sent, kept):
        self.sent, self.kept, self.stage, self.gathering = sent, kept, 0, False
        self.send()

    def send(self):
        if not self.gathering:
            self.moving = self.swap(self.sent, self.stage)
        else:
            self.moving = self.swap(self.kept, self.stage)

    def step(self, order):
        other, self.kept = order.take(self.moving, self.kept)
        if not self.gathering:
            self.stage += 1
            if self.stage == self.stages:
                self.kept = self.kept + other
                if self.tail is not None:
                    self.kept = jnp.concatenate([self.kept, self.tail])
                self.gathering = True
                self.stage -= 1
            else:
                half = self.kept.shape[0] // 2
                up = self.up(self.stage)
                if half % 16 == 0:
                    self.sent, self.kept = halve_call(up.reshape(1), self.kept, other)
                else:
                    part = lambda x, at: lax.dynamic_slice_in_dim(x, at * half, half, 0)
                    self.sent = part(self.kept, 1 - up) + part(other, 1 - up)
                    self.kept = part(self.kept, up) + part(other, up)
        else:
            tail = 0 if self.tail is None else self.tail.shape[0]
            self.kept = double_call(self.up(self.stage).reshape(1), self.kept, other, tail)
            self.stage -= 1
        order.mark(self.kept)
        self.send()

    def finish(self, order):
        theirs = order.take(self.moving)
        return ((self.me >> self.core) & 1).reshape(1), self.kept, theirs


PLAN = (
    "m1", "m2", "m3", "m4", "o", "1", "ab1", "1", "x", "ab2", "2", "1", "O", "js", "tok", "2", "jk", "1", "2", "3",
    "1", "3", "2", "1", "3", "2", "3", "1", "g", "3", "2", "3", "2", "1", "a", "3", "3", "1", "b", "c", "2", "3",
    "G", "2",
)


def on_device(n_dp, n_blk, tokens, live_count, first_gain, first_shift, joint_weight, query_bias, value_bias,
              out_weight, out_bias, second_gain, second_shift, up_weight, up_bias, down_weight, down_bias, cotangent):
    slots, block, d = tokens.shape
    ff = up_weight.shape[1]
    assert ff == 4 * d
    pairs = d // 128
    moves = Moves(n_dp, n_blk, slots)
    order = Order()
    mine = moves.slot(moves.blk)
    live = ((mine < slots) & (mine < live_count[0])).astype(F32)
    core = moves.odd.reshape(1)
    vecs = vectors_call([first_gain, first_shift, query_bias, value_bias, out_bias, second_gain, second_shift,
                         down_bias, up_bias], live.reshape(1))
    live_slots = jnp.arange(slots, dtype=jnp.int32) < live_count[0]

    x_parts = moves.send_out(tokens, vecs)
    x = moves.join(x_parts)
    attn_in, qkv = joint_call(x, joint_weight, vecs)
    c = jnp.where(live_slots[:, None, None], lax.optimization_barrier((cotangent, x))[0], jnp.zeros_like(cotangent))
    c_parts = moves.send_out(c)
    c_parts[0] = jnp.where(mine < slots, c_parts[0], jnp.zeros_like(c_parts[0]))
    mixed, p, inv = attend_call(qkv)
    order.mark(mixed)
    c = moves.join(list(order.take(*c_parts)))

    sums = {name: Sum(moves) for name in "123"}
    got = {}
    bit = sums["2"].up(0).reshape(1)
    tile = lambda which, tiles, **more: mlp_call(which, tiles, c, up_weight, down_weight, vecs, **more)

    def m1():
        got["hidden"], got["a"], sent, got["gb1"], *past = tile(1 - core, 1, before=(mixed, out_weight, x))
        sums["1"].cross(sent[0])
        got["past"] = tuple(past)
        return past[0]

    def m2():
        sent, got["gb3"], *past = tile(3 - core, 1, a=order.take(got["a"]))
        sums["2"].cross(sent[0])
        got["past"] += tuple(past)
        return past[0]

    def m3():
        other = sums["1"].crossed(order)
        sent, kept, got["gb0"], *past = tile(jnp.concatenate([core, bit]), 1, a=order.take(got["a"]), other=other)
        sums["1"].begin(sent, kept)
        got["past"] += tuple(past)
        return past[0]

    def m4():
        other = sums["2"].crossed(order)
        after = (got["hidden"], mixed, out_weight) + got["past"]
        sent, kept, gb, out, gh, gm, dwo, s = tile(jnp.concatenate([2 + core, bit]), 1, a=order.take(got["a"]), other=other,
                                                   after=after)
        sums["2"].begin(sent, kept)
        got.update(gb2=gb, out=out, gh=gh, gm=gm, dwo=dwo, sums2=s)
        return gh

    def ab1():
        count = pairs // 2 if "ab2" in PLAN else pairs
        got["back"] = attend_back_call(qkv, p, inv, order.take(got["gm"]), mixed, 0, count)
        return got["back"][0]

    def ab2():
        got["back"] = attend_back_call(qkv, p, inv, order.take(got["gm"]), mixed, pairs // 2, pairs - pairs // 2,
                                       got["back"])
        return got["back"][0]

    def js():
        sent, got["sums1"] = joint_sent_call(core, order.take(attn_in), *got["back"], got["dwo"])
        sums["3"].cross(sent)
        return sent

    def jk():
        other = sums["3"].crossed(order)
        sent, kept = joint_kept_call(jnp.concatenate([core, bit]), order.take(attn_in), *got["back"], got["dwo"], other)
        sums["3"].begin(sent, kept)
        return kept

    def tok():
        dq, dk, dv = got["back"]
        got["gx"], sums0 = tokens_call(order.take(dq), dk, dv, joint_weight, x, got["gh"], vecs)
        order.mark(got["gx"])
        sums["3"].tail = small_call(core, order.take(sums0), got["sums1"], got["sums2"], [got["gb%d" % n] for n in range(4)])
        return sums["3"].tail

    def send(name):
        if name == "out" and not PLAN.count("x"):
            got["out_moved"] = moves.exchange_back(order.take(got["out"]))
        else:
            got[name + "_parts"] = moves.send_back(order.take(got[name]))

    def part(name, k):
        parts = got[name + "_parts"]
        if k < len(parts):
            parts[k] = order.take(parts[k])
            order.mark(parts[k])

    def join(name):
        if name == "out" and "out_moved" in got:
            got["out"] = moves.unexchange(order.take(got["out_moved"]))
            return got["out"]
        got[name] = moves.unjoin(list(order.take(*got[name + "_parts"])))
        return got[name]

    def step(name):
        total = sums.get(name)
        if total is None:
            return
        if not total.gathering or total.stage >= 0:
            total.step(order)
            if name == "3" and total.gathering and total.stage < 0:
                got["joint"] = place_half(core, order.take(total.kept), d)
                order.mark(got["joint"][1])
        else:
            sums[name] = None
            if name == "3":
                _, own, theirs = total.finish(order)
                got["joint"] = place_half(core, theirs, d, own, got["joint"])
                order.mark(got["joint"][1])
            else:
                got["wide"] = place_call(*total.finish(order), 2 * int(name) - 2, ff, got.get("wide", ()))
                order.mark(got["wide"][0])

    kernels = dict(m1=m1, m2=m2, m3=m3, m4=m4, ab1=ab1, ab2=ab2, js=js, jk=jk, tok=tok)
    for word in PLAN + ("2", "1", "3") * 12:
        if word in kernels:
            order.mark(kernels[word]())
        elif word in "abc":
            part("gx", 1 + "abc".index(word))
        elif word in "xyz":
            part("out", 1 + "xyz".index(word))
        elif word in "og":
            send({"o": "out", "g": "gx"}[word])
        elif word in "OG":
            order.mark(join({"O": "out", "G": "gx"}[word]))
        else:
            step(word)
    small = got["joint"][2]
    return (got["out"], got["gx"], small[0], small[1], got["joint"][0], small[2], small[3], got["joint"][1], small[6],
            small[4], small[5], got["wide"][1], small[8:12].reshape(-1), got["wide"][0], small[7])


def solution(mesh):
    seq = P("dp", "blk", None)
    n_dp, n_blk = mesh.shape["dp"], mesh.shape["blk"]
    return jax.shard_map(
        partial(on_device, n_dp, n_blk), mesh=mesh,
        in_specs=(seq, P("dp")) + (P(),) * 13 + (seq,),
        out_specs=(seq, seq) + (P(),) * 13,
        check_vma=False,
    )
```
